512 devices in a mesh: seq: 128 (over y, z, core), grp: 4 (over x).
Axes of the slice: x: 4, y: 8, z: 8, core: 2. Of those that a mesh axis runs over, the one named last changes fastest.
Arguments:
- queries: bfloat16 [32768, 4096], P('seq', 'grp'), parts along dimension 1, may hold values from -4.5 to 4.5
- keys: bfloat16 [32768, 512], P('seq', 'grp'), parts along dimension 1, may hold values from -4.5 to 4.5
- values: bfloat16 [32768, 512], P('seq', 'grp'), parts along dimension 1, may hold values from -4.5 to 4.5
- grad_out: bfloat16 [32768, 4096], P('seq', 'grp'), parts along dimension 1, may hold values from -6 to 6
- lengths: int32 [516], replicated, may hold values from 0 to 512, as said below
- assign: int32 [128, 2], replicated, may hold values from 0 to 255, as said below
Outputs:
- attn_out: bfloat16 [32768, 4096], P('seq', 'grp'), parts along dimension 1
- grad_queries: bfloat16 [32768, 4096], P('seq', 'grp'), parts along dimension 1
- grad_keys: bfloat16 [32768, 512], P('seq', 'grp'), parts along dimension 1
- grad_values: bfloat16 [32768, 512], P('seq', 'grp'), parts along dimension 1
The draws below stay inside these ranges and needn't reach their ends.
There are 4 independent parts, one for each index of `grp`. The reference program is written for one: setup_inputs(seed, part) draws one part's arguments, and reference() takes and returns one part's arrays. A program takes and returns all parts, laid end to end along the dimension named above; an argument that names none is the same for every part. Nothing has to cross between parts.
Inputs may be any that keep to these rules, and one draw needn't show every extreme that they name: The lengths sum to 32768; all positive lengths come first and zeros after them; the longest is exactly 512. `assign`: row d names the two spans held by device d, in increasing order; devices 2p and 2p + 1 hold the spans 4p to 4p + 3 between them, each once.
All inputs are finite; a program needn't handle non-finite values.
Results may differ from the reference program's by a relative error of at most 0.03.
Values may be sent and summed in bfloat16 or wider, within the bound.
A program may use at most 64 MiB of HBM per device.

```python
import math
import jax
import jax.numpy as jnp
from jax import lax

HEADS = 8
HEAD_DIM = 128
SPAN = 128
NCHUNK = 256
TOKENS = 32768
MOSTDOC = 512
NDOC = 516


def document_lengths(key):
    doc_key = jax.random.fold_in(key, 11)
    spare = jax.random.randint(doc_key, (NDOC,), 0, 3 * MOSTDOC // 4)
    slot_index = jnp.arange(NDOC, dtype=jnp.int32)
    raw_lengths = jnp.where(slot_index % 4 == 0, MOSTDOC, MOSTDOC - spare).astype(jnp.int32)
    doc_ends = jnp.cumsum(raw_lengths).astype(jnp.int32)
    doc_starts = doc_ends - raw_lengths
    return jnp.clip(TOKENS - doc_starts, 0, raw_lengths).astype(jnp.int32)


def draw_lengths(key, part):
    return document_lengths(key)


def draw_assign(key, part):
    lengths = document_lengths(key)
    doc_ends = jnp.cumsum(lengths).astype(jnp.int32)
    position = jnp.arange(TOKENS, dtype=jnp.int32)
    doc_index = jnp.searchsorted(doc_ends, position, side='right').astype(jnp.int32)
    doc_start = doc_ends[doc_index] - lengths[doc_index]
    depth = position - doc_start + 1
    area = depth.reshape(NCHUNK // 4, 4, SPAN).sum(axis=2)
    order = jnp.argsort(area, axis=1, stable=True).astype(jnp.int32)
    order = order + 4 * jnp.arange(NCHUNK // 4, dtype=jnp.int32)[:, None]
    even_pair = jnp.stack([jnp.minimum(order[:, 0], order[:, 3]), jnp.maximum(order[:, 0], order[:, 3])], axis=1)
    odd_pair = jnp.stack([jnp.minimum(order[:, 1], order[:, 2]), jnp.maximum(order[:, 1], order[:, 2])], axis=1)
    return jnp.stack([even_pair, odd_pair], axis=1).reshape(NCHUNK // 2, 2).astype(jnp.int32)


def draw_queries(key, part):
    key = jax.random.fold_in(key, 3)
    return jnp.clip(jax.random.normal(key, (TOKENS, HEADS * HEAD_DIM), jnp.float32), -4.5, 4.5).astype(jnp.bfloat16)


def draw_keys(key, part):
    key = jax.random.fold_in(key, 5)
    return jnp.clip(jax.random.normal(key, (TOKENS, HEAD_DIM), jnp.float32), -4.5, 4.5).astype(jnp.bfloat16)


def block_scale(stream_key, shape, cuts, smallest, top_value):
    loudness = 1.0
    for dim, parts in cuts:
        draws = jax.random.uniform(jax.random.fold_in(jax.random.fold_in(stream_key, 6), dim), (parts,), jnp.float32, smallest / len(cuts), top_value / len(cuts))
        loudness = loudness * jnp.repeat(jnp.exp(draws), shape[dim] // parts).reshape((-1,) + (1,) * (len(shape) - 1 - dim))
    return loudness


def scatter_about(rng, dims, width, bound, cuts=(), kind=jnp.bfloat16):
    gain = block_scale(rng, dims, cuts, -0.22, 0.18) if cuts else 1.0
    array = jax.random.normal(rng, dims, jnp.float32) * width * gain
    return jnp.minimum(jnp.maximum(array, -bound), bound).astype(kind)


def setup_inputs(seed: int = 0, part: int = 0) -> dict:
    splits = jax.random.split(jax.random.key(seed), 7)
    own_keys = jax.random.split(jax.random.fold_in(splits[6], part), 7)
    return {
        "queries": draw_queries(jax.random.fold_in(jax.random.fold_in(splits[6], part), 71), part),
        "keys": draw_keys(jax.random.fold_in(jax.random.fold_in(splits[6], part), 71), part),
        "values": scatter_about(own_keys[2], (TOKENS, HEAD_DIM), 1.0, 4.5, ((0, 128),)),
        "grad_out": scatter_about(own_keys[3], (TOKENS, HEADS * HEAD_DIM), 1.0, 6.0, ((0, 128),)),
        "lengths": draw_lengths(jax.random.fold_in(splits[6], 71), part),
        "assign": draw_assign(jax.random.fold_in(splits[6], 71), part),
    }


def attend(query_block, dout_block, key_block, value_block, allowed):
    row_count = query_block.shape[0]
    inv_root = 1.0 / math.sqrt(HEAD_DIM)
    query3 = query_block.astype(jnp.float32).reshape(row_count, HEADS, HEAD_DIM)
    dout3 = dout_block.astype(jnp.float32).reshape(row_count, HEADS, HEAD_DIM)
    keys32 = key_block.astype(jnp.float32)
    values32 = value_block.astype(jnp.float32)
    scores = jnp.einsum('qhd,kd->hqk', query3, keys32) * inv_root
    scores = jnp.where(allowed[None], scores, -1e+30)
    top = lax.optimization_barrier(jnp.max(scores, axis=2, keepdims=True))
    log_total = top + jnp.log(lax.optimization_barrier(jnp.sum(jnp.exp(scores - top), axis=2, keepdims=True)))
    probs = jnp.exp(scores - log_total)
    probs_low = probs.astype(jnp.bfloat16)
    attn = jnp.einsum('hqk,kd->qhd', probs_low.astype(jnp.float32), values32).astype(jnp.bfloat16)
    delta = lax.optimization_barrier(jnp.sum(dout3 * attn.astype(jnp.float32), axis=2))
    dprobs = jnp.einsum('qhd,kd->hqk', dout3, values32)
    dscores = (probs * (dprobs - jnp.transpose(delta)[:, :, None])).astype(jnp.bfloat16)
    dscores32 = dscores.astype(jnp.float32)
    grad_query = (jnp.einsum('hqk,kd->qhd', dscores32, keys32) * inv_root).astype(jnp.bfloat16)
    grad_key = jnp.einsum('hqk,qhd->kd', dscores32, query3) * inv_root
    grad_value = jnp.einsum('hqk,qhd->kd', probs_low.astype(jnp.float32), dout3)
    return (attn.reshape(row_count, HEADS * HEAD_DIM), grad_query.reshape(row_count, HEADS * HEAD_DIM), grad_key, grad_value)

def reference(queries, keys, values, grad_out, lengths, assign):
    doc_ends = jnp.cumsum(lengths).astype(jnp.int32)
    within = jnp.arange(SPAN, dtype=jnp.int32)
    position = (assign.astype(jnp.int32)[:, :, None] * SPAN + within[None, None, :]).reshape(-1).astype(jnp.int32)
    seq_queries = jnp.zeros_like(queries).at[position].set(queries)
    seq_keys = jnp.zeros_like(keys).at[position].set(keys)
    seq_values = jnp.zeros_like(values).at[position].set(values)
    seq_dout = jnp.zeros_like(grad_out).at[position].set(grad_out)
    seq_index = jnp.arange(TOKENS, dtype=jnp.int32)
    seq_doc = jnp.searchsorted(doc_ends, seq_index, side='right').astype(jnp.int32)
    window = 5 * SPAN

    def one_span(carry, span_id):
        key_sum, value_sum = carry
        query_begin = (span_id * SPAN).astype(jnp.int32)
        key_begin = (jnp.maximum(span_id - 4, 0) * SPAN).astype(jnp.int32)
        query_block = lax.dynamic_slice_in_dim(seq_queries, query_begin, SPAN, 0)
        dout_block = lax.dynamic_slice_in_dim(seq_dout, query_begin, SPAN, 0)
        key_block = lax.dynamic_slice_in_dim(seq_keys, key_begin, window, 0)
        value_block = lax.dynamic_slice_in_dim(seq_values, key_begin, window, 0)
        query_pos = query_begin + jnp.arange(SPAN, dtype=jnp.int32)
        key_pos = key_begin + jnp.arange(window, dtype=jnp.int32)
        query_doc = lax.dynamic_slice_in_dim(seq_doc, query_begin, SPAN, 0)
        key_doc = lax.dynamic_slice_in_dim(seq_doc, key_begin, window, 0)
        allowed = (key_doc[None, :] == query_doc[:, None]) & (key_pos[None, :] <= query_pos[:, None])
        attn, grad_query, grad_key, grad_value = attend(query_block, dout_block, key_block, value_block, allowed)
        key_sum = lax.dynamic_update_slice_in_dim(key_sum, lax.dynamic_slice_in_dim(key_sum, key_begin, window, 0) + grad_key, key_begin, 0)
        value_sum = lax.dynamic_update_slice_in_dim(value_sum, lax.dynamic_slice_in_dim(value_sum, key_begin, window, 0) + grad_value, key_begin, 0)
        return ((key_sum, value_sum), (attn, grad_query))
    initial = (jnp.zeros((TOKENS, HEAD_DIM), jnp.float32), jnp.zeros((TOKENS, HEAD_DIM), jnp.float32))
    (key_sum, value_sum), (attn_blocks, query_blocks) = lax.scan(one_span, initial, jnp.arange(NCHUNK, dtype=jnp.int32))
    attn_seq = attn_blocks.reshape(TOKENS, HEADS * HEAD_DIM)
    query_seq = query_blocks.reshape(TOKENS, HEADS * HEAD_DIM)
    return (attn_seq[position], query_seq[position], key_sum[position].astype(jnp.bfloat16), value_sum[position].astype(jnp.bfloat16))
```

```python
import functools
import math

import jax
import jax.numpy as jnp
from jax import lax
from jax.experimental import pallas as pl
from jax.experimental.pallas import tpu as pltpu
from jax.sharding import PartitionSpec as P

MESH = pl.DeviceIdType.MESH
SPAN = 128
DIM = 128
REACH = 5
F32 = jnp.float32
BF16 = jnp.bfloat16
NT = (((1,), (1,)), ((), ()))
NN = (((1,), (0,)), ((), ()))


def dot(a, b, dims):
    return lax.dot_general(a, b, dims, preferred_element_type=F32)


def places(count):
    me = lax.axis_index("seq")
    core = lax.rem(me, 2)
    return me, core, me + 1 - 2 * core, lax.rem(me + 2, count), lax.rem(me + count - 2, count)


def greet(devices, grp):
    barrier = pltpu.get_barrier_semaphore()
    for device in devices:
        pl.semaphore_signal(barrier, inc=1, device_id=(device, grp), device_id_type=MESH)
    pl.semaphore_wait(barrier, len(devices))


def gather_kernel(
    count, keys, values, lens, assign, kwin, vwin, starts, padded, own_sem, far_send, far_recv,
    near_send, near_recv, relay_send, relay_recv,
):
    me, core, beside, after, before = places(count)
    grp = lax.axis_index("grp")
    greet((beside, after, before), grp)

    def remote(src, dst, send, recv, device):
        return pltpu.make_async_remote_copy(
            src_ref=src, dst_ref=dst, send_sem=send, recv_sem=recv,
            device_id=(device, grp), device_id_type=MESH,
        )

    arrays = ((keys, kwin), (values, vwin))
    far, near, relay, own = [], [], [], []
    for span in range(2):
        for which, (src, win) in enumerate(arrays):
            slot = 2 * span + which
            far.append(remote(
                src.at[span], win.at[2 * core + span], far_send.at[slot], far_recv.at[slot], after))
            relay.append(remote(
                win.at[2 * core + span], win.at[2 * core + span],
                relay_send.at[slot], relay_recv.at[slot], beside))
    for which, (src, win) in enumerate(arrays):
        mine = win.at[pl.ds(4 + 2 * core, 2)]
        near.append(remote(src, mine, near_send.at[which], near_recv.at[which], beside))
        own.append(pltpu.make_async_copy(src, mine, own_sem.at[which]))
    for copy in far + near + own:
        copy.start()

    docs = lens.shape[1]
    wide = padded.shape[1]
    padded[...] = jnp.zeros_like(padded)
    padded[0:1, 0:docs] = lens[...]
    length = padded[...]
    high = length >> 8
    low = length - (high << 8)
    row = lax.broadcasted_iota(jnp.int32, (8, wide), 0)
    both = jnp.where(row == 1, pltpu.roll(low, 1, 0), high).astype(F32).astype(BF16)
    until = lax.broadcasted_iota(jnp.int32, (wide, wide), 0)
    upto = lax.broadcasted_iota(jnp.int32, (wide, wide), 1)
    lower = jnp.where(upto <= until, 1.0, 0.0).astype(BF16)
    sums = dot(lower, both, NT)
    ends = sums[:, 0:1] * 256.0 + sums[:, 1:2]
    for half in range(2):
        base = assign[me, half] * SPAN
        pos = (base + lax.broadcasted_iota(jnp.int32, (1, SPAN), 1)).astype(F32)
        start = jnp.max(jnp.where(ends <= pos, ends, 0.0), axis=0, keepdims=True)
        starts[:, half * SPAN : (half + 1) * SPAN] = jnp.broadcast_to(
            start, (8, SPAN)).astype(jnp.int32)

    for slot in range(4):
        far[slot].wait_recv()
        relay[slot].start()
    for copy in own:
        copy.wait()
    for copy in near:
        copy.wait()
    for slot in range(4):
        far[slot].wait_send()
        relay[slot].wait()


def attend_kernel(
    count, assign, first, queries, dout, kwin, vwin, starts, attn, dqueries, mine, theirs,
    kblk, vblk, ktr, vtr, bias, dkey, dvalue, part,
):
    half = pl.program_id(0)
    me, core, _, _, _ = places(count)
    chip = me // 2
    prev = lax.rem(chip + count // 2 - 1, count // 2)
    wrapped = jnp.where(chip == 0, 2 * count, 0)
    ids = [assign[2 * prev + w // 2, w % 2] - wrapped for w in range(4)]
    ids += [assign[2 * chip + w // 2, w % 2] for w in range(4)]
    span = assign[me, half]
    slots = []
    for back in range(REACH):
        slot = jnp.int32(0)
        for w in range(8):
            slot = jnp.where(ids[w] == span - back, w, slot)
        slots.append(slot)
    needed = span - first[0, half * SPAN] // SPAN + 1
    root = 1.0 / math.sqrt(DIM)
    scale = root * math.log2(math.e)
    heads = queries.shape[1] // DIM

    @pl.when(half == 0)
    def _():
        part[...] = jnp.zeros_like(part)

    def window(back):
        rows = slice(back * SPAN, (back + 1) * SPAN)
        kb = kwin[slots[back]]
        vb = vwin[slots[back]]
        kblk[rows] = kb
        vblk[rows] = vb
        ktr[:, rows] = kb.T
        vtr[:, rows] = vb.T
        kpos = (span - back) * SPAN + lax.broadcasted_iota(jnp.int32, (SPAN, SPAN), 0)
        qpos = span * SPAN + lax.broadcasted_iota(jnp.int32, (SPAN, SPAN), 1)
        ok = (kpos >= starts[0:1, :]) & (kpos <= qpos)
        bias[rows] = jnp.where(ok, 0.0, -1e30)

    def pair(reach, group):
        rows = slice(0, reach * SPAN)
        cols = pl.ds(pl.multiple_of(group * 2 * DIM, 2 * DIM), 2 * DIM)
        q2 = queries[:, cols]
        g2 = dout[:, cols]
        qr = jnp.concatenate([q2[:, :DIM], q2[:, DIM:]], axis=0)
        gr = jnp.concatenate([g2[:, :DIM], g2[:, DIM:]], axis=0)
        mask = bias[rows]
        scores = dot(kblk[rows], qr, NT) * scale + jnp.concatenate([mask, mask], axis=1)
        top = jnp.max(scores, axis=0, keepdims=True)
        raw = jnp.exp2(scores - top)
        probs = raw * (1.0 / jnp.sum(raw, axis=0, keepdims=True))
        low = probs.astype(BF16)
        dprobs = dot(vblk[rows], gr, NT)
        delta = jnp.sum(probs * dprobs, axis=0, keepdims=True)
        ds = (probs * (dprobs - delta)).astype(BF16)
        out = dot(vtr[:, rows], low, NN)
        dq = dot(ktr[:, rows], ds, NN) * root
        attn[:, cols] = jnp.concatenate([out[:, :SPAN].T, out[:, SPAN:].T], axis=1).astype(BF16)
        dqueries[:, cols] = jnp.concatenate([dq[:, :SPAN].T, dq[:, SPAN:].T], axis=1).astype(BF16)
        return dot(ds, qr, NN), dot(low, gr, NN)

    for reach in range(1, REACH + 1):

        @pl.when(needed == reach)
        def _(reach=reach):
            rows = slice(0, reach * SPAN)
            for back in range(reach):
                window(back)

            def step(i, carry):
                dk, dv = pair(reach, 2 * i)
                dk2, dv2 = pair(reach, 2 * i + 1)
                dk = dk + dk2
                dv = dv + dv2

                @pl.when(i == 0)
                def _():
                    dkey[rows] = dk
                    dvalue[rows] = dv

                @pl.when(i > 0)
                def _():
                    dkey[rows] += dk
                    dvalue[rows] += dv

                return carry

            lax.fori_loop(0, heads // 4, step, 0)
            for back in range(reach):
                part[slots[back], :, 0:DIM] += dkey[back * SPAN : (back + 1) * SPAN] * root
                part[slots[back], :, DIM:] += dvalue[back * SPAN : (back + 1) * SPAN]

    @pl.when(half == 1)
    def _():
        for i in range(2):
            mine[i] = part[2 * core + i]
            mine[2 + i] = part[4 + 2 * core + i]
            theirs[i] = part[2 - 2 * core + i].astype(BF16)
            theirs[2 + i] = part[6 - 2 * core + i].astype(BF16)


def reduce_kernel(
    count, mine, theirs, dkeys, dvalues, near_buf, out_buf, far_buf, near_send, near_recv,
    far_send, far_recv,
):
    _, core, beside, after, before = places(count)
    grp = lax.axis_index("grp")
    greet((beside, after, before), grp)

    def remote(src, dst, send, recv, device):
        return pltpu.make_async_remote_copy(
            src_ref=src, dst_ref=dst, send_sem=send, recv_sem=recv,
            device_id=(device, grp), device_id_type=MESH,
        )

    near = [
        remote(theirs.at[i], near_buf.at[i], near_send.at[i], near_recv.at[i], beside)
        for i in range(4)
    ]
    far = [
        remote(out_buf.at[i], far_buf.at[i], far_send.at[i], far_recv.at[i], before)
        for i in range(2)
    ]
    for copy in near:
        copy.start()
    for i in range(2):
        near[i].wait_recv()
        out_buf[i] = (mine[i] + near_buf[i].astype(F32)).astype(BF16)
        far[i].start()
    for i in range(2):
        near[2 + i].wait_recv()
    for i in range(2):
        far[i].wait_recv()
        total = mine[2 + i] + near_buf[2 + i].astype(F32) + far_buf[i].astype(F32)
        dkeys[i] = total[:, 0:DIM].astype(BF16)
        dvalues[i] = total[:, DIM:].astype(BF16)
    for copy in near + far:
        copy.wait_send()


def shards(count, queries, keys, values, grad_out, lengths, assign):
    width = queries.shape[1]
    any_spec = pl.BlockSpec(memory_space=pl.ANY)
    vmem = pl.BlockSpec(memory_space=pltpu.VMEM)
    smem = pl.BlockSpec(memory_space=pltpu.SMEM)
    dma = pltpu.SemaphoreType.DMA
    docs = lengths.shape[0]
    wide = -(-docs // 128) * 128
    shape = jax.ShapeDtypeStruct
    kwin, vwin, starts = pl.pallas_call(
        functools.partial(gather_kernel, count),
        out_shape=(
            shape((8, SPAN, DIM), BF16),
            shape((8, SPAN, DIM), BF16),
            shape((8, 2 * SPAN), jnp.int32),
        ),
        in_specs=[any_spec, any_spec, vmem, smem],
        out_specs=(any_spec, any_spec, vmem),
        scratch_shapes=[
            pltpu.VMEM((8, wide), jnp.int32),
            dma((2,)), dma((4,)), dma((4,)), dma((2,)), dma((2,)), dma((4,)), dma((4,)),
        ],
        compiler_params=pltpu.CompilerParams(
            collective_id=0, has_side_effects=True, vmem_limit_bytes=16 * 2**20),
        name="gather",
    )(
        keys.reshape(2, SPAN, DIM), values.reshape(2, SPAN, DIM), lengths.reshape(1, docs), assign
    )

    rows = pl.BlockSpec((SPAN, width), lambda half: (half, 0))
    attn, dqueries, mine, theirs = pl.pallas_call(
        functools.partial(attend_kernel, count),
        grid=(2,),
        out_shape=(
            shape((2 * SPAN, width), BF16),
            shape((2 * SPAN, width), BF16),
            shape((4, SPAN, 2 * DIM), F32),
            shape((4, SPAN, 2 * DIM), BF16),
        ),
        in_specs=[
            smem, smem, rows, rows,
            pl.BlockSpec((8, SPAN, DIM), lambda half: (0, 0, 0)),
            pl.BlockSpec((8, SPAN, DIM), lambda half: (0, 0, 0)),
            pl.BlockSpec((8, SPAN), lambda half: (0, half)),
        ],
        out_specs=(
            rows, rows,
            pl.BlockSpec((4, SPAN, 2 * DIM), lambda half: (0, 0, 0)),
            pl.BlockSpec((4, SPAN, 2 * DIM), lambda half: (0, 0, 0)),
        ),
        scratch_shapes=[
            pltpu.VMEM((REACH * SPAN, DIM), BF16),
            pltpu.VMEM((REACH * SPAN, DIM), BF16),
            pltpu.VMEM((DIM, REACH * SPAN), BF16),
            pltpu.VMEM((DIM, REACH * SPAN), BF16),
            pltpu.VMEM((REACH * SPAN, SPAN), F32),
            pltpu.VMEM((REACH * SPAN, DIM), F32),
            pltpu.VMEM((REACH * SPAN, DIM), F32),
            pltpu.VMEM((8, SPAN, 2 * DIM), F32),
        ],
        compiler_params=pltpu.CompilerParams(
            dimension_semantics=("arbitrary",), vmem_limit_bytes=40 * 2**20),
        name="attend",
    )(assign, starts, queries, grad_out, kwin, vwin, starts)

    dkeys, dvalues = pl.pallas_call(
        functools.partial(reduce_kernel, count),
        out_shape=(shape((2, SPAN, DIM), BF16), shape((2, SPAN, DIM), BF16)),
        in_specs=[vmem, vmem],
        out_specs=(vmem, vmem),
        scratch_shapes=[
            pltpu.VMEM((4, SPAN, 2 * DIM), BF16),
            pltpu.VMEM((2, SPAN, 2 * DIM), BF16),
            pltpu.VMEM((2, SPAN, 2 * DIM), BF16),
            dma((4,)), dma((4,)), dma((2,)), dma((2,)),
        ],
        compiler_params=pltpu.CompilerParams(
            collective_id=1, has_side_effects=True, vmem_limit_bytes=16 * 2**20),
        name="reduce",
    )(mine, theirs)
    return (
        attn, dqueries, dkeys.reshape(2 * SPAN, DIM), dvalues.reshape(2 * SPAN, DIM))


def solution(mesh):
    split = P("seq", "grp")
    return jax.shard_map(
        functools.partial(shards, mesh.shape["seq"]),
        mesh=mesh,
        in_specs=(split, split, split, split, P(), P()),
        out_specs=(split, split, split, split),
        check_vma=False,
    )
```

```python
import functools
import math

import jax
import jax.numpy as jnp
from jax import lax
from jax.experimental import pallas as pl
from jax.experimental.pallas import tpu as pltpu
from jax.sharding import PartitionSpec as P

MESH = pl.DeviceIdType.MESH
SPAN = 128
DIM = 128
GROUP = 4
F32 = jnp.float32
BF16 = jnp.bfloat16
NT = (((1,), (1,)), ((), ()))
NN = (((1,), (0,)), ((), ()))
ROOT = 1.0 / math.sqrt(DIM)


def dot(a, b, dims):
    return lax.dot_general(a, b, dims, preferred_element_type=F32)


def pick(values, wanted):
    index = jnp.int32(0)
    for i, value in enumerate(values):
        index = jnp.where(value == wanted, i, index)
    return index


def twice(x):
    return jnp.concatenate([x, x], axis=1)


def spans(x):
    return x.reshape(x.shape[0] // SPAN, SPAN, x.shape[1])


def main_kernel(
    count, q, g, k, v, lens, assign, attn, dq, dk, dv,
    lens_v, assign_s, padded, qslot, gslot, kown, vown, kprev, vprev, qr, gr,
    ko, vo, kot, vot, kp, vp, kpt, vpt, bias, expo, dpo, pb, sb, oto, stat,
    part_p, part_o, sum_send, sum_near, far_send_buf, far_buf, own_send, own_near,
    oq_mine, oq_near0, oq_near1,
    loc_sem, far_ks, far_kr, far_vs, far_vr, rel_ks, rel_kr, rel_vs, rel_vr,
    near_s, near_r, p_s, p_r, f_s, f_r, o_s, o_r, oq_s, oq_r,
):
    me = lax.axis_index("seq")
    grp = lax.axis_index("grp")
    core = lax.rem(me, 2)
    other = 1 - core
    chip = me // 2
    beside = me + 1 - 2 * core
    has_prev = chip > 0
    has_next = chip < count // 2 - 1
    before = jnp.where(has_prev, me - 2, me)
    after = jnp.where(has_next, me + 2, me)
    width = q.shape[2] // 2
    pairs = width // (2 * DIM)

    def remote(src, dst, send, recv, device):
        return pltpu.make_async_remote_copy(
            src_ref=src, dst_ref=dst, send_sem=send, recv_sem=recv,
            device_id=(device, grp), device_id_type=MESH,
        )

    def columns(which):
        return pl.ds(pl.multiple_of(which * width, width), width)

    own_slots = pl.ds(2 * core, 2)
    local = [
        pltpu.make_async_copy(k, kown.at[own_slots], loc_sem.at[0]),
        pltpu.make_async_copy(v, vown.at[own_slots], loc_sem.at[1]),
        pltpu.make_async_copy(lens, lens_v, loc_sem.at[2]),
        pltpu.make_async_copy(assign, assign_s, loc_sem.at[3]),
        pltpu.make_async_copy(q.at[:, :, columns(core)], qslot.at[own_slots], loc_sem.at[4]),
        pltpu.make_async_copy(g.at[:, :, columns(core)], gslot.at[own_slots], loc_sem.at[5]),
    ]
    far_k = [remote(k.at[a], kprev.at[2 * core + a], far_ks.at[a], far_kr.at[a], after)
             for a in range(2)]
    far_v = [remote(v.at[a], vprev.at[2 * core + a], far_vs.at[a], far_vr.at[a], after)
             for a in range(2)]
    relay_k = [remote(kprev.at[2 * core + a], kprev.at[2 * core + a], rel_ks.at[a], rel_kr.at[a],
                      beside) for a in range(2)]
    relay_v = [remote(vprev.at[2 * core + a], vprev.at[2 * core + a], rel_vs.at[a], rel_vr.at[a],
                      beside) for a in range(2)]
    near = [
        remote(k, kown.at[own_slots], near_s.at[0], near_r.at[0], beside),
        remote(v, vown.at[own_slots], near_s.at[1], near_r.at[1], beside),
        remote(q.at[:, :, columns(other)], qslot.at[own_slots], near_s.at[2], near_r.at[2], beside),
        remote(g.at[:, :, columns(other)], gslot.at[own_slots], near_s.at[3], near_r.at[3], beside),
    ]

    barrier = pltpu.get_barrier_semaphore()
    pl.semaphore_signal(barrier, inc=1, device_id=(beside, grp), device_id_type=MESH)

    @pl.when(has_prev)
    def _():
        pl.semaphore_signal(barrier, inc=1, device_id=(before, grp), device_id_type=MESH)

    @pl.when(has_next)
    def _():
        pl.semaphore_signal(barrier, inc=1, device_id=(after, grp), device_id_type=MESH)

    for copy in local:
        copy.start()
    pl.semaphore_wait(
        barrier, 1 + has_prev.astype(jnp.int32) + has_next.astype(jnp.int32))

    @pl.when(has_next)
    def _():
        for copy in far_k + far_v:
            copy.start()

    for copy in near:
        copy.start()

    docs = lens_v.shape[0]
    wide = padded.shape[1]
    padded[...] = jnp.zeros_like(padded)
    local[2].wait()
    padded[0:1, 0:docs] = lens_v[...].reshape(1, docs)
    length = padded[...]
    high = length >> 8
    low = length - (high << 8)
    row8 = lax.broadcasted_iota(jnp.int32, (8, wide), 0)
    both = jnp.where(row8 == 1, pltpu.roll(low, 1, 0), high).astype(F32).astype(BF16)
    until = lax.broadcasted_iota(jnp.int32, (wide, wide), 0)
    upto = lax.broadcasted_iota(jnp.int32, (wide, wide), 1)
    lower = jnp.where(upto <= until, 1.0, 0.0).astype(BF16)
    sums = dot(lower, both, NT)
    base = chip * (GROUP * SPAN)
    ends = sums[:, 0:1] * 256.0 + sums[:, 1:2] - base.astype(F32)
    least = -base.astype(F32)
    key_row = lax.broadcasted_iota(jnp.int32, (SPAN, SPAN), 0).astype(F32)
    query_col = lax.broadcasted_iota(jnp.int32, (SPAN, SPAN), 1).astype(F32)
    for j in range(GROUP):
        pos = query_col[0:1] + float(j * SPAN)
        start = jnp.max(jnp.where(ends <= pos, ends, least), axis=0, keepdims=True)
        for b in range(GROUP + 1):
            key = b if b <= j else b - 1 - GROUP
            ok = key_row + float(key * SPAN) >= start
            if b == j:
                ok = ok & (key_row <= query_col)
            bias[j, b * SPAN : (b + 1) * SPAN] = jnp.where(ok, 0.0, -1e30)

    local[3].wait()
    back = jnp.maximum(chip - 1, 0)
    here = [assign_s[s % 2, 2 * chip + s // 2] & (GROUP - 1) for s in range(GROUP)]
    there = [assign_s[s % 2, 2 * back + s // 2] & (GROUP - 1) for s in range(GROUP)]
    for copy in (local[0], local[1], local[4], local[5]):
        copy.wait()
    for copy in near:
        copy.wait_recv()
    for j in range(GROUP):
        slot = pick(here, j)
        rows = slice(j * SPAN, (j + 1) * SPAN)
        kb = kown[slot]
        vb = vown[slot]
        ko[rows] = kb
        vo[rows] = vb
        kot[:, rows] = kb.T
        vot[:, rows] = vb.T
        qb = qslot[slot]
        gb = gslot[slot]
        for h in range(2 * pairs):
            qr[j, h * SPAN : (h + 1) * SPAN] = qb[:, h * DIM : (h + 1) * DIM]
            gr[j, h * SPAN : (h + 1) * SPAN] = gb[:, h * DIM : (h + 1) * DIM]

    scale = ROOT * math.log2(math.e)
    part_p[...] = jnp.zeros_like(part_p)
    part_o[...] = jnp.zeros_like(part_o)

    def heads(p):
        return pl.ds(pl.multiple_of(p * 2 * SPAN, 2 * SPAN), 2 * SPAN)

    def own_scores(p, carry):
        for j in range(GROUP):
            n = (j + 1) * SPAN
            qj = qr[j, heads(p)]
            gj = gr[j, heads(p)]
            s = dot(ko[0:n], qj, NT) * scale + twice(bias[j, 0:n])
            m = jnp.max(s, axis=0, keepdims=True)
            e = jnp.exp2(s - m)
            expo[p, j, 0:n] = e
            dp = dot(vo[0:n], gj, NT)
            dpo[p, j, 0:n] = dp
            stat[p, j, 0:1] = m
            stat[p, j, 1:2] = jnp.sum(e, axis=0, keepdims=True)
            stat[p, j, 2:3] = jnp.sum(e * dp, axis=0, keepdims=True)
            oto[p, j] = dot(vot[:, 0:n], e.astype(BF16), NN)
        return carry

    lax.fori_loop(0, pairs, own_scores, 0)

    @pl.when(has_prev)
    def _():
        for a in range(2):
            far_k[a].wait_recv()
            relay_k[a].start()
        for a in range(2):
            relay_k[a].wait_recv()

    @pl.when(jnp.logical_not(has_prev))
    def _():
        kprev[...] = jnp.zeros_like(kprev)
        vprev[...] = jnp.zeros_like(vprev)

    for i in range(GROUP):
        rows = slice(i * SPAN, (i + 1) * SPAN)
        kb = kprev[pick(there, i)]
        kp[rows] = kb
        kpt[:, rows] = kb.T

    def prev_scores(p, carry):
        for j in range(GROUP):
            at = (j + 1) * SPAN
            s = dot(kp[j * SPAN :], qr[j, heads(p)], NT) * scale + twice(bias[j, at:])
            mo = stat[p, j, 0:1]
            m = jnp.maximum(mo, jnp.max(s, axis=0, keepdims=True))
            e = jnp.exp2(s - m)
            shrink = jnp.exp2(mo - m)
            r = 1.0 / (stat[p, j, 1:2] * shrink + jnp.sum(e, axis=0, keepdims=True))
            expo[p, j, at:] = e * r
            stat[p, j, 3:4] = shrink * r
        return carry

    lax.fori_loop(0, pairs, prev_scores, 0)

    @pl.when(has_prev)
    def _():
        for a in range(2):
            far_v[a].wait_recv()
            relay_v[a].start()
        for a in range(2):
            relay_v[a].wait_recv()

    for i in range(GROUP):
        rows = slice(i * SPAN, (i + 1) * SPAN)
        vb = vprev[pick(there, i)]
        vp[rows] = vb
        vpt[:, rows] = vb.T

    def prev_grads(p, carry):
        for j in range(GROUP):
            at = (j + 1) * SPAN
            qj = qr[j, heads(p)]
            gj = gr[j, heads(p)]
            dp = dot(vp[j * SPAN :], gj, NT)
            pr = expo[p, j, at:]
            delta = stat[p, j, 3:4] * stat[p, j, 2:3] + jnp.sum(pr * dp, axis=0, keepdims=True)
            stat[p, j, 4:5] = delta
            ds = (pr * (dp - delta)).astype(BF16)
            low = pr.astype(BF16)
            pb[p, j, at:] = low
            sb[p, j, at:] = ds
            part_p[j:, :, 0:DIM] += spans(dot(ds, qj, NN) * ROOT)
            part_p[j:, :, DIM:] += spans(dot(low, gj, NN))
        return carry

    lax.fori_loop(0, pairs, prev_grads, 0)

    def mine_of(spans, a):
        return jnp.where(core == 0, spans[a], spans[2 + a])

    def theirs_of(spans, a):
        return jnp.where(core == 0, spans[2 + a], spans[a])

    swap_p = [remote(sum_send.at[a], sum_near.at[a], p_s.at[a], p_r.at[a], beside)
              for a in range(2)]
    far_p = [remote(far_send_buf.at[a], far_buf.at[a], f_s.at[a], f_r.at[a], before)
             for a in range(2)]
    for a in range(2):
        sum_send[a] = part_p[theirs_of(there, a)].astype(BF16)
        swap_p[a].start()

    oq_near = (oq_near0, oq_near1)
    swap_oq = [remote(oq_mine.at[p], oq_near[p], oq_s.at[p], oq_r.at[p], beside)
               for p in range(pairs)]

    def own_grads(p):
        for j in range(GROUP):
            n = (j + 1) * SPAN
            qj = qr[j, heads(p)]
            gj = gr[j, heads(p)]
            alpha = stat[p, j, 3:4]
            pr = expo[p, j, 0:n] * alpha
            ds = (pr * (dpo[p, j, 0:n] - stat[p, j, 4:5])).astype(BF16)
            low = pr.astype(BF16)
            part_o[0 : j + 1, :, 0:DIM] += spans(dot(ds, qj, NN) * ROOT)
            part_o[0 : j + 1, :, DIM:] += spans(dot(low, gj, NN))
            out = oto[p, j] * alpha + dot(vpt[:, j * SPAN :], pb[p, j, n:], NN)
            dqt = dot(kot[:, 0:n], ds, NN) + dot(kpt[:, j * SPAN :], sb[p, j, n:], NN)
            dqt = dqt * ROOT
            for h in range(2):
                cols = slice(h * DIM, (h + 1) * DIM)
                oq_mine[p, 0, j, :, cols] = out[:, cols].T.astype(BF16)
                oq_mine[p, 1, j, :, cols] = dqt[:, cols].T.astype(BF16)

    own_grads(0)
    swap_oq[0].start()

    for a in range(2):
        swap_p[a].wait_recv()
        far_send_buf[a] = (
            part_p[mine_of(there, a)] + sum_near[a].astype(F32)).astype(BF16)

        @pl.when(has_prev)
        def _(a=a):
            far_p[a].start()

    for p in range(1, pairs):
        own_grads(p)
        swap_oq[p].start()

    swap_o = [remote(own_send.at[a], own_near.at[a], o_s.at[a], o_r.at[a], beside)
              for a in range(2)]
    for a in range(2):
        own_send[a] = part_o[theirs_of(here, a)].astype(BF16)
        swap_o[a].start()

    for p in range(pairs):
        swap_oq[p].wait_recv()
        for a in range(2):
            j = mine_of(here, a)
            for half, source in ((core, oq_mine.at[p]), (other, oq_near[p])):
                cols = pl.ds(
                    pl.multiple_of(half * width + p * 2 * DIM, 2 * DIM), 2 * DIM)
                attn[a, :, cols] = source[0, j]
                dq[a, :, cols] = source[1, j]

    @pl.when(jnp.logical_not(has_next))
    def _():
        far_buf[...] = jnp.zeros_like(far_buf)

    for a in range(2):
        swap_o[a].wait_recv()

        @pl.when(has_next)
        def _(a=a):
            far_p[a].wait_recv()

        total = part_o[mine_of(here, a)] + own_near[a].astype(F32) + far_buf[a].astype(F32)
        dk[a] = total[:, 0:DIM].astype(BF16)
        dv[a] = total[:, DIM:].astype(BF16)

    for copy in near + swap_p + swap_oq + swap_o:
        copy.wait_send()

    @pl.when(has_next)
    def _():
        for copy in far_k + far_v:
            copy.wait_send()

    @pl.when(has_prev)
    def _():
        for copy in relay_k + relay_v + far_p:
            copy.wait_send()


def store_kernel(*refs):
    n = (len(refs) - 1) // 2
    copies = [
        pltpu.make_async_copy(refs[i], refs[n + i], refs[2 * n].at[i]) for i in range(n)
    ]
    for copy in copies:
        copy.start()
    for copy in copies:
        copy.wait()


def shards(count, queries, keys, values, grad_out, lengths, assign):
    width = queries.shape[1]
    half = width // 2
    pairs = half // (2 * DIM)
    docs = lengths.shape[0]
    wide = -(-docs // 128) * 128
    hbm = pl.BlockSpec(memory_space=pltpu.HBM)
    vmem = pl.BlockSpec(memory_space=pltpu.VMEM)
    dma = pltpu.SemaphoreType.DMA
    shape = jax.ShapeDtypeStruct
    keyed = GROUP * SPAN
    seen = keyed + SPAN
    outs = (
        shape((2, SPAN, width), BF16),
        shape((2, SPAN, width), BF16),
        shape((2, SPAN, DIM), BF16),
        shape((2, SPAN, DIM), BF16),
    )
    results = pl.pallas_call(
        functools.partial(main_kernel, count),
        out_shape=outs,
        in_specs=[hbm] * 6,
        out_specs=(vmem,) * 4,
        scratch_shapes=[
            pltpu.VMEM((docs,), jnp.int32),
            pltpu.SMEM(assign.shape[::-1], jnp.int32),
            pltpu.VMEM((8, wide), jnp.int32),
            pltpu.VMEM((GROUP, SPAN, half), BF16),
            pltpu.VMEM((GROUP, SPAN, half), BF16),
            pltpu.VMEM((GROUP, SPAN, DIM), BF16),
            pltpu.VMEM((GROUP, SPAN, DIM), BF16),
            pltpu.VMEM((GROUP, SPAN, DIM), BF16),
            pltpu.VMEM((GROUP, SPAN, DIM), BF16),
            pltpu.VMEM((GROUP, half, DIM), BF16),
            pltpu.VMEM((GROUP, half, DIM), BF16),
            pltpu.VMEM((keyed, DIM), BF16),
            pltpu.VMEM((keyed, DIM), BF16),
            pltpu.VMEM((DIM, keyed), BF16),
            pltpu.VMEM((DIM, keyed), BF16),
            pltpu.VMEM((keyed, DIM), BF16),
            pltpu.VMEM((keyed, DIM), BF16),
            pltpu.VMEM((DIM, keyed), BF16),
            pltpu.VMEM((DIM, keyed), BF16),
            pltpu.VMEM((GROUP, seen, SPAN), F32),
            pltpu.VMEM((pairs, GROUP, seen, 2 * SPAN), F32),
            pltpu.VMEM((pairs, GROUP, keyed, 2 * SPAN), F32),
            pltpu.VMEM((pairs, GROUP, seen, 2 * SPAN), BF16),
            pltpu.VMEM((pairs, GROUP, seen, 2 * SPAN), BF16),
            pltpu.VMEM((pairs, GROUP, DIM, 2 * SPAN), F32),
            pltpu.VMEM((pairs, GROUP, 8, 2 * SPAN), F32),
            pltpu.VMEM((GROUP, SPAN, 2 * DIM), F32),
            pltpu.VMEM((GROUP, SPAN, 2 * DIM), F32),
            pltpu.VMEM((2, SPAN, 2 * DIM), BF16),
            pltpu.VMEM((2, SPAN, 2 * DIM), BF16),
            pltpu.VMEM((2, SPAN, 2 * DIM), BF16),
            pltpu.VMEM((2, SPAN, 2 * DIM), BF16),
            pltpu.VMEM((2, SPAN, 2 * DIM), BF16),
            pltpu.VMEM((2, SPAN, 2 * DIM), BF16),
            pltpu.VMEM((pairs, 2, GROUP, SPAN, 2 * DIM), BF16),
            pltpu.VMEM((2, GROUP, SPAN, 2 * DIM), BF16),
            pltpu.VMEM((2, GROUP, SPAN, 2 * DIM), BF16),
            dma((6,)),
            dma((2,)), dma((2,)), dma((2,)), dma((2,)),
            dma((2,)), dma((2,)), dma((2,)), dma((2,)),
            dma((4,)), dma((4,)),
            dma((2,)), dma((2,)), dma((2,)), dma((2,)), dma((2,)), dma((2,)),
            dma((pairs,)), dma((pairs,)),
        ],
        compiler_params=pltpu.CompilerParams(
            collective_id=0, has_side_effects=True, vmem_limit_bytes=40 * 2**20),
        name="attend",
    )(*[
        pltpu.with_memory_space_constraint(x, pltpu.HBM)
        for x in (
            queries.reshape(2, SPAN, width), grad_out.reshape(2, SPAN, width),
            keys.reshape(2, SPAN, DIM), values.reshape(2, SPAN, DIM), lengths, assign.T,
        )
    ])
    results = pl.pallas_call(
        store_kernel,
        out_shape=outs,
        in_specs=[pl.BlockSpec(memory_space=pl.ANY)] * 4,
        out_specs=(hbm,) * 4,
        scratch_shapes=[dma((4,))],
        name="store",
    )(*results)
    return tuple(r.reshape(2 * SPAN, r.shape[2]) for r in results)


def solution(mesh):
    split = P("seq", "grp")
    return jax.shard_map(
        functools.partial(shards, mesh.shape["seq"]),
        mesh=mesh,
        in_specs=(split, split, split, split, P(), P()),
        out_specs=(split, split, split, split),
        check_vma=False,
    )
```

```python
import functools
import math

import jax
import jax.numpy as jnp
from jax import lax
from jax.experimental import pallas as pl
from jax.experimental.pallas import tpu as pltpu
from jax.sharding import PartitionSpec as P

MESH = pl.DeviceIdType.MESH
SPAN = 128
DIM = 128
GROUP = 4
F32 = jnp.float32
BF16 = jnp.bfloat16
NT = (((1,), (1,)), ((), ()))
NN = (((1,), (0,)), ((), ()))
ROOT = 1.0 / math.sqrt(DIM)


def dot(a, b, dims):
    return lax.dot_general(a, b, dims, preferred_element_type=F32)


def pick(values, wanted):
    index = jnp.int32(0)
    for i, value in enumerate(values):
        index = jnp.where(value == wanted, i, index)
    return index


def every_head(x, heads):
    return jnp.concatenate([x] * heads, axis=1)


def spans(x):
    return x.reshape(x.shape[0] // SPAN, SPAN, x.shape[1])


def main_kernel(
    count, q, g, k, v, lens, assign, attn, dq, dk, dv,
    lens_v, assign_s, padded, qslot, gslot, kown, vown, kprev, vprev, qr, gr,
    ko, vo, kot, vot, kp, vp, kpt, vpt, bias, expo, dpo, pb, sb, oto, stat,
    part_p, part_o, sum_send, sum_near, far_send_buf, far_buf, own_send, own_near,
    oq_mine, oq_near,
    loc_sem, far_ks, far_kr, far_vs, far_vr, rel_ks, rel_kr, rel_vs, rel_vr,
    near_s, near_r, p_s, p_r, f_s, f_r, o_s, o_r, oq_s, oq_r,
):
    me = lax.axis_index("seq")
    grp = lax.axis_index("grp")
    core = lax.rem(me, 2)
    other = 1 - core
    chip = me // 2
    beside = me + 1 - 2 * core
    has_prev = chip > 0
    has_next = chip < count // 2 - 1
    before = jnp.where(has_prev, me - 2, me)
    after = jnp.where(has_next, me + 2, me)
    width = q.shape[2] // 2
    heads = width // DIM

    def remote(src, dst, send, recv, device):
        return pltpu.make_async_remote_copy(
            src_ref=src, dst_ref=dst, send_sem=send, recv_sem=recv,
            device_id=(device, grp), device_id_type=MESH,
        )

    def columns(which):
        return pl.ds(pl.multiple_of(which * width, width), width)

    own_slots = pl.ds(2 * core, 2)
    local = [
        pltpu.make_async_copy(k, kown.at[own_slots], loc_sem.at[0]),
        pltpu.make_async_copy(v, vown.at[own_slots], loc_sem.at[1]),
        pltpu.make_async_copy(lens, lens_v, loc_sem.at[2]),
        pltpu.make_async_copy(assign, assign_s, loc_sem.at[3]),
        pltpu.make_async_copy(q.at[:, :, columns(core)], qslot.at[own_slots], loc_sem.at[4]),
        pltpu.make_async_copy(g.at[:, :, columns(core)], gslot.at[own_slots], loc_sem.at[5]),
    ]
    far_k = [remote(k.at[a], kprev.at[2 * core + a], far_ks.at[a], far_kr.at[a], after)
             for a in range(2)]
    far_v = [remote(v.at[a], vprev.at[2 * core + a], far_vs.at[a], far_vr.at[a], after)
             for a in range(2)]
    relay_k = [remote(kprev.at[2 * core + a], kprev.at[2 * core + a], rel_ks.at[a], rel_kr.at[a],
                      beside) for a in range(2)]
    relay_v = [remote(vprev.at[2 * core + a], vprev.at[2 * core + a], rel_vs.at[a], rel_vr.at[a],
                      beside) for a in range(2)]
    near = [
        remote(k, kown.at[own_slots], near_s.at[0], near_r.at[0], beside),
        remote(v, vown.at[own_slots], near_s.at[1], near_r.at[1], beside),
        remote(q.at[:, :, columns(other)], qslot.at[own_slots], near_s.at[2], near_r.at[2], beside),
        remote(g.at[:, :, columns(other)], gslot.at[own_slots], near_s.at[3], near_r.at[3], beside),
    ]

    barrier = pltpu.get_barrier_semaphore()
    pl.semaphore_signal(barrier, inc=1, device_id=(beside, grp), device_id_type=MESH)

    @pl.when(has_prev)
    def _():
        pl.semaphore_signal(barrier, inc=1, device_id=(before, grp), device_id_type=MESH)

    @pl.when(has_next)
    def _():
        pl.semaphore_signal(barrier, inc=1, device_id=(after, grp), device_id_type=MESH)

    for copy in local:
        copy.start()
    pl.semaphore_wait(
        barrier, 1 + has_prev.astype(jnp.int32) + has_next.astype(jnp.int32))

    @pl.when(has_next)
    def _():
        for copy in far_k + far_v:
            copy.start()

    for copy in near:
        copy.start()

    docs = lens_v.shape[0]
    wide = padded.shape[1]
    padded[...] = jnp.zeros_like(padded)
    local[2].wait()
    padded[0:1, 0:docs] = lens_v[...].reshape(1, docs)
    length = padded[...]
    high = length >> 8
    low = length - (high << 8)
    row8 = lax.broadcasted_iota(jnp.int32, (8, wide), 0)
    both = jnp.where(row8 == 1, pltpu.roll(low, 1, 0), high).astype(F32).astype(BF16)
    until = lax.broadcasted_iota(jnp.int32, (wide, wide), 0)
    upto = lax.broadcasted_iota(jnp.int32, (wide, wide), 1)
    lower = jnp.where(upto <= until, 1.0, 0.0).astype(BF16)
    sums = dot(lower, both, NT)
    base = chip * (GROUP * SPAN)
    ends = sums[:, 0:1] * 256.0 + sums[:, 1:2] - base.astype(F32)
    least = -base.astype(F32)
    key_row = lax.broadcasted_iota(jnp.int32, (SPAN, SPAN), 0).astype(F32)
    query_col = lax.broadcasted_iota(jnp.int32, (SPAN, SPAN), 1).astype(F32)
    for j in range(GROUP):
        pos = query_col[0:1] + float(j * SPAN)
        start = jnp.max(jnp.where(ends <= pos, ends, least), axis=0, keepdims=True)
        for b in range(GROUP + 1):
            key = b if b <= j else b - 1 - GROUP
            ok = key_row + float(key * SPAN) >= start
            if b == j:
                ok = ok & (key_row <= query_col)
            bias[j, b * SPAN : (b + 1) * SPAN] = jnp.where(ok, 0.0, -1e30)

    local[3].wait()
    back = jnp.maximum(chip - 1, 0)
    here = [assign_s[s % 2, 2 * chip + s // 2] & (GROUP - 1) for s in range(GROUP)]
    there = [assign_s[s % 2, 2 * back + s // 2] & (GROUP - 1) for s in range(GROUP)]
    for copy in (local[0], local[1], local[4], local[5]):
        copy.wait()
    for copy in near:
        copy.wait_recv()
    for j in range(GROUP):
        slot = pick(here, j)
        rows = slice(j * SPAN, (j + 1) * SPAN)
        kb = kown[slot]
        vb = vown[slot]
        ko[rows] = kb
        vo[rows] = vb
        kot[:, rows] = kb.T
        vot[:, rows] = vb.T
        qb = qslot[slot]
        gb = gslot[slot]
        for h in range(heads):
            qr[j, h * SPAN : (h + 1) * SPAN] = qb[:, h * DIM : (h + 1) * DIM]
            gr[j, h * SPAN : (h + 1) * SPAN] = gb[:, h * DIM : (h + 1) * DIM]

    scale = ROOT * math.log2(math.e)
    part_p[...] = jnp.zeros_like(part_p)
    part_o[...] = jnp.zeros_like(part_o)

    def masked(keys, j, rows):
        return dot(keys, qr[j], NT) * scale + every_head(bias[j, rows], heads)

    tops = []
    for j in range(GROUP):
        own = slice(0, (j + 1) * SPAN)
        s = masked(ko[own], j, own)
        expo[j, own] = s
        tops.append(jnp.max(s, axis=0, keepdims=True))
    for j in range(GROUP):
        own = slice(0, (j + 1) * SPAN)
        dpo[j, own] = dot(vo[own], gr[j], NT)
    for j in range(GROUP):
        own = slice(0, (j + 1) * SPAN)
        e = jnp.exp2(expo[j, own] - tops[j])
        expo[j, own] = e
        stat[j, 0:1] = tops[j]
        stat[j, 1:2] = jnp.sum(e, axis=0, keepdims=True)
        stat[j, 2:3] = jnp.sum(e * dpo[j, own], axis=0, keepdims=True)
        oto[j] = dot(vot[:, own], e.astype(BF16), NN)

    @pl.when(has_prev)
    def _():
        for a in range(2):
            far_k[a].wait_recv()
            relay_k[a].start()
        for a in range(2):
            relay_k[a].wait_recv()

    @pl.when(jnp.logical_not(has_prev))
    def _():
        kprev[...] = jnp.zeros_like(kprev)
        vprev[...] = jnp.zeros_like(vprev)

    for i in range(GROUP):
        rows = slice(i * SPAN, (i + 1) * SPAN)
        kb = kprev[pick(there, i)]
        kp[rows] = kb
        kpt[:, rows] = kb.T

    tops = []
    for j in range(GROUP):
        at = (j + 1) * SPAN
        s = masked(kp[j * SPAN :], j, slice(at, None))
        expo[j, at:] = s
        tops.append(jnp.maximum(stat[j, 0:1], jnp.max(s, axis=0, keepdims=True)))
    norms = []
    alphas = []
    for j in range(GROUP):
        at = (j + 1) * SPAN
        e = jnp.exp2(expo[j, at:] - tops[j])
        expo[j, at:] = e
        shrink = jnp.exp2(stat[j, 0:1] - tops[j])
        r = 1.0 / (stat[j, 1:2] * shrink + jnp.sum(e, axis=0, keepdims=True))
        norms.append(r)
        alphas.append(shrink * r)

    @pl.when(has_prev)
    def _():
        for a in range(2):
            far_v[a].wait_recv()
            relay_v[a].start()
        for a in range(2):
            relay_v[a].wait_recv()

    for i in range(GROUP):
        rows = slice(i * SPAN, (i + 1) * SPAN)
        vb = vprev[pick(there, i)]
        vp[rows] = vb
        vpt[:, rows] = vb.T

    for j in range(GROUP):
        dpo[j, (j + 1) * SPAN :] = dot(vp[j * SPAN :], gr[j], NT)
    deltas = []
    for j in range(GROUP):
        at = (j + 1) * SPAN
        pr = expo[j, at:] * norms[j]
        dp = dpo[j, at:]
        delta = alphas[j] * stat[j, 2:3] + jnp.sum(pr * dp, axis=0, keepdims=True)
        deltas.append(delta)
        pb[j, at:] = pr.astype(BF16)
        sb[j, at:] = (pr * (dp - delta)).astype(BF16)
    for j in range(GROUP):
        at = (j + 1) * SPAN
        part_p[j:, :, 0:DIM] += spans(dot(sb[j, at:], qr[j], NN) * ROOT)
        part_p[j:, :, DIM:] += spans(dot(pb[j, at:], gr[j], NN))

    def mine_of(spans, a):
        return jnp.where(core == 0, spans[a], spans[2 + a])

    def theirs_of(spans, a):
        return jnp.where(core == 0, spans[2 + a], spans[a])

    swap_p = [remote(sum_send.at[a], sum_near.at[a], p_s.at[a], p_r.at[a], beside)
              for a in range(2)]
    far_p = [remote(far_send_buf.at[a], far_buf.at[a], f_s.at[a], f_r.at[a], before)
             for a in range(2)]
    for a in range(2):
        sum_send[a] = part_p[theirs_of(there, a)].astype(BF16)
        swap_p[a].start()

    swap_oq = [remote(oq_mine.at[j], oq_near.at[j], oq_s.at[j], oq_r.at[j], beside)
               for j in range(GROUP)]

    def own_grads(j):
        own = slice(0, (j + 1) * SPAN)
        at = (j + 1) * SPAN
        pr = expo[j, own] * alphas[j]
        ds = (pr * (dpo[j, own] - deltas[j])).astype(BF16)
        low = pr.astype(BF16)
        part_o[0 : j + 1, :, 0:DIM] += spans(dot(ds, qr[j], NN) * ROOT)
        part_o[0 : j + 1, :, DIM:] += spans(dot(low, gr[j], NN))
        out = oto[j] * alphas[j] + dot(vpt[:, j * SPAN :], pb[j, at:], NN)
        dqt = dot(kot[:, own], ds, NN) + dot(kpt[:, j * SPAN :], sb[j, at:], NN)
        out = out.astype(BF16)
        dqt = (dqt * ROOT).astype(BF16)
        for h in range(heads):
            cols = slice(h * DIM, (h + 1) * DIM)
            oq_mine[j, 0, :, cols] = out[:, cols].T
            oq_mine[j, 1, :, cols] = dqt[:, cols].T
        swap_oq[j].start()

    own_grads(0)
    own_grads(1)

    for a in range(2):
        swap_p[a].wait_recv()
        far_send_buf[a] = (
            part_p[mine_of(there, a)] + sum_near[a].astype(F32)).astype(BF16)

        @pl.when(has_prev)
        def _(a=a):
            far_p[a].start()

    own_grads(2)
    own_grads(3)

    swap_o = [remote(own_send.at[a], own_near.at[a], o_s.at[a], o_r.at[a], beside)
              for a in range(2)]
    for a in range(2):
        own_send[a] = part_o[theirs_of(here, a)].astype(BF16)
        swap_o[a].start()

    for j in range(GROUP):
        swap_oq[j].wait_recv()
    for a in range(2):
        j = mine_of(here, a)
        for half, source in ((core, oq_mine), (other, oq_near)):
            attn[a, :, columns(half)] = source[j, 0]
            dq[a, :, columns(half)] = source[j, 1]

    @pl.when(jnp.logical_not(has_next))
    def _():
        far_buf[...] = jnp.zeros_like(far_buf)

    for a in range(2):
        swap_o[a].wait_recv()

        @pl.when(has_next)
        def _(a=a):
            far_p[a].wait_recv()

        total = part_o[mine_of(here, a)] + own_near[a].astype(F32) + far_buf[a].astype(F32)
        dk[a] = total[:, 0:DIM].astype(BF16)
        dv[a] = total[:, DIM:].astype(BF16)

    for copy in near + swap_p + swap_oq + swap_o:
        copy.wait_send()

    @pl.when(has_next)
    def _():
        for copy in far_k + far_v:
            copy.wait_send()

    @pl.when(has_prev)
    def _():
        for copy in relay_k + relay_v + far_p:
            copy.wait_send()


def store_kernel(*refs):
    n = (len(refs) - 1) // 2
    copies = [
        pltpu.make_async_copy(refs[i], refs[n + i], refs[2 * n].at[i]) for i in range(n)
    ]
    for copy in copies:
        copy.start()
    for copy in copies:
        copy.wait()


def shards(count, queries, keys, values, grad_out, lengths, assign):
    width = queries.shape[1]
    half = width // 2
    docs = lengths.shape[0]
    wide = -(-docs // 128) * 128
    hbm = pl.BlockSpec(memory_space=pltpu.HBM)
    vmem = pl.BlockSpec(memory_space=pltpu.VMEM)
    dma = pltpu.SemaphoreType.DMA
    shape = jax.ShapeDtypeStruct
    keyed = GROUP * SPAN
    seen = keyed + SPAN
    outs = (
        shape((2, SPAN, width), BF16),
        shape((2, SPAN, width), BF16),
        shape((2, SPAN, DIM), BF16),
        shape((2, SPAN, DIM), BF16),
    )
    results = pl.pallas_call(
        functools.partial(main_kernel, count),
        out_shape=outs,
        in_specs=[hbm] * 6,
        out_specs=(vmem,) * 4,
        scratch_shapes=[
            pltpu.VMEM((docs,), jnp.int32),
            pltpu.SMEM(assign.shape[::-1], jnp.int32),
            pltpu.VMEM((8, wide), jnp.int32),
            pltpu.VMEM((GROUP, SPAN, half), BF16),
            pltpu.VMEM((GROUP, SPAN, half), BF16),
            pltpu.VMEM((GROUP, SPAN, DIM), BF16),
            pltpu.VMEM((GROUP, SPAN, DIM), BF16),
            pltpu.VMEM((GROUP, SPAN, DIM), BF16),
            pltpu.VMEM((GROUP, SPAN, DIM), BF16),
            pltpu.VMEM((GROUP, half, DIM), BF16),
            pltpu.VMEM((GROUP, half, DIM), BF16),
            pltpu.VMEM((keyed, DIM), BF16),
            pltpu.VMEM((keyed, DIM), BF16),
            pltpu.VMEM((DIM, keyed), BF16),
            pltpu.VMEM((DIM, keyed), BF16),
            pltpu.VMEM((keyed, DIM), BF16),
            pltpu.VMEM((keyed, DIM), BF16),
            pltpu.VMEM((DIM, keyed), BF16),
            pltpu.VMEM((DIM, keyed), BF16),
            pltpu.VMEM((GROUP, seen, SPAN), F32),
            pltpu.VMEM((GROUP, seen, half), F32),
            pltpu.VMEM((GROUP, seen, half), F32),
            pltpu.VMEM((GROUP, seen, half), BF16),
            pltpu.VMEM((GROUP, seen, half), BF16),
            pltpu.VMEM((GROUP, DIM, half), F32),
            pltpu.VMEM((GROUP, 8, half), F32),
            pltpu.VMEM((GROUP, SPAN, 2 * DIM), F32),
            pltpu.VMEM((GROUP, SPAN, 2 * DIM), F32),
            pltpu.VMEM((2, SPAN, 2 * DIM), BF16),
            pltpu.VMEM((2, SPAN, 2 * DIM), BF16),
            pltpu.VMEM((2, SPAN, 2 * DIM), BF16),
            pltpu.VMEM((2, SPAN, 2 * DIM), BF16),
            pltpu.VMEM((2, SPAN, 2 * DIM), BF16),
            pltpu.VMEM((2, SPAN, 2 * DIM), BF16),
            pltpu.VMEM((GROUP, 2, SPAN, half), BF16),
            pltpu.VMEM((GROUP, 2, SPAN, half), BF16),
            dma((6,)),
            dma((2,)), dma((2,)), dma((2,)), dma((2,)),
            dma((2,)), dma((2,)), dma((2,)), dma((2,)),
            dma((4,)), dma((4,)),
            dma((2,)), dma((2,)), dma((2,)), dma((2,)), dma((2,)), dma((2,)),
            dma((GROUP,)), dma((GROUP,)),
        ],
        compiler_params=pltpu.CompilerParams(
            collective_id=0, has_side_effects=True, vmem_limit_bytes=40 * 2**20),
        name="attend",
    )(*[
        pltpu.with_memory_space_constraint(x, pltpu.HBM)
        for x in (
            queries.reshape(2, SPAN, width), grad_out.reshape(2, SPAN, width),
            keys.reshape(2, SPAN, DIM), values.reshape(2, SPAN, DIM), lengths, assign.T,
        )
    ])
    results = pl.pallas_call(
        store_kernel,
        out_shape=outs,
        in_specs=[pl.BlockSpec(memory_space=pltpu.VMEM)] * 4,
        out_specs=(hbm,) * 4,
        scratch_shapes=[dma((4,))],
        name="store",
    )(*[pltpu.with_memory_space_constraint(r, pltpu.VMEM) for r in results])
    return tuple(r.reshape(2 * SPAN, r.shape[2]) for r in results)


def solution(mesh):
    split = P("seq", "grp")
    return jax.shard_map(
        functools.partial(shards, mesh.shape["seq"]),
        mesh=mesh,
        in_specs=(split, split, split, split, P(), P()),
        out_specs=(split, split, split, split),
        check_vma=False,
    )
```

```python
import functools
import math

import jax
import jax.numpy as jnp
from jax import lax
from jax.experimental import pallas as pl
from jax.experimental.pallas import tpu as pltpu
from jax.sharding import PartitionSpec as P

MESH = pl.DeviceIdType.MESH
SPAN = 128
DIM = 128
GROUP = 4
F32 = jnp.float32
BF16 = jnp.bfloat16
NT = (((1,), (1,)), ((), ()))
NN = (((1,), (0,)), ((), ()))
ROOT = 1.0 / math.sqrt(DIM)


def dot(a, b, dims):
    return lax.dot_general(a, b, dims, preferred_element_type=F32)


def pick(values, wanted):
    index = jnp.int32(0)
    for i, value in enumerate(values):
        index = jnp.where(value == wanted, i, index)
    return index


def every_head(x, heads):
    return jnp.concatenate([x] * heads, axis=1)


def spans(x):
    return x.reshape(x.shape[0] // SPAN, SPAN, x.shape[1])


def main_kernel(
    count, q, g, k, v, lens, assign, attn, dq, dk, dv,
    lens_v, assign_s, padded, qslot, gslot, kown, vown, kprev, vprev, qr, gr,
    ko, vo, kot, vot, kp, vp, kpt, vpt, bias, expo, dpo, pb, sb, oto, stat,
    part_p, part_o, sum_send, sum_near, far_send_buf, far_buf, own_send, own_near,
    oq_mine, oq_near,
    loc_sem, far_ks, far_kr, far_vs, far_vr, rel_ks, rel_kr, rel_vs, rel_vr,
    near_s, near_r, p_s, p_r, f_s, f_r, o_s, o_r, oq_s, oq_r,
):
    me = lax.axis_index("seq")
    grp = lax.axis_index("grp")
    core = lax.rem(me, 2)
    other = 1 - core
    chip = me // 2
    beside = me + 1 - 2 * core
    has_prev = chip > 0
    has_next = chip < count // 2 - 1
    before = jnp.where(has_prev, me - 2, me)
    after = jnp.where(has_next, me + 2, me)
    width = q.shape[2] // 2
    heads = width // DIM

    def remote(src, dst, send, recv, device):
        return pltpu.make_async_remote_copy(
            src_ref=src, dst_ref=dst, send_sem=send, recv_sem=recv,
            device_id=(device, grp), device_id_type=MESH,
        )

    def columns(which):
        return pl.ds(pl.multiple_of(which * width, width), width)

    own_slots = pl.ds(2 * core, 2)
    local = [
        pltpu.make_async_copy(k, kown.at[own_slots], loc_sem.at[0]),
        pltpu.make_async_copy(v, vown.at[own_slots], loc_sem.at[1]),
        pltpu.make_async_copy(lens, lens_v, loc_sem.at[2]),
        pltpu.make_async_copy(assign, assign_s, loc_sem.at[3]),
        pltpu.make_async_copy(q.at[:, :, columns(core)], qslot.at[own_slots], loc_sem.at[4]),
        pltpu.make_async_copy(g.at[:, :, columns(core)], gslot.at[own_slots], loc_sem.at[5]),
    ]
    far_k = [remote(k.at[a], kprev.at[2 * core + a], far_ks.at[a], far_kr.at[a], after)
             for a in range(2)]
    far_v = [remote(v.at[a], vprev.at[2 * core + a], far_vs.at[a], far_vr.at[a], after)
             for a in range(2)]
    relay_k = [remote(kprev.at[2 * core + a], kprev.at[2 * core + a], rel_ks.at[a], rel_kr.at[a],
                      beside) for a in range(2)]
    relay_v = [remote(vprev.at[2 * core + a], vprev.at[2 * core + a], rel_vs.at[a], rel_vr.at[a],
                      beside) for a in range(2)]
    near = [
        remote(k, kown.at[own_slots], near_s.at[0], near_r.at[0], beside),
        remote(v, vown.at[own_slots], near_s.at[1], near_r.at[1], beside),
        remote(q.at[:, :, columns(other)], qslot.at[own_slots], near_s.at[2], near_r.at[2], beside),
        remote(g.at[:, :, columns(other)], gslot.at[own_slots], near_s.at[3], near_r.at[3], beside),
    ]

    barrier = pltpu.get_barrier_semaphore()
    pl.semaphore_signal(barrier, inc=1, device_id=(beside, grp), device_id_type=MESH)

    @pl.when(has_prev)
    def _():
        pl.semaphore_signal(barrier, inc=1, device_id=(before, grp), device_id_type=MESH)

    @pl.when(has_next)
    def _():
        pl.semaphore_signal(barrier, inc=1, device_id=(after, grp), device_id_type=MESH)

    for copy in local:
        copy.start()
    pl.semaphore_wait(
        barrier, 1 + has_prev.astype(jnp.int32) + has_next.astype(jnp.int32))

    @pl.when(has_next)
    def _():
        for copy in far_k + far_v:
            copy.start()

    for copy in near[:2]:
        copy.start()

    docs = lens_v.shape[0]
    wide = padded.shape[1]
    padded[...] = jnp.zeros_like(padded)
    local[2].wait()
    padded[0:1, 0:docs] = lens_v[...].reshape(1, docs)
    length = padded[...]
    high = length >> 8
    low = length - (high << 8)
    row8 = lax.broadcasted_iota(jnp.int32, (8, wide), 0)
    both = jnp.where(row8 == 1, pltpu.roll(low, 1, 0), high).astype(F32).astype(BF16)
    until = lax.broadcasted_iota(jnp.int32, (wide, wide), 0)
    upto = lax.broadcasted_iota(jnp.int32, (wide, wide), 1)
    lower = jnp.where(upto <= until, 1.0, 0.0).astype(BF16)
    sums = dot(lower, both, NT)
    base = chip * (GROUP * SPAN)
    ends = sums[:, 0:1] * 256.0 + sums[:, 1:2] - base.astype(F32)
    least = -base.astype(F32)
    key_row = lax.broadcasted_iota(jnp.int32, (SPAN, SPAN), 0).astype(F32)
    query_col = lax.broadcasted_iota(jnp.int32, (SPAN, SPAN), 1).astype(F32)
    for j in range(GROUP):
        pos = query_col[0:1] + float(j * SPAN)
        start = jnp.max(jnp.where(ends <= pos, ends, least), axis=0, keepdims=True)
        for b in range(GROUP + 1):
            key = b if b <= j else b - 1 - GROUP
            ok = key_row + float(key * SPAN) >= start
            if b == j:
                ok = ok & (key_row <= query_col)
            bias[j, b * SPAN : (b + 1) * SPAN] = jnp.where(ok, 0.0, -1e30)

    @pl.when(has_next)
    def _():
        for copy in far_k + far_v:
            copy.wait_send()

    for copy in near[2:]:
        copy.start()

    local[3].wait()
    back = jnp.maximum(chip - 1, 0)
    here = [assign_s[s % 2, 2 * chip + s // 2] & (GROUP - 1) for s in range(GROUP)]
    there = [assign_s[s % 2, 2 * back + s // 2] & (GROUP - 1) for s in range(GROUP)]
    for copy in (local[0], local[1], local[4], local[5]):
        copy.wait()
    for copy in near:
        copy.wait_recv()
    for j in range(GROUP):
        slot = pick(here, j)
        rows = slice(j * SPAN, (j + 1) * SPAN)
        kb = kown[slot]
        vb = vown[slot]
        ko[rows] = kb
        vo[rows] = vb
        kot[:, rows] = kb.T
        vot[:, rows] = vb.T
        qb = qslot[slot]
        gb = gslot[slot]
        for h in range(heads):
            qr[j, h * SPAN : (h + 1) * SPAN] = qb[:, h * DIM : (h + 1) * DIM]
            gr[j, h * SPAN : (h + 1) * SPAN] = gb[:, h * DIM : (h + 1) * DIM]

    scale = ROOT * math.log2(math.e)
    part_p[...] = jnp.zeros_like(part_p)
    part_o[...] = jnp.zeros_like(part_o)

    def masked(keys, j, rows):
        return dot(keys, qr[j], NT) * scale + every_head(bias[j, rows], heads)

    tops = []
    for j in range(GROUP):
        own = slice(0, (j + 1) * SPAN)
        s = masked(ko[own], j, own)
        expo[j, own] = s
        tops.append(jnp.max(s, axis=0, keepdims=True))
    for j in range(GROUP):
        own = slice(0, (j + 1) * SPAN)
        dpo[j, own] = dot(vo[own], gr[j], NT)
    for j in range(GROUP):
        own = slice(0, (j + 1) * SPAN)
        e = jnp.exp2(expo[j, own] - tops[j])
        expo[j, own] = e
        stat[j, 0:1] = tops[j]
        stat[j, 1:2] = jnp.sum(e, axis=0, keepdims=True)
        stat[j, 2:3] = jnp.sum(e * dpo[j, own], axis=0, keepdims=True)
        oto[j] = dot(vot[:, own], e.astype(BF16), NN)

    @pl.when(has_prev)
    def _():
        for a in range(2):
            far_k[a].wait_recv()
            relay_k[a].start()
        for a in range(2):
            relay_k[a].wait_recv()

    @pl.when(jnp.logical_not(has_prev))
    def _():
        kprev[...] = jnp.zeros_like(kprev)
        vprev[...] = jnp.zeros_like(vprev)

    for i in range(GROUP):
        rows = slice(i * SPAN, (i + 1) * SPAN)
        kb = kprev[pick(there, i)]
        kp[rows] = kb
        kpt[:, rows] = kb.T

    tops = []
    for j in range(GROUP):
        at = (j + 1) * SPAN
        s = masked(kp[j * SPAN :], j, slice(at, None))
        expo[j, at:] = s
        tops.append(jnp.maximum(stat[j, 0:1], jnp.max(s, axis=0, keepdims=True)))

    @pl.when(has_prev)
    def _():
        for a in range(2):
            far_v[a].wait_recv()
            relay_v[a].start()

    norms = []
    alphas = []
    for j in range(GROUP):
        at = (j + 1) * SPAN
        e = jnp.exp2(expo[j, at:] - tops[j])
        expo[j, at:] = e
        shrink = jnp.exp2(stat[j, 0:1] - tops[j])
        r = 1.0 / (stat[j, 1:2] * shrink + jnp.sum(e, axis=0, keepdims=True))
        norms.append(r)
        alphas.append(shrink * r)

    @pl.when(has_prev)
    def _():
        for a in range(2):
            relay_v[a].wait_recv()

    for i in range(GROUP):
        rows = slice(i * SPAN, (i + 1) * SPAN)
        vb = vprev[pick(there, i)]
        vp[rows] = vb
        vpt[:, rows] = vb.T

    for j in range(GROUP):
        dpo[j, (j + 1) * SPAN :] = dot(vp[j * SPAN :], gr[j], NT)
    deltas = []
    for j in range(GROUP):
        at = (j + 1) * SPAN
        pr = expo[j, at:] * norms[j]
        dp = dpo[j, at:]
        delta = alphas[j] * stat[j, 2:3] + jnp.sum(pr * dp, axis=0, keepdims=True)
        deltas.append(delta)
        pb[j, at:] = pr.astype(BF16)
        sb[j, at:] = (pr * (dp - delta)).astype(BF16)
    for j in range(GROUP):
        at = (j + 1) * SPAN
        part_p[j:, :, 0:DIM] += spans(dot(sb[j, at:], qr[j], NN) * ROOT)
        part_p[j:, :, DIM:] += spans(dot(pb[j, at:], gr[j], NN))

    def mine_of(spans, a):
        return jnp.where(core == 0, spans[a], spans[2 + a])

    def theirs_of(spans, a):
        return jnp.where(core == 0, spans[2 + a], spans[a])

    swap_p = [remote(sum_send.at[a], sum_near.at[a], p_s.at[a], p_r.at[a], beside)
              for a in range(2)]
    far_p = [remote(far_send_buf.at[a], far_buf.at[a], f_s.at[a], f_r.at[a], before)
             for a in range(2)]
    for a in range(2):
        sum_send[a] = part_p[theirs_of(there, a)].astype(BF16)
        swap_p[a].start()

    swap_oq = [remote(oq_mine.at[j], oq_near.at[j], oq_s.at[j], oq_r.at[j], beside)
               for j in range(GROUP)]

    def own_grads(j):
        own = slice(0, (j + 1) * SPAN)
        at = (j + 1) * SPAN
        pr = expo[j, own] * alphas[j]
        ds = (pr * (dpo[j, own] - deltas[j])).astype(BF16)
        low = pr.astype(BF16)
        part_o[0 : j + 1, :, 0:DIM] += spans(dot(ds, qr[j], NN) * ROOT)
        part_o[0 : j + 1, :, DIM:] += spans(dot(low, gr[j], NN))
        out = oto[j] * alphas[j] + dot(vpt[:, j * SPAN :], pb[j, at:], NN)
        dqt = dot(kot[:, own], ds, NN) + dot(kpt[:, j * SPAN :], sb[j, at:], NN)
        out = out.astype(BF16)
        dqt = (dqt * ROOT).astype(BF16)
        for h in range(heads):
            cols = slice(h * DIM, (h + 1) * DIM)
            oq_mine[j, 0, :, cols] = out[:, cols].T
            oq_mine[j, 1, :, cols] = dqt[:, cols].T

    own_grads(0)

    for a in range(2):
        swap_p[a].wait_recv()
        far_send_buf[a] = (
            part_p[mine_of(there, a)] + sum_near[a].astype(F32)).astype(BF16)

        @pl.when(has_prev)
        def _(a=a):
            far_p[a].start()

    swap_oq[0].start()
    for j in range(1, GROUP):
        own_grads(j)
        swap_oq[j].start()

    swap_o = [remote(own_send.at[a], own_near.at[a], o_s.at[a], o_r.at[a], beside)
              for a in range(2)]
    for a in range(2):
        own_send[a] = part_o[theirs_of(here, a)].astype(BF16)
        swap_o[a].start()

    for j in range(GROUP):
        swap_oq[j].wait_recv()
    for a in range(2):
        j = mine_of(here, a)
        for half, source in ((core, oq_mine), (other, oq_near)):
            attn[a, :, columns(half)] = source[j, 0]
            dq[a, :, columns(half)] = source[j, 1]

    @pl.when(jnp.logical_not(has_next))
    def _():
        far_buf[...] = jnp.zeros_like(far_buf)

    for a in range(2):
        swap_o[a].wait_recv()

        @pl.when(has_next)
        def _(a=a):
            far_p[a].wait_recv()

        total = part_o[mine_of(here, a)] + own_near[a].astype(F32) + far_buf[a].astype(F32)
        dk[a] = total[:, 0:DIM].astype(BF16)
        dv[a] = total[:, DIM:].astype(BF16)

    for copy in near + swap_p + swap_oq + swap_o:
        copy.wait_send()

    @pl.when(has_prev)
    def _():
        for copy in relay_k + relay_v + far_p:
            copy.wait_send()


def store_kernel(*refs):
    n = (len(refs) - 1) // 2
    copies = [
        pltpu.make_async_copy(refs[i], refs[n + i], refs[2 * n].at[i]) for i in range(n)
    ]
    for copy in copies:
        copy.start()
    for copy in copies:
        copy.wait()


def shards(count, queries, keys, values, grad_out, lengths, assign):
    width = queries.shape[1]
    half = width // 2
    docs = lengths.shape[0]
    wide = -(-docs // 128) * 128
    hbm = pl.BlockSpec(memory_space=pltpu.HBM)
    vmem = pl.BlockSpec(memory_space=pltpu.VMEM)
    dma = pltpu.SemaphoreType.DMA
    shape = jax.ShapeDtypeStruct
    keyed = GROUP * SPAN
    seen = keyed + SPAN
    outs = (
        shape((2, SPAN, width), BF16),
        shape((2, SPAN, width), BF16),
        shape((2, SPAN, DIM), BF16),
        shape((2, SPAN, DIM), BF16),
    )
    results = pl.pallas_call(
        functools.partial(main_kernel, count),
        out_shape=outs,
        in_specs=[hbm] * 6,
        out_specs=(vmem,) * 4,
        scratch_shapes=[
            pltpu.VMEM((docs,), jnp.int32),
            pltpu.SMEM(assign.shape[::-1], jnp.int32),
            pltpu.VMEM((8, wide), jnp.int32),
            pltpu.VMEM((GROUP, SPAN, half), BF16),
            pltpu.VMEM((GROUP, SPAN, half), BF16),
            pltpu.VMEM((GROUP, SPAN, DIM), BF16),
            pltpu.VMEM((GROUP, SPAN, DIM), BF16),
            pltpu.VMEM((GROUP, SPAN, DIM), BF16),
            pltpu.VMEM((GROUP, SPAN, DIM), BF16),
            pltpu.VMEM((GROUP, half, DIM), BF16),
            pltpu.VMEM((GROUP, half, DIM), BF16),
            pltpu.VMEM((keyed, DIM), BF16),
            pltpu.VMEM((keyed, DIM), BF16),
            pltpu.VMEM((DIM, keyed), BF16),
            pltpu.VMEM((DIM, keyed), BF16),
            pltpu.VMEM((keyed, DIM), BF16),
            pltpu.VMEM((keyed, DIM), BF16),
            pltpu.VMEM((DIM, keyed), BF16),
            pltpu.VMEM((DIM, keyed), BF16),
            pltpu.VMEM((GROUP, seen, SPAN), F32),
            pltpu.VMEM((GROUP, seen, half), F32),
            pltpu.VMEM((GROUP, seen, half), F32),
            pltpu.VMEM((GROUP, seen, half), BF16),
            pltpu.VMEM((GROUP, seen, half), BF16),
            pltpu.VMEM((GROUP, DIM, half), F32),
            pltpu.VMEM((GROUP, 8, half), F32),
            pltpu.VMEM((GROUP, SPAN, 2 * DIM), F32),
            pltpu.VMEM((GROUP, SPAN, 2 * DIM), F32),
            pltpu.VMEM((2, SPAN, 2 * DIM), BF16),
            pltpu.VMEM((2, SPAN, 2 * DIM), BF16),
            pltpu.VMEM((2, SPAN, 2 * DIM), BF16),
            pltpu.VMEM((2, SPAN, 2 * DIM), BF16),
            pltpu.VMEM((2, SPAN, 2 * DIM), BF16),
            pltpu.VMEM((2, SPAN, 2 * DIM), BF16),
            pltpu.VMEM((GROUP, 2, SPAN, half), BF16),
            pltpu.VMEM((GROUP, 2, SPAN, half), BF16),
            dma((6,)),
            dma((2,)), dma((2,)), dma((2,)), dma((2,)),
            dma((2,)), dma((2,)), dma((2,)), dma((2,)),
            dma((4,)), dma((4,)),
            dma((2,)), dma((2,)), dma((2,)), dma((2,)), dma((2,)), dma((2,)),
            dma((GROUP,)), dma((GROUP,)),
        ],
        compiler_params=pltpu.CompilerParams(
            collective_id=0, has_side_effects=True, vmem_limit_bytes=40 * 2**20),
        name="attend",
    )(*[
        pltpu.with_memory_space_constraint(x, pltpu.HBM)
        for x in (
            queries.reshape(2, SPAN, width), grad_out.reshape(2, SPAN, width),
            keys.reshape(2, SPAN, DIM), values.reshape(2, SPAN, DIM), lengths, assign.T,
        )
    ])
    results = pl.pallas_call(
        store_kernel,
        out_shape=outs,
        in_specs=[pl.BlockSpec(memory_space=pltpu.VMEM)] * 4,
        out_specs=(hbm,) * 4,
        scratch_shapes=[dma((4,))],
        name="store",
    )(*[pltpu.with_memory_space_constraint(r, pltpu.VMEM) for r in results])
    return tuple(r.reshape(2 * SPAN, r.shape[2]) for r in results)


def solution(mesh):
    split = P("seq", "grp")
    return jax.shard_map(
        functools.partial(shards, mesh.shape["seq"]),
        mesh=mesh,
        in_specs=(split, split, split, split, P(), P()),
        out_specs=(split, split, split, split),
        check_vma=False,
    )
```

```python
import functools
import math

import jax
import jax.numpy as jnp
from jax import lax
from jax.experimental import pallas as pl
from jax.experimental.pallas import tpu as pltpu
from jax.sharding import PartitionSpec as P

MESH = pl.DeviceIdType.MESH
SPAN = 128
DIM = 128
GROUP = 4
F32 = jnp.float32
BF16 = jnp.bfloat16
NT = (((1,), (1,)), ((), ()))
NN = (((1,), (0,)), ((), ()))
ROOT = 1.0 / math.sqrt(DIM)


def dot(a, b, dims):
    return lax.dot_general(a, b, dims, preferred_element_type=F32)


def pick(values, wanted):
    index = jnp.int32(0)
    for i, value in enumerate(values):
        index = jnp.where(value == wanted, i, index)
    return index


def every_head(x, heads):
    return jnp.concatenate([x] * heads, axis=1)


def spans(x):
    return x.reshape(x.shape[0] // SPAN, SPAN, x.shape[1])


def main_kernel(
    count, q, g, k, v, lens, assign, attn, dq, dk, dv,
    lens_v, assign_s, padded, qslot, gslot, kown, vown, kprev, vprev, qr, gr, qt, gt,
    ko, vo, kot, vot, kp, vp, kpt, vpt, bias, expo, dpo, pb, sb, oto, stat,
    part_p, part_o, sum_send, sum_near, far_send_buf, far_buf, own_send, own_near,
    o_mine, o_near, q_mine, q_near,
    loc_sem, far_ks, far_kr, far_vs, far_vr, rel_ks, rel_kr, rel_vs, rel_vr,
    near_s, near_r, p_s, p_r, f_s, f_r, o_s, o_r, oq_s, oq_r,
):
    me = lax.axis_index("seq")
    grp = lax.axis_index("grp")
    core = lax.rem(me, 2)
    other = 1 - core
    chip = me // 2
    beside = me + 1 - 2 * core
    has_prev = chip > 0
    has_next = chip < count // 2 - 1
    before = jnp.where(has_prev, me - 2, me)
    after = jnp.where(has_next, me + 2, me)
    width = q.shape[2] // 2
    heads = width // DIM

    def remote(src, dst, send, recv, device):
        return pltpu.make_async_remote_copy(
            src_ref=src, dst_ref=dst, send_sem=send, recv_sem=recv,
            device_id=(device, grp), device_id_type=MESH,
        )

    def columns(which):
        return pl.ds(pl.multiple_of(which * width, width), width)

    own_slots = pl.ds(2 * core, 2)
    local = [
        pltpu.make_async_copy(k, kown.at[own_slots], loc_sem.at[0]),
        pltpu.make_async_copy(v, vown.at[own_slots], loc_sem.at[1]),
        pltpu.make_async_copy(lens, lens_v, loc_sem.at[2]),
        pltpu.make_async_copy(assign, assign_s, loc_sem.at[3]),
        pltpu.make_async_copy(q.at[:, :, columns(core)], qslot.at[own_slots], loc_sem.at[4]),
        pltpu.make_async_copy(g.at[:, :, columns(core)], gslot.at[own_slots], loc_sem.at[5]),
    ]
    far_k = [remote(k.at[a], kprev.at[2 * core + a], far_ks.at[a], far_kr.at[a], after)
             for a in range(2)]
    far_v = [remote(v.at[a], vprev.at[2 * core + a], far_vs.at[a], far_vr.at[a], after)
             for a in range(2)]
    relay_k = [remote(kprev.at[2 * core + a], kprev.at[2 * core + a], rel_ks.at[a], rel_kr.at[a],
                      beside) for a in range(2)]
    relay_v = [remote(vprev.at[2 * core + a], vprev.at[2 * core + a], rel_vs.at[a], rel_vr.at[a],
                      beside) for a in range(2)]
    near = [
        remote(k, kown.at[own_slots], near_s.at[0], near_r.at[0], beside),
        remote(v, vown.at[own_slots], near_s.at[1], near_r.at[1], beside),
        remote(q.at[:, :, columns(other)], qslot.at[own_slots], near_s.at[2], near_r.at[2], beside),
        remote(g.at[:, :, columns(other)], gslot.at[own_slots], near_s.at[3], near_r.at[3], beside),
    ]

    barrier = pltpu.get_barrier_semaphore()
    pl.semaphore_signal(barrier, inc=1, device_id=(beside, grp), device_id_type=MESH)

    @pl.when(has_prev)
    def _():
        pl.semaphore_signal(barrier, inc=1, device_id=(before, grp), device_id_type=MESH)

    @pl.when(has_next)
    def _():
        pl.semaphore_signal(barrier, inc=1, device_id=(after, grp), device_id_type=MESH)

    for copy in local:
        copy.start()
    pl.semaphore_wait(
        barrier, 1 + has_prev.astype(jnp.int32) + has_next.astype(jnp.int32))

    @pl.when(has_next)
    def _():
        for copy in far_k:
            copy.start()

    for copy in near:
        copy.start()

    docs = lens_v.shape[0]
    wide = padded.shape[1]
    padded[...] = jnp.zeros_like(padded)
    local[2].wait()
    padded[0:1, 0:docs] = lens_v[...].reshape(1, docs)
    length = padded[...]
    high = length >> 8
    low = length - (high << 8)
    row8 = lax.broadcasted_iota(jnp.int32, (8, wide), 0)
    both = jnp.where(row8 == 1, pltpu.roll(low, 1, 0), high).astype(F32).astype(BF16)
    until = lax.broadcasted_iota(jnp.int32, (wide, wide), 0)
    upto = lax.broadcasted_iota(jnp.int32, (wide, wide), 1)
    lower = jnp.where(upto <= until, 1.0, 0.0).astype(BF16)
    sums = dot(lower, both, NT)

    @pl.when(has_next)
    def _():
        for copy in far_v:
            copy.start()

    base = chip * (GROUP * SPAN)
    ends = sums[:, 0:1] * 256.0 + sums[:, 1:2] - base.astype(F32)
    least = -base.astype(F32)
    key_row = lax.broadcasted_iota(jnp.int32, (SPAN, SPAN), 0).astype(F32)
    query_col = lax.broadcasted_iota(jnp.int32, (SPAN, SPAN), 1).astype(F32)
    for j in range(GROUP):
        pos = query_col[0:1] + float(j * SPAN)
        start = jnp.max(jnp.where(ends <= pos, ends, least), axis=0, keepdims=True)
        for b in range(GROUP + 1):
            key = b if b <= j else b - 1 - GROUP
            ok = key_row + float(key * SPAN) >= start
            if b == j:
                ok = ok & (key_row <= query_col)
            bias[j, b * SPAN : (b + 1) * SPAN] = jnp.where(ok, 0.0, -1e30)

    local[3].wait()
    back = jnp.maximum(chip - 1, 0)
    here = [assign_s[s % 2, 2 * chip + s // 2] & (GROUP - 1) for s in range(GROUP)]
    there = [assign_s[s % 2, 2 * back + s // 2] & (GROUP - 1) for s in range(GROUP)]
    for copy in (local[0], local[1], local[4], local[5]):
        copy.wait()
    for copy in near:
        copy.wait_recv()
    for j in range(GROUP):
        slot = pick(here, j)
        rows = slice(j * SPAN, (j + 1) * SPAN)
        kb = kown[slot]
        vb = vown[slot]
        ko[rows] = kb
        vo[rows] = vb
        kot[:, rows] = kb.T
        vot[:, rows] = vb.T
        qb = qslot[slot]
        gb = gslot[slot]
        for h in range(heads):
            cols = slice(h * DIM, (h + 1) * DIM)
            qr[j, cols] = qb[:, cols]
            gr[j, cols] = gb[:, cols]
            qt[j, :, cols] = qb[:, cols].T
            gt[j, :, cols] = gb[:, cols].T

    scale = ROOT * math.log2(math.e)
    part_p[...] = jnp.zeros_like(part_p)
    part_o[...] = jnp.zeros_like(part_o)

    def masked(keys, j, rows):
        return dot(keys, qt[j], NN) * scale + every_head(bias[j, rows], heads)

    tops = []
    for j in range(GROUP):
        own = slice(0, (j + 1) * SPAN)
        s = masked(ko[own], j, own)
        expo[j, own] = s
        tops.append(jnp.max(s, axis=0, keepdims=True))
    for j in range(GROUP):
        own = slice(0, (j + 1) * SPAN)
        dpo[j, own] = dot(vo[own], gt[j], NN)
    for j in range(GROUP):
        own = slice(0, (j + 1) * SPAN)
        e = jnp.exp2(expo[j, own] - tops[j])
        expo[j, own] = e
        stat[j, 0:1] = tops[j]
        stat[j, 1:2] = jnp.sum(e, axis=0, keepdims=True)
        oto[j] = dot(vot[:, own], e.astype(BF16), NN)

    @pl.when(has_prev)
    def _():
        for a in range(2):
            far_k[a].wait_recv()
            relay_k[a].start()
        for a in range(2):
            relay_k[a].wait_recv()

    @pl.when(jnp.logical_not(has_prev))
    def _():
        kprev[...] = jnp.zeros_like(kprev)
        vprev[...] = jnp.zeros_like(vprev)

    for i in range(GROUP):
        rows = slice(i * SPAN, (i + 1) * SPAN)
        kb = kprev[pick(there, i)]
        kp[rows] = kb
        kpt[:, rows] = kb.T

    tops = []
    for j in range(GROUP):
        at = (j + 1) * SPAN
        s = masked(kp[j * SPAN :], j, slice(at, None))
        expo[j, at:] = s
        tops.append(jnp.maximum(stat[j, 0:1], jnp.max(s, axis=0, keepdims=True)))
    norms = []
    alphas = []
    for j in range(GROUP):
        at = (j + 1) * SPAN
        e = jnp.exp2(expo[j, at:] - tops[j])
        expo[j, at:] = e
        shrink = jnp.exp2(stat[j, 0:1] - tops[j])
        r = 1.0 / (stat[j, 1:2] * shrink + jnp.sum(e, axis=0, keepdims=True))
        norms.append(r)
        alphas.append(shrink * r)
        if j == 1:

            @pl.when(has_prev)
            def _():
                for a in range(2):
                    far_v[a].wait_recv()
                    relay_v[a].start()

    for j in range(GROUP):
        at = (j + 1) * SPAN
        pb[j, at:] = (expo[j, at:] * norms[j]).astype(BF16)

    @pl.when(has_prev)
    def _():
        for a in range(2):
            relay_v[a].wait_recv()

    for i in range(GROUP):
        rows = slice(i * SPAN, (i + 1) * SPAN)
        vb = vprev[pick(there, i)]
        vp[rows] = vb
        vpt[:, rows] = vb.T

    deltas = []

    def finish_out(j):
        out = oto[j] * alphas[j] + dot(vpt[:, j * SPAN :], pb[j, (j + 1) * SPAN :], NN)
        deltas.append(jnp.sum(out * gt[j].astype(F32), axis=0, keepdims=True))
        out = out.astype(BF16)
        for h in range(heads):
            cols = slice(h * DIM, (h + 1) * DIM)
            o_mine[j, :, cols] = out[:, cols].T

    def prev_dprobs(j):
        return dot(vp[j * SPAN :], gt[j], NN)

    def prev_grads(j, dp):
        at = (j + 1) * SPAN
        ds = (expo[j, at:] * norms[j] * (dp - deltas[j])).astype(BF16)
        sb[j, at:] = ds
        part_p[j:, :, 0:DIM] += spans(dot(ds, qr[j], NN) * ROOT)
        part_p[j:, :, DIM:] += spans(dot(pb[j, at:], gr[j], NN))

    finish_out(0)
    dp = prev_dprobs(0)
    for j in range(1, GROUP):
        finish_out(j)
        next_dp = prev_dprobs(j)
        prev_grads(j - 1, dp)
        dp = next_dp
    prev_grads(GROUP - 1, dp)

    def mine_of(spans, a):
        return jnp.where(core == 0, spans[a], spans[2 + a])

    def theirs_of(spans, a):
        return jnp.where(core == 0, spans[2 + a], spans[a])

    swap_p = [remote(sum_send.at[a], sum_near.at[a], p_s.at[a], p_r.at[a], beside)
              for a in range(2)]
    far_p = [remote(far_send_buf.at[a], far_buf.at[a], f_s.at[a], f_r.at[a], before)
             for a in range(2)]
    for a in range(2):
        sum_send[a] = part_p[theirs_of(there, a)].astype(BF16)
        swap_p[a].start()

    swap_out = remote(o_mine, o_near, oq_s.at[GROUP], oq_r.at[GROUP], beside)
    swap_dq = [remote(q_mine.at[j], q_near.at[j], oq_s.at[j], oq_r.at[j], beside)
               for j in range(GROUP)]
    swap_out.start()

    def own_dscores(j):
        own = slice(0, (j + 1) * SPAN)
        pr = expo[j, own] * alphas[j]
        pb[j, own] = pr.astype(BF16)
        sb[j, own] = (pr * (dpo[j, own] - deltas[j])).astype(BF16)

    def own_grads(j):
        own = slice(0, (j + 1) * SPAN)
        at = (j + 1) * SPAN
        dqt = dot(kot[:, own], sb[j, own], NN) + dot(kpt[:, j * SPAN :], sb[j, at:], NN)
        dqt = (dqt * ROOT).astype(BF16)
        for h in range(heads):
            cols = slice(h * DIM, (h + 1) * DIM)
            q_mine[j, :, cols] = dqt[:, cols].T
        part_o[0 : j + 1, :, 0:DIM] += spans(dot(sb[j, own], qr[j], NN) * ROOT)
        part_o[0 : j + 1, :, DIM:] += spans(dot(pb[j, own], gr[j], NN))

    own_dscores(0)
    own_dscores(1)
    own_grads(0)
    own_dscores(2)
    own_grads(1)

    for a in range(2):
        swap_p[a].wait_recv()
        far_send_buf[a] = (
            part_p[mine_of(there, a)] + sum_near[a].astype(F32)).astype(BF16)

        @pl.when(has_prev)
        def _(a=a):
            far_p[a].start()

    for j in range(2):
        swap_dq[j].start()
    own_dscores(3)
    own_grads(2)
    swap_dq[2].start()
    own_grads(3)
    swap_dq[3].start()

    swap_o = [remote(own_send.at[a], own_near.at[a], o_s.at[a], o_r.at[a], beside)
              for a in range(2)]
    for a in range(2):
        own_send[a] = part_o[theirs_of(here, a)].astype(BF16)
        swap_o[a].start()

    for a in range(2):
        j = mine_of(here, a)
        attn[a, :, columns(core)] = o_mine[j]
        dq[a, :, columns(core)] = q_mine[j]
    swap_out.wait_recv()
    for a in range(2):
        attn[a, :, columns(other)] = o_near[mine_of(here, a)]
    for j in range(GROUP):
        swap_dq[j].wait_recv()
    for a in range(2):
        dq[a, :, columns(other)] = q_near[mine_of(here, a)]

    @pl.when(jnp.logical_not(has_next))
    def _():
        far_buf[...] = jnp.zeros_like(far_buf)

    for a in range(2):
        swap_o[a].wait_recv()

        @pl.when(has_next)
        def _(a=a):
            far_p[a].wait_recv()

        total = part_o[mine_of(here, a)] + own_near[a].astype(F32) + far_buf[a].astype(F32)
        dk[a] = total[:, 0:DIM].astype(BF16)
        dv[a] = total[:, DIM:].astype(BF16)

    for copy in near + swap_p + [swap_out] + swap_dq + swap_o:
        copy.wait_send()

    @pl.when(has_next)
    def _():
        for copy in far_k + far_v:
            copy.wait_send()

    @pl.when(has_prev)
    def _():
        for copy in relay_k + relay_v + far_p:
            copy.wait_send()


def store_kernel(*refs):
    n = (len(refs) - 1) // 2
    sem = refs[2 * n]
    copies = []
    for i in range(n):
        for a in range(2):
            copies.append(
                pltpu.make_async_copy(refs[i].at[a], refs[n + i].at[a], sem.at[len(copies)]))
    for copy in copies:
        copy.start()
    for copy in copies:
        copy.wait()


def shards(count, queries, keys, values, grad_out, lengths, assign):
    width = queries.shape[1]
    half = width // 2
    docs = lengths.shape[0]
    wide = -(-docs // 128) * 128
    hbm = pl.BlockSpec(memory_space=pltpu.HBM)
    vmem = pl.BlockSpec(memory_space=pltpu.VMEM)
    dma = pltpu.SemaphoreType.DMA
    shape = jax.ShapeDtypeStruct
    keyed = GROUP * SPAN
    seen = keyed + SPAN
    outs = (
        shape((2, SPAN, width), BF16),
        shape((2, SPAN, width), BF16),
        shape((2, SPAN, DIM), BF16),
        shape((2, SPAN, DIM), BF16),
    )
    results = pl.pallas_call(
        functools.partial(main_kernel, count),
        out_shape=outs,
        in_specs=[hbm] * 6,
        out_specs=(vmem,) * 4,
        scratch_shapes=[
            pltpu.VMEM((docs,), jnp.int32),
            pltpu.SMEM(assign.shape[::-1], jnp.int32),
            pltpu.VMEM((8, wide), jnp.int32),
            pltpu.VMEM((GROUP, SPAN, half), BF16),
            pltpu.VMEM((GROUP, SPAN, half), BF16),
            pltpu.VMEM((GROUP, SPAN, DIM), BF16),
            pltpu.VMEM((GROUP, SPAN, DIM), BF16),
            pltpu.VMEM((GROUP, SPAN, DIM), BF16),
            pltpu.VMEM((GROUP, SPAN, DIM), BF16),
            pltpu.VMEM((GROUP, half, DIM), BF16),
            pltpu.VMEM((GROUP, half, DIM), BF16),
            pltpu.VMEM((GROUP, DIM, half), BF16),
            pltpu.VMEM((GROUP, DIM, half), BF16),
            pltpu.VMEM((keyed, DIM), BF16),
            pltpu.VMEM((keyed, DIM), BF16),
            pltpu.VMEM((DIM, keyed), BF16),
            pltpu.VMEM((DIM, keyed), BF16),
            pltpu.VMEM((keyed, DIM), BF16),
            pltpu.VMEM((keyed, DIM), BF16),
            pltpu.VMEM((DIM, keyed), BF16),
            pltpu.VMEM((DIM, keyed), BF16),
            pltpu.VMEM((GROUP, seen, SPAN), F32),
            pltpu.VMEM((GROUP, seen, half), F32),
            pltpu.VMEM((GROUP, keyed, half), F32),
            pltpu.VMEM((GROUP, seen, half), BF16),
            pltpu.VMEM((GROUP, seen, half), BF16),
            pltpu.VMEM((GROUP, DIM, half), F32),
            pltpu.VMEM((GROUP, 8, half), F32),
            pltpu.VMEM((GROUP, SPAN, 2 * DIM), F32),
            pltpu.VMEM((GROUP, SPAN, 2 * DIM), F32),
            pltpu.VMEM((2, SPAN, 2 * DIM), BF16),
            pltpu.VMEM((2, SPAN, 2 * DIM), BF16),
            pltpu.VMEM((2, SPAN, 2 * DIM), BF16),
            pltpu.VMEM((2, SPAN, 2 * DIM), BF16),
            pltpu.VMEM((2, SPAN, 2 * DIM), BF16),
            pltpu.VMEM((2, SPAN, 2 * DIM), BF16),
            pltpu.VMEM((GROUP, SPAN, half), BF16),
            pltpu.VMEM((GROUP, SPAN, half), BF16),
            pltpu.VMEM((GROUP, SPAN, half), BF16),
            pltpu.VMEM((GROUP, SPAN, half), BF16),
            dma((6,)),
            dma((2,)), dma((2,)), dma((2,)), dma((2,)),
            dma((2,)), dma((2,)), dma((2,)), dma((2,)),
            dma((4,)), dma((4,)),
            dma((2,)), dma((2,)), dma((2,)), dma((2,)), dma((2,)), dma((2,)),
            dma((GROUP + 1,)), dma((GROUP + 1,)),
        ],
        compiler_params=pltpu.CompilerParams(
            collective_id=0, has_side_effects=True, vmem_limit_bytes=40 * 2**20),
        name="attend",
    )(*[
        pltpu.with_memory_space_constraint(x, pltpu.HBM)
        for x in (
            queries.reshape(2, SPAN, width), grad_out.reshape(2, SPAN, width),
            keys.reshape(2, SPAN, DIM), values.reshape(2, SPAN, DIM), lengths, assign.T,
        )
    ])
    results = pl.pallas_call(
        store_kernel,
        out_shape=outs,
        in_specs=[pl.BlockSpec(memory_space=pltpu.VMEM)] * 4,
        out_specs=(hbm,) * 4,
        scratch_shapes=[dma((8,))],
        name="store",
    )(*[pltpu.with_memory_space_constraint(r, pltpu.VMEM) for r in results])
    return tuple(r.reshape(2 * SPAN, r.shape[2]) for r in results)


def solution(mesh):
    split = P("seq", "grp")
    return jax.shard_map(
        functools.partial(shards, mesh.shape["seq"]),
        mesh=mesh,
        in_specs=(split, split, split, split, P(), P()),
        out_specs=(split, split, split, split),
        check_vma=False,
    )
```

```python
import functools
import math

import jax
import jax.numpy as jnp
from jax import lax
from jax.experimental import pallas as pl
from jax.experimental.pallas import tpu as pltpu
from jax.sharding import PartitionSpec as P

MESH = pl.DeviceIdType.MESH
SPAN = 128
DIM = 128
GROUP = 4
F32 = jnp.float32
BF16 = jnp.bfloat16
NT = (((1,), (1,)), ((), ()))
NN = (((1,), (0,)), ((), ()))
ROOT = 1.0 / math.sqrt(DIM)
PIECE = 32


def dot(a, b, dims):
    return lax.dot_general(a, b, dims, preferred_element_type=F32)


def pick(values, wanted):
    index = jnp.int32(0)
    for i, value in enumerate(values):
        index = jnp.where(value == wanted, i, index)
    return index


def every_head(x, heads):
    return jnp.concatenate([x] * heads, axis=1)


def spans(x):
    return x.reshape(x.shape[0] // SPAN, SPAN, x.shape[1])


def fold(x, reduce):
    return reduce(x.reshape(x.shape[0] // 8, 8, x.shape[1]), axis=0)


def main_kernel(
    count, q, g, k, v, lens, assign, attn, dq, dk, dv,
    lens_v, assign_s, padded, qslot, gslot, kown, vown, kprev, vprev, qr, gr, qt, gt,
    ko, vo, kot, vot, kp, vp, kpt, vpt, bias, expo, dpo, pb, sb, oto, stat,
    part_p, part_o, sum_send, sum_near, far_send_buf, far_buf, own_send, own_near,
    o_mine, o_near, q_mine, q_near,
    loc_sem, far_ks, far_kr, far_vs, far_vr, rel_ks, rel_kr, rel_vs, rel_vr,
    near_s, near_r, p_s, p_r, f_s, f_r, o_s, o_r, oq_s, oq_r,
):
    me = lax.axis_index("seq")
    grp = lax.axis_index("grp")
    core = lax.rem(me, 2)
    other = 1 - core
    chip = me // 2
    beside = me + 1 - 2 * core
    has_prev = chip > 0
    has_next = chip < count // 2 - 1
    before = jnp.where(has_prev, me - 2, me)
    after = jnp.where(has_next, me + 2, me)
    width = q.shape[2] // 2
    heads = width // DIM

    def remote(src, dst, send, recv, device):
        return pltpu.make_async_remote_copy(
            src_ref=src, dst_ref=dst, send_sem=send, recv_sem=recv,
            device_id=(device, grp), device_id_type=MESH,
        )

    def columns(which):
        return pl.ds(pl.multiple_of(which * width, width), width)

    own_slots = pl.ds(2 * core, 2)
    local = [
        pltpu.make_async_copy(k, kown.at[own_slots], loc_sem.at[0]),
        pltpu.make_async_copy(v, vown.at[own_slots], loc_sem.at[1]),
        pltpu.make_async_copy(lens, lens_v, loc_sem.at[2]),
        pltpu.make_async_copy(assign, assign_s, loc_sem.at[3]),
        pltpu.make_async_copy(q.at[:, :, columns(core)], qslot.at[own_slots], loc_sem.at[4]),
        pltpu.make_async_copy(g.at[:, :, columns(core)], gslot.at[own_slots], loc_sem.at[5]),
    ]
    far_k = [remote(k.at[a], kprev.at[2 * core + a], far_ks.at[a], far_kr.at[a], after)
             for a in range(2)]
    far_v = [remote(v.at[a], vprev.at[2 * core + a], far_vs.at[a], far_vr.at[a], after)
             for a in range(2)]
    relay_k = [remote(kprev.at[2 * core + a], kprev.at[2 * core + a], rel_ks.at[a], rel_kr.at[a],
                      beside) for a in range(2)]
    relay_v = [remote(vprev.at[2 * core + a], vprev.at[2 * core + a], rel_vs.at[a], rel_vr.at[a],
                      beside) for a in range(2)]
    near = [
        remote(k, kown.at[own_slots], near_s.at[0], near_r.at[0], beside),
        remote(v, vown.at[own_slots], near_s.at[1], near_r.at[1], beside),
        remote(q.at[:, :, columns(other)], qslot.at[own_slots], near_s.at[2], near_r.at[2], beside),
        remote(g.at[:, :, columns(other)], gslot.at[own_slots], near_s.at[3], near_r.at[3], beside),
    ]

    barrier = pltpu.get_barrier_semaphore()
    pl.semaphore_signal(barrier, inc=1, device_id=(beside, grp), device_id_type=MESH)

    @pl.when(has_prev)
    def _():
        pl.semaphore_signal(barrier, inc=1, device_id=(before, grp), device_id_type=MESH)

    @pl.when(has_next)
    def _():
        pl.semaphore_signal(barrier, inc=1, device_id=(after, grp), device_id_type=MESH)

    for copy in local:
        copy.start()
    pl.semaphore_wait(
        barrier, 1 + has_prev.astype(jnp.int32) + has_next.astype(jnp.int32))

    @pl.when(has_next)
    def _():
        for copy in far_k:
            copy.start()

    for copy in near:
        copy.start()

    docs = lens_v.shape[0]
    wide = padded.shape[1]
    padded[...] = jnp.zeros_like(padded)
    local[2].wait()
    padded[0:1, 0:docs] = lens_v[...].reshape(1, docs)
    length = padded[...]
    high = length >> 8
    low = length - (high << 8)
    row8 = lax.broadcasted_iota(jnp.int32, (8, wide), 0)
    both = jnp.where(row8 == 1, pltpu.roll(low, 1, 0), high).astype(F32).astype(BF16)
    until = lax.broadcasted_iota(jnp.int32, (wide, wide), 0)
    upto = lax.broadcasted_iota(jnp.int32, (wide, wide), 1)
    lower = jnp.where(upto <= until, 1.0, 0.0).astype(BF16)
    sums = dot(lower, both, NT)

    @pl.when(has_next)
    def _():
        for copy in far_v:
            copy.start()

    base = chip * (GROUP * SPAN)
    ends = sums[:, 0:1] * 256.0 + sums[:, 1:2] - base.astype(F32)
    least = -base.astype(F32)
    key_row = lax.broadcasted_iota(jnp.int32, (SPAN, SPAN), 0).astype(F32)
    query_col = lax.broadcasted_iota(jnp.int32, (SPAN, SPAN), 1).astype(F32)
    for j in range(GROUP):
        pos = query_col[0:1] + float(j * SPAN)
        start = jnp.max(jnp.where(ends <= pos, ends, least), axis=0, keepdims=True)
        for b in range(GROUP + 1):
            key = b if b <= j else b - 1 - GROUP
            ok = key_row + float(key * SPAN) >= start
            if b == j:
                ok = ok & (key_row <= query_col)
            bias[j, b * SPAN : (b + 1) * SPAN] = jnp.where(ok, 0.0, -1e30)

    local[3].wait()
    back = jnp.maximum(chip - 1, 0)
    here = [assign_s[s % 2, 2 * chip + s // 2] & (GROUP - 1) for s in range(GROUP)]
    there = [assign_s[s % 2, 2 * back + s // 2] & (GROUP - 1) for s in range(GROUP)]
    for copy in (local[0], local[1], local[4], local[5]):
        copy.wait()
    for copy in near:
        copy.wait_recv()
    for j in range(GROUP):
        slot = pick(here, j)
        rows = slice(j * SPAN, (j + 1) * SPAN)
        kb = kown[slot]
        vb = vown[slot]
        ko[rows] = kb
        vo[rows] = vb
        kot[:, rows] = kb.T
        vot[:, rows] = vb.T
        qb = qslot[slot]
        gb = gslot[slot]
        for h in range(heads):
            cols = slice(h * DIM, (h + 1) * DIM)
            qr[j, cols] = qb[:, cols]
            gr[j, cols] = gb[:, cols]
            qt[j, :, cols] = qb[:, cols].T
            gt[j, :, cols] = gb[:, cols].T

    scale = ROOT * math.log2(math.e)
    part_p[...] = jnp.zeros_like(part_p)
    part_o[...] = jnp.zeros_like(part_o)

    def scores(keys, j, first, n):
        s = dot(keys, qt[j], NN)
        top = None
        for at in range(0, n, PIECE):
            rows = slice(first + at, first + at + PIECE)
            piece = s[at : at + PIECE] * scale + every_head(bias[j, rows], heads)
            expo[j, rows] = piece
            top = fold(piece, jnp.max) if top is None else jnp.maximum(top, fold(piece, jnp.max))
        return jnp.max(top, axis=0, keepdims=True)

    def exponentials(j, first, n, top, low=None):
        total = None
        for at in range(0, n, PIECE):
            rows = slice(first + at, first + at + PIECE)
            e = jnp.exp2(expo[j, rows] - top)
            expo[j, rows] = e
            if low is not None:
                low[j, rows] = e.astype(BF16)
            total = fold(e, jnp.sum) if total is None else total + fold(e, jnp.sum)
        return jnp.sum(total, axis=0, keepdims=True)

    tops = []
    for j in range(GROUP):
        n = (j + 1) * SPAN
        tops.append(scores(ko[0:n], j, 0, n))
        dpo[j, 0:n] = dot(vo[0:n], gt[j], NN)
    for j in range(GROUP):
        n = (j + 1) * SPAN
        stat[j, 0:1] = tops[j]
        stat[j, 1:2] = exponentials(j, 0, n, tops[j], pb)
        oto[j] = dot(vot[:, 0:n], pb[j, 0:n], NN)

    @pl.when(has_prev)
    def _():
        for a in range(2):
            far_k[a].wait_recv()
            relay_k[a].start()
        for a in range(2):
            relay_k[a].wait_recv()

    @pl.when(jnp.logical_not(has_prev))
    def _():
        kprev[...] = jnp.zeros_like(kprev)
        vprev[...] = jnp.zeros_like(vprev)

    for i in range(GROUP):
        rows = slice(i * SPAN, (i + 1) * SPAN)
        kb = kprev[pick(there, i)]
        kp[rows] = kb
        kpt[:, rows] = kb.T

    tops = []
    for j in range(GROUP):
        top = scores(kp[j * SPAN :], j, (j + 1) * SPAN, (GROUP - j) * SPAN)
        tops.append(jnp.maximum(stat[j, 0:1], top))
    norms = []
    alphas = []
    for j in range(GROUP):
        total = exponentials(j, (j + 1) * SPAN, (GROUP - j) * SPAN, tops[j])
        shrink = jnp.exp2(stat[j, 0:1] - tops[j])
        r = 1.0 / (stat[j, 1:2] * shrink + total)
        norms.append(r)
        alphas.append(shrink * r)
        if j == 1:

            @pl.when(has_prev)
            def _():
                for a in range(2):
                    far_v[a].wait_recv()
                    relay_v[a].start()

    for j in range(GROUP):
        for at in range((j + 1) * SPAN, expo.shape[1], PIECE):
            rows = slice(at, at + PIECE)
            pr = expo[j, rows] * norms[j]
            expo[j, rows] = pr
            pb[j, rows] = pr.astype(BF16)

    @pl.when(has_prev)
    def _():
        for a in range(2):
            relay_v[a].wait_recv()

    for i in range(GROUP):
        rows = slice(i * SPAN, (i + 1) * SPAN)
        vb = vprev[pick(there, i)]
        vp[rows] = vb
        vpt[:, rows] = vb.T

    deltas = []

    def finish_out(j):
        out = oto[j] * alphas[j] + dot(vpt[:, j * SPAN :], pb[j, (j + 1) * SPAN :], NN)
        deltas.append(jnp.sum(out * gt[j].astype(F32), axis=0, keepdims=True))
        out = out.astype(BF16)
        for h in range(heads):
            cols = slice(h * DIM, (h + 1) * DIM)
            o_mine[j, :, cols] = out[:, cols].T

    def prev_dprobs(j):
        return dot(vp[j * SPAN :], gt[j], NN)

    def prev_grads(j, dp):
        at = (j + 1) * SPAN
        for p in range(0, dp.shape[0], PIECE):
            rows = slice(at + p, at + p + PIECE)
            sb[j, rows] = (expo[j, rows] * (dp[p : p + PIECE] - deltas[j])).astype(BF16)
        part_p[j:, :, 0:DIM] += spans(dot(sb[j, at:], qr[j], NN) * ROOT)
        part_p[j:, :, DIM:] += spans(dot(pb[j, at:], gr[j], NN))

    finish_out(0)
    dp = prev_dprobs(0)
    for j in range(1, GROUP):
        finish_out(j)
        next_dp = prev_dprobs(j)
        prev_grads(j - 1, dp)
        dp = next_dp
    prev_grads(GROUP - 1, dp)

    def mine_of(spans, a):
        return jnp.where(core == 0, spans[a], spans[2 + a])

    def theirs_of(spans, a):
        return jnp.where(core == 0, spans[2 + a], spans[a])

    swap_p = [remote(sum_send.at[a], sum_near.at[a], p_s.at[a], p_r.at[a], beside)
              for a in range(2)]
    far_p = [remote(far_send_buf.at[a], far_buf.at[a], f_s.at[a], f_r.at[a], before)
             for a in range(2)]
    for a in range(2):
        sum_send[a] = part_p[theirs_of(there, a)].astype(BF16)
        swap_p[a].start()

    swap_out = remote(o_mine, o_near, oq_s.at[GROUP], oq_r.at[GROUP], beside)
    swap_dq = [remote(q_mine.at[j], q_near.at[j], oq_s.at[j], oq_r.at[j], beside)
               for j in range(GROUP)]
    swap_out.start()

    def own_dscores(j):
        for at in range(0, (j + 1) * SPAN, PIECE):
            rows = slice(at, at + PIECE)
            pr = expo[j, rows] * alphas[j]
            pb[j, rows] = pr.astype(BF16)
            sb[j, rows] = (pr * (dpo[j, rows] - deltas[j])).astype(BF16)

    def own_grads(j):
        own = slice(0, (j + 1) * SPAN)
        at = (j + 1) * SPAN
        dqt = dot(kot[:, own], sb[j, own], NN) + dot(kpt[:, j * SPAN :], sb[j, at:], NN)
        dqt = (dqt * ROOT).astype(BF16)
        for h in range(heads):
            cols = slice(h * DIM, (h + 1) * DIM)
            q_mine[j, :, cols] = dqt[:, cols].T
        part_o[0 : j + 1, :, 0:DIM] += spans(dot(sb[j, own], qr[j], NN) * ROOT)
        part_o[0 : j + 1, :, DIM:] += spans(dot(pb[j, own], gr[j], NN))

    own_dscores(0)
    own_dscores(1)
    own_grads(0)
    own_dscores(2)
    own_grads(1)

    for a in range(2):
        swap_p[a].wait_recv()
        far_send_buf[a] = (
            part_p[mine_of(there, a)] + sum_near[a].astype(F32)).astype(BF16)

        @pl.when(has_prev)
        def _(a=a):
            far_p[a].start()

    for j in range(2):
        swap_dq[j].start()
    own_dscores(3)
    own_grads(2)
    swap_dq[2].start()
    own_grads(3)
    swap_dq[3].start()

    swap_o = [remote(own_send.at[a], own_near.at[a], o_s.at[a], o_r.at[a], beside)
              for a in range(2)]
    for a in range(2):
        own_send[a] = part_o[theirs_of(here, a)].astype(BF16)
        swap_o[a].start()

    for a in range(2):
        j = mine_of(here, a)
        attn[a, :, columns(core)] = o_mine[j]
        dq[a, :, columns(core)] = q_mine[j]
    swap_out.wait_recv()
    for a in range(2):
        attn[a, :, columns(other)] = o_near[mine_of(here, a)]
    for j in range(GROUP):
        swap_dq[j].wait_recv()
    for a in range(2):
        dq[a, :, columns(other)] = q_near[mine_of(here, a)]

    @pl.when(jnp.logical_not(has_next))
    def _():
        far_buf[...] = jnp.zeros_like(far_buf)

    for a in range(2):
        swap_o[a].wait_recv()

        @pl.when(has_next)
        def _(a=a):
            far_p[a].wait_recv()

        total = part_o[mine_of(here, a)] + own_near[a].astype(F32) + far_buf[a].astype(F32)
        dk[a] = total[:, 0:DIM].astype(BF16)
        dv[a] = total[:, DIM:].astype(BF16)

    for copy in near + swap_p + [swap_out] + swap_dq + swap_o:
        copy.wait_send()

    @pl.when(has_next)
    def _():
        for copy in far_k + far_v:
            copy.wait_send()

    @pl.when(has_prev)
    def _():
        for copy in relay_k + relay_v + far_p:
            copy.wait_send()


def store_kernel(*refs):
    n = (len(refs) - 1) // 2
    sem = refs[2 * n]
    copies = []
    for i in range(n):
        for a in range(2):
            copies.append(
                pltpu.make_async_copy(refs[i].at[a], refs[n + i].at[a], sem.at[len(copies)]))
    for copy in copies:
        copy.start()
    for copy in copies:
        copy.wait()


def shards(count, queries, keys, values, grad_out, lengths, assign):
    width = queries.shape[1]
    half = width // 2
    docs = lengths.shape[0]
    wide = -(-docs // 128) * 128
    hbm = pl.BlockSpec(memory_space=pltpu.HBM)
    vmem = pl.BlockSpec(memory_space=pltpu.VMEM)
    dma = pltpu.SemaphoreType.DMA
    shape = jax.ShapeDtypeStruct
    keyed = GROUP * SPAN
    seen = keyed + SPAN
    outs = (
        shape((2, SPAN, width), BF16),
        shape((2, SPAN, width), BF16),
        shape((2, SPAN, DIM), BF16),
        shape((2, SPAN, DIM), BF16),
    )
    results = pl.pallas_call(
        functools.partial(main_kernel, count),
        out_shape=outs,
        in_specs=[hbm] * 6,
        out_specs=(vmem,) * 4,
        scratch_shapes=[
            pltpu.VMEM((docs,), jnp.int32),
            pltpu.SMEM(assign.shape[::-1], jnp.int32),
            pltpu.VMEM((8, wide), jnp.int32),
            pltpu.VMEM((GROUP, SPAN, half), BF16),
            pltpu.VMEM((GROUP, SPAN, half), BF16),
            pltpu.VMEM((GROUP, SPAN, DIM), BF16),
            pltpu.VMEM((GROUP, SPAN, DIM), BF16),
            pltpu.VMEM((GROUP, SPAN, DIM), BF16),
            pltpu.VMEM((GROUP, SPAN, DIM), BF16),
            pltpu.VMEM((GROUP, half, DIM), BF16),
            pltpu.VMEM((GROUP, half, DIM), BF16),
            pltpu.VMEM((GROUP, DIM, half), BF16),
            pltpu.VMEM((GROUP, DIM, half), BF16),
            pltpu.VMEM((keyed, DIM), BF16),
            pltpu.VMEM((keyed, DIM), BF16),
            pltpu.VMEM((DIM, keyed), BF16),
            pltpu.VMEM((DIM, keyed), BF16),
            pltpu.VMEM((keyed, DIM), BF16),
            pltpu.VMEM((keyed, DIM), BF16),
            pltpu.VMEM((DIM, keyed), BF16),
            pltpu.VMEM((DIM, keyed), BF16),
            pltpu.VMEM((GROUP, seen, SPAN), F32),
            pltpu.VMEM((GROUP, seen, half), F32),
            pltpu.VMEM((GROUP, keyed, half), F32),
            pltpu.VMEM((GROUP, seen, half), BF16),
            pltpu.VMEM((GROUP, seen, half), BF16),
            pltpu.VMEM((GROUP, DIM, half), F32),
            pltpu.VMEM((GROUP, 8, half), F32),
            pltpu.VMEM((GROUP, SPAN, 2 * DIM), F32),
            pltpu.VMEM((GROUP, SPAN, 2 * DIM), F32),
            pltpu.VMEM((2, SPAN, 2 * DIM), BF16),
            pltpu.VMEM((2, SPAN, 2 * DIM), BF16),
            pltpu.VMEM((2, SPAN, 2 * DIM), BF16),
            pltpu.VMEM((2, SPAN, 2 * DIM), BF16),
            pltpu.VMEM((2, SPAN, 2 * DIM), BF16),
            pltpu.VMEM((2, SPAN, 2 * DIM), BF16),
            pltpu.VMEM((GROUP, SPAN, half), BF16),
            pltpu.VMEM((GROUP, SPAN, half), BF16),
            pltpu.VMEM((GROUP, SPAN, half), BF16),
            pltpu.VMEM((GROUP, SPAN, half), BF16),
            dma((6,)),
            dma((2,)), dma((2,)), dma((2,)), dma((2,)),
            dma((2,)), dma((2,)), dma((2,)), dma((2,)),
            dma((4,)), dma((4,)),
            dma((2,)), dma((2,)), dma((2,)), dma((2,)), dma((2,)), dma((2,)),
            dma((GROUP + 1,)), dma((GROUP + 1,)),
        ],
        compiler_params=pltpu.CompilerParams(
            collective_id=0, has_side_effects=True, vmem_limit_bytes=40 * 2**20),
        name="attend",
    )(*[
        pltpu.with_memory_space_constraint(x, pltpu.HBM)
        for x in (
            queries.reshape(2, SPAN, width), grad_out.reshape(2, SPAN, width),
            keys.reshape(2, SPAN, DIM), values.reshape(2, SPAN, DIM), lengths, assign.T,
        )
    ])
    results = pl.pallas_call(
        store_kernel,
        out_shape=outs,
        in_specs=[pl.BlockSpec(memory_space=pltpu.VMEM)] * 4,
        out_specs=(hbm,) * 4,
        scratch_shapes=[dma((8,))],
        name="store",
    )(*[pltpu.with_memory_space_constraint(r, pltpu.VMEM) for r in results])
    return tuple(r.reshape(2 * SPAN, r.shape[2]) for r in results)


def solution(mesh):
    split = P("seq", "grp")
    return jax.shard_map(
        functools.partial(shards, mesh.shape["seq"]),
        mesh=mesh,
        in_specs=(split, split, split, split, P(), P()),
        out_specs=(split, split, split, split),
        check_vma=False,
    )
```

```python
import functools
import math

import jax
import jax.numpy as jnp
from jax import lax
from jax.experimental import pallas as pl
from jax.experimental.pallas import tpu as pltpu
from jax.sharding import PartitionSpec as P

MESH = pl.DeviceIdType.MESH
SPAN = 128
DIM = 128
GROUP = 4
F32 = jnp.float32
BF16 = jnp.bfloat16
NT = (((1,), (1,)), ((), ()))
NN = (((1,), (0,)), ((), ()))
ROOT = 1.0 / math.sqrt(DIM)
PIECE = 32


def dot(a, b, dims):
    return lax.dot_general(a, b, dims, preferred_element_type=F32)


def pick(values, wanted):
    index = jnp.int32(0)
    for i, value in enumerate(values):
        index = jnp.where(value == wanted, i, index)
    return index


def every_head(x, heads):
    return jnp.concatenate([x] * heads, axis=1)


def spans(x):
    return x.reshape(x.shape[0] // SPAN, SPAN, x.shape[1])


def fold(x, reduce):
    return reduce(x.reshape(x.shape[0] // 8, 8, x.shape[1]), axis=0)


def main_kernel(
    count, q, g, k, v, lens, assign, attn, dq, dk, dv,
    lens_v, assign_s, padded, qslot, gslot, kown, vown, kprev, vprev, qr, gr, qt, gt,
    ko, vo, kot, vot, kp, vp, kpt, vpt, bias, expo, dpo, pb, sb, oto, stat,
    part_p, part_o, sum_send, sum_near, far_send_buf, far_buf, own_send, own_near,
    o_mine, o_send, o_near, q_mine, q_send, q_near,
    loc_sem, far_ks, far_kr, far_vs, far_vr, rel_ks, rel_kr, rel_vs, rel_vr,
    near_s, near_r, p_s, p_r, f_s, f_r, o_s, o_r, oq_s, oq_r,
):
    me = lax.axis_index("seq")
    grp = lax.axis_index("grp")
    core = lax.rem(me, 2)
    other = 1 - core
    chip = me // 2
    beside = me + 1 - 2 * core
    has_prev = chip > 0
    has_next = chip < count // 2 - 1
    before = jnp.where(has_prev, me - 2, me)
    after = jnp.where(has_next, me + 2, me)
    width = q.shape[2] // 2
    heads = width // DIM

    def remote(src, dst, send, recv, device):
        return pltpu.make_async_remote_copy(
            src_ref=src, dst_ref=dst, send_sem=send, recv_sem=recv,
            device_id=(device, grp), device_id_type=MESH,
        )

    def columns(which):
        return pl.ds(pl.multiple_of(which * width, width), width)

    own_slots = pl.ds(2 * core, 2)
    local = [
        pltpu.make_async_copy(k, kown.at[own_slots], loc_sem.at[0]),
        pltpu.make_async_copy(v, vown.at[own_slots], loc_sem.at[1]),
        pltpu.make_async_copy(lens, lens_v, loc_sem.at[2]),
        pltpu.make_async_copy(assign, assign_s, loc_sem.at[3]),
        pltpu.make_async_copy(q.at[:, :, columns(core)], qslot.at[own_slots], loc_sem.at[4]),
        pltpu.make_async_copy(g.at[:, :, columns(core)], gslot.at[own_slots], loc_sem.at[5]),
    ]
    far_k = [remote(k.at[a], kprev.at[2 * core + a], far_ks.at[a], far_kr.at[a], after)
             for a in range(2)]
    far_v = [remote(v.at[a], vprev.at[2 * core + a], far_vs.at[a], far_vr.at[a], after)
             for a in range(2)]
    relay_k = [remote(kprev.at[2 * core + a], kprev.at[2 * core + a], rel_ks.at[a], rel_kr.at[a],
                      beside) for a in range(2)]
    relay_v = [remote(vprev.at[2 * core + a], vprev.at[2 * core + a], rel_vs.at[a], rel_vr.at[a],
                      beside) for a in range(2)]
    near = [
        remote(k, kown.at[own_slots], near_s.at[0], near_r.at[0], beside),
        remote(v, vown.at[own_slots], near_s.at[1], near_r.at[1], beside),
        remote(q.at[:, :, columns(other)], qslot.at[own_slots], near_s.at[2], near_r.at[2], beside),
        remote(g.at[:, :, columns(other)], gslot.at[own_slots], near_s.at[3], near_r.at[3], beside),
    ]

    barrier = pltpu.get_barrier_semaphore()
    pl.semaphore_signal(barrier, inc=1, device_id=(beside, grp), device_id_type=MESH)

    @pl.when(has_prev)
    def _():
        pl.semaphore_signal(barrier, inc=1, device_id=(before, grp), device_id_type=MESH)

    @pl.when(has_next)
    def _():
        pl.semaphore_signal(barrier, inc=1, device_id=(after, grp), device_id_type=MESH)

    for copy in local:
        copy.start()
    pl.semaphore_wait(
        barrier, 1 + has_prev.astype(jnp.int32) + has_next.astype(jnp.int32))

    @pl.when(has_next)
    def _():
        for copy in far_k + far_v:
            copy.start()

    for copy in near[:2]:
        copy.start()

    docs = lens_v.shape[0]
    wide = padded.shape[1]
    padded[...] = jnp.zeros_like(padded)
    local[2].wait()
    padded[0:1, 0:docs] = lens_v[...].reshape(1, docs)
    length = padded[...]
    high = length >> 8
    low = length - (high << 8)
    row8 = lax.broadcasted_iota(jnp.int32, (8, wide), 0)
    both = jnp.where(row8 == 1, pltpu.roll(low, 1, 0), high).astype(F32).astype(BF16)
    until = lax.broadcasted_iota(jnp.int32, (wide, wide), 0)
    upto = lax.broadcasted_iota(jnp.int32, (wide, wide), 1)
    lower = jnp.where(upto <= until, 1.0, 0.0).astype(BF16)
    sums = dot(lower, both, NT)
    base = chip * (GROUP * SPAN)
    ends = sums[:, 0:1] * 256.0 + sums[:, 1:2] - base.astype(F32)
    least = -base.astype(F32)
    key_row = lax.broadcasted_iota(jnp.int32, (SPAN, SPAN), 0).astype(F32)
    query_col = lax.broadcasted_iota(jnp.int32, (SPAN, SPAN), 1).astype(F32)
    for j in range(GROUP):
        pos = query_col[0:1] + float(j * SPAN)
        start = jnp.max(jnp.where(ends <= pos, ends, least), axis=0, keepdims=True)
        for b in range(GROUP + 1):
            key = b if b <= j else b - 1 - GROUP
            ok = key_row + float(key * SPAN) >= start
            if b == j:
                ok = ok & (key_row <= query_col)
            bias[j, b * SPAN : (b + 1) * SPAN] = jnp.where(ok, 0.0, -1e30)

    for copy in near[2:]:
        copy.start()

    local[3].wait()
    back = jnp.maximum(chip - 1, 0)
    here = [assign_s[s % 2, 2 * chip + s // 2] & (GROUP - 1) for s in range(GROUP)]
    there = [assign_s[s % 2, 2 * back + s // 2] & (GROUP - 1) for s in range(GROUP)]
    for copy in (local[0], local[1], local[4], local[5]):
        copy.wait()
    for copy in near:
        copy.wait_recv()
    for j in range(GROUP):
        slot = pick(here, j)
        rows = slice(j * SPAN, (j + 1) * SPAN)
        kb = kown[slot]
        vb = vown[slot]
        ko[rows] = kb
        vo[rows] = vb
        kot[:, rows] = kb.T
        vot[:, rows] = vb.T
        qb = qslot[slot]
        gb = gslot[slot]
        for h in range(heads):
            cols = slice(h * DIM, (h + 1) * DIM)
            qr[j, cols] = qb[:, cols]
            gr[j, cols] = gb[:, cols]
            qt[j, :, cols] = qb[:, cols].T
            gt[j, :, cols] = gb[:, cols].T

    scale = ROOT * math.log2(math.e)
    part_p[...] = jnp.zeros_like(part_p)
    part_o[...] = jnp.zeros_like(part_o)

    def scores(keys, j, first, n):
        s = dot(keys, qt[j], NN)
        top = None
        for at in range(0, n, PIECE):
            rows = slice(first + at, first + at + PIECE)
            piece = s[at : at + PIECE] * scale + every_head(bias[j, rows], heads)
            expo[j, rows] = piece
            top = fold(piece, jnp.max) if top is None else jnp.maximum(top, fold(piece, jnp.max))
        return jnp.max(top, axis=0, keepdims=True)

    def exponentials(j, first, n, top, low=None):
        total = None
        for at in range(0, n, PIECE):
            rows = slice(first + at, first + at + PIECE)
            e = jnp.exp2(expo[j, rows] - top)
            expo[j, rows] = e
            if low is not None:
                low[j, rows] = e.astype(BF16)
            total = fold(e, jnp.sum) if total is None else total + fold(e, jnp.sum)
        return jnp.sum(total, axis=0, keepdims=True)

    tops = []
    for j in range(GROUP):
        n = (j + 1) * SPAN
        tops.append(scores(ko[0:n], j, 0, n))
        dpo[j, 0:n] = dot(vo[0:n], gt[j], NN)
    for j in range(GROUP):
        n = (j + 1) * SPAN
        stat[j, 0:1] = tops[j]
        stat[j, 1:2] = exponentials(j, 0, n, tops[j], pb)
        oto[j] = dot(vot[:, 0:n], pb[j, 0:n], NN)

    @pl.when(has_prev)
    def _():
        for a in range(2):
            far_k[a].wait_recv()
            relay_k[a].start()
        for a in range(2):
            relay_k[a].wait_recv()

    @pl.when(jnp.logical_not(has_prev))
    def _():
        kprev[...] = jnp.zeros_like(kprev)
        vprev[...] = jnp.zeros_like(vprev)

    for i in range(GROUP):
        rows = slice(i * SPAN, (i + 1) * SPAN)
        kb = kprev[pick(there, i)]
        kp[rows] = kb
        kpt[:, rows] = kb.T

    tops = []
    for j in range(GROUP):
        top = scores(kp[j * SPAN :], j, (j + 1) * SPAN, (GROUP - j) * SPAN)
        tops.append(jnp.maximum(stat[j, 0:1], top))
    norms = []
    alphas = []
    for j in range(GROUP):
        total = exponentials(j, (j + 1) * SPAN, (GROUP - j) * SPAN, tops[j])
        shrink = jnp.exp2(stat[j, 0:1] - tops[j])
        r = 1.0 / (stat[j, 1:2] * shrink + total)
        norms.append(r)
        alphas.append(shrink * r)
        if j == 1:

            @pl.when(has_prev)
            def _():
                for a in range(2):
                    far_v[a].wait_recv()
                    relay_v[a].start()

    for j in range(GROUP):
        for at in range((j + 1) * SPAN, expo.shape[1], PIECE):
            rows = slice(at, at + PIECE)
            pr = expo[j, rows] * norms[j]
            expo[j, rows] = pr
            pb[j, rows] = pr.astype(BF16)

    @pl.when(has_prev)
    def _():
        for a in range(2):
            relay_v[a].wait_recv()

    for i in range(GROUP):
        rows = slice(i * SPAN, (i + 1) * SPAN)
        vb = vprev[pick(there, i)]
        vp[rows] = vb
        vpt[:, rows] = vb.T

    deltas = []

    def finish_out(j):
        out = oto[j] * alphas[j] + dot(vpt[:, j * SPAN :], pb[j, (j + 1) * SPAN :], NN)
        deltas.append(jnp.sum(out * gt[j].astype(F32), axis=0, keepdims=True))
        out = out.astype(BF16)
        for h in range(heads):
            cols = slice(h * DIM, (h + 1) * DIM)
            o_mine[j, :, cols] = out[:, cols].T

    def prev_dprobs(j):
        return dot(vp[j * SPAN :], gt[j], NN)

    def prev_grads(j, dp):
        at = (j + 1) * SPAN
        for p in range(0, dp.shape[0], PIECE):
            rows = slice(at + p, at + p + PIECE)
            sb[j, rows] = (expo[j, rows] * (dp[p : p + PIECE] - deltas[j])).astype(BF16)
        part_p[j:, :, 0:DIM] += spans(dot(sb[j, at:], qr[j], NN) * ROOT)
        part_p[j:, :, DIM:] += spans(dot(pb[j, at:], gr[j], NN))

    finish_out(0)
    dp = prev_dprobs(0)
    for j in range(1, GROUP):
        finish_out(j)
        next_dp = prev_dprobs(j)
        prev_grads(j - 1, dp)
        dp = next_dp
    prev_grads(GROUP - 1, dp)

    def mine_of(spans, a):
        return jnp.where(core == 0, spans[a], spans[2 + a])

    def theirs_of(spans, a):
        return jnp.where(core == 0, spans[2 + a], spans[a])

    swap_p = [remote(sum_send.at[a], sum_near.at[a], p_s.at[a], p_r.at[a], beside)
              for a in range(2)]
    far_p = [remote(far_send_buf.at[a], far_buf.at[a], f_s.at[a], f_r.at[a], before)
             for a in range(2)]
    for a in range(2):
        sum_send[a] = part_p[theirs_of(there, a)].astype(BF16)
        swap_p[a].start()

    swap_out = remote(o_send, o_near, oq_s.at[0], oq_r.at[0], beside)
    swap_dq = remote(q_send, q_near, oq_s.at[1], oq_r.at[1], beside)
    for a in range(2):
        o_send[a] = o_mine[theirs_of(here, a)]
    swap_out.start()

    def own_dscores(j):
        for at in range(0, (j + 1) * SPAN, PIECE):
            rows = slice(at, at + PIECE)
            pr = expo[j, rows] * alphas[j]
            pb[j, rows] = pr.astype(BF16)
            sb[j, rows] = (pr * (dpo[j, rows] - deltas[j])).astype(BF16)

    def query_grads(j):
        own = slice(0, (j + 1) * SPAN)
        at = (j + 1) * SPAN
        dqt = dot(kot[:, own], sb[j, own], NN) + dot(kpt[:, j * SPAN :], sb[j, at:], NN)
        dqt = (dqt * ROOT).astype(BF16)
        for h in range(heads):
            cols = slice(h * DIM, (h + 1) * DIM)
            q_mine[j, :, cols] = dqt[:, cols].T

    def own_grads(j):
        own = slice(0, (j + 1) * SPAN)
        part_o[0 : j + 1, :, 0:DIM] += spans(dot(sb[j, own], qr[j], NN) * ROOT)
        part_o[0 : j + 1, :, DIM:] += spans(dot(pb[j, own], gr[j], NN))

    own_dscores(0)
    for j in range(1, GROUP):
        own_dscores(j)
        query_grads(j - 1)
    query_grads(GROUP - 1)
    for a in range(2):
        q_send[a] = q_mine[theirs_of(here, a)]
    swap_dq.start()

    for a in range(2):
        swap_p[a].wait_recv()
        far_send_buf[a] = (
            part_p[mine_of(there, a)] + sum_near[a].astype(F32)).astype(BF16)

        @pl.when(has_prev)
        def _(a=a):
            far_p[a].start()

    for j in range(GROUP):
        own_grads(j)

    swap_o = [remote(own_send.at[a], own_near.at[a], o_s.at[a], o_r.at[a], beside)
              for a in range(2)]
    for a in range(2):
        own_send[a] = part_o[theirs_of(here, a)].astype(BF16)
        swap_o[a].start()

    for a in range(2):
        j = mine_of(here, a)
        attn[a, :, columns(core)] = o_mine[j]
        dq[a, :, columns(core)] = q_mine[j]
    swap_out.wait_recv()
    for a in range(2):
        attn[a, :, columns(other)] = o_near[a]
    swap_dq.wait_recv()
    for a in range(2):
        dq[a, :, columns(other)] = q_near[a]

    @pl.when(jnp.logical_not(has_next))
    def _():
        far_buf[...] = jnp.zeros_like(far_buf)

    for a in range(2):
        swap_o[a].wait_recv()

        @pl.when(has_next)
        def _(a=a):
            far_p[a].wait_recv()

        total = part_o[mine_of(here, a)] + own_near[a].astype(F32) + far_buf[a].astype(F32)
        dk[a] = total[:, 0:DIM].astype(BF16)
        dv[a] = total[:, DIM:].astype(BF16)

    for copy in near + swap_p + [swap_out, swap_dq] + swap_o:
        copy.wait_send()

    @pl.when(has_next)
    def _():
        for copy in far_k + far_v:
            copy.wait_send()

    @pl.when(has_prev)
    def _():
        for copy in relay_k + relay_v + far_p:
            copy.wait_send()


def store_kernel(*refs):
    n = (len(refs) - 1) // 2
    sem = refs[2 * n]
    copies = []
    for i in range(n):
        for a in range(2):
            copies.append(
                pltpu.make_async_copy(refs[i].at[a], refs[n + i].at[a], sem.at[len(copies)]))
    for copy in copies:
        copy.start()
    for copy in copies:
        copy.wait()


def shards(count, queries, keys, values, grad_out, lengths, assign):
    width = queries.shape[1]
    half = width // 2
    docs = lengths.shape[0]
    wide = -(-docs // 128) * 128
    hbm = pl.BlockSpec(memory_space=pltpu.HBM)
    vmem = pl.BlockSpec(memory_space=pltpu.VMEM)
    dma = pltpu.SemaphoreType.DMA
    shape = jax.ShapeDtypeStruct
    keyed = GROUP * SPAN
    seen = keyed + SPAN
    outs = (
        shape((2, SPAN, width), BF16),
        shape((2, SPAN, width), BF16),
        shape((2, SPAN, DIM), BF16),
        shape((2, SPAN, DIM), BF16),
    )
    results = pl.pallas_call(
        functools.partial(main_kernel, count),
        out_shape=outs,
        in_specs=[hbm] * 6,
        out_specs=(vmem,) * 4,
        scratch_shapes=[
            pltpu.VMEM((docs,), jnp.int32),
            pltpu.SMEM(assign.shape[::-1], jnp.int32),
            pltpu.VMEM((8, wide), jnp.int32),
            pltpu.VMEM((GROUP, SPAN, half), BF16),
            pltpu.VMEM((GROUP, SPAN, half), BF16),
            pltpu.VMEM((GROUP, SPAN, DIM), BF16),
            pltpu.VMEM((GROUP, SPAN, DIM), BF16),
            pltpu.VMEM((GROUP, SPAN, DIM), BF16),
            pltpu.VMEM((GROUP, SPAN, DIM), BF16),
            pltpu.VMEM((GROUP, half, DIM), BF16),
            pltpu.VMEM((GROUP, half, DIM), BF16),
            pltpu.VMEM((GROUP, DIM, half), BF16),
            pltpu.VMEM((GROUP, DIM, half), BF16),
            pltpu.VMEM((keyed, DIM), BF16),
            pltpu.VMEM((keyed, DIM), BF16),
            pltpu.VMEM((DIM, keyed), BF16),
            pltpu.VMEM((DIM, keyed), BF16),
            pltpu.VMEM((keyed, DIM), BF16),
            pltpu.VMEM((keyed, DIM), BF16),
            pltpu.VMEM((DIM, keyed), BF16),
            pltpu.VMEM((DIM, keyed), BF16),
            pltpu.VMEM((GROUP, seen, SPAN), F32),
            pltpu.VMEM((GROUP, seen, half), F32),
            pltpu.VMEM((GROUP, keyed, half), F32),
            pltpu.VMEM((GROUP, seen, half), BF16),
            pltpu.VMEM((GROUP, seen, half), BF16),
            pltpu.VMEM((GROUP, DIM, half), F32),
            pltpu.VMEM((GROUP, 8, half), F32),
            pltpu.VMEM((GROUP, SPAN, 2 * DIM), F32),
            pltpu.VMEM((GROUP, SPAN, 2 * DIM), F32),
            pltpu.VMEM((2, SPAN, 2 * DIM), BF16),
            pltpu.VMEM((2, SPAN, 2 * DIM), BF16),
            pltpu.VMEM((2, SPAN, 2 * DIM), BF16),
            pltpu.VMEM((2, SPAN, 2 * DIM), BF16),
            pltpu.VMEM((2, SPAN, 2 * DIM), BF16),
            pltpu.VMEM((2, SPAN, 2 * DIM), BF16),
            pltpu.VMEM((GROUP, SPAN, half), BF16),
            pltpu.VMEM((2, SPAN, half), BF16),
            pltpu.VMEM((2, SPAN, half), BF16),
            pltpu.VMEM((GROUP, SPAN, half), BF16),
            pltpu.VMEM((2, SPAN, half), BF16),
            pltpu.VMEM((2, SPAN, half), BF16),
            dma((6,)),
            dma((2,)), dma((2,)), dma((2,)), dma((2,)),
            dma((2,)), dma((2,)), dma((2,)), dma((2,)),
            dma((4,)), dma((4,)),
            dma((2,)), dma((2,)), dma((2,)), dma((2,)), dma((2,)), dma((2,)),
            dma((2,)), dma((2,)),
        ],
        compiler_params=pltpu.CompilerParams(
            collective_id=0, has_side_effects=True, vmem_limit_bytes=40 * 2**20),
        name="attend",
    )(*[
        pltpu.with_memory_space_constraint(x, pltpu.HBM)
        for x in (
            queries.reshape(2, SPAN, width), grad_out.reshape(2, SPAN, width),
            keys.reshape(2, SPAN, DIM), values.reshape(2, SPAN, DIM), lengths, assign.T,
        )
    ])
    results = pl.pallas_call(
        store_kernel,
        out_shape=outs,
        in_specs=[pl.BlockSpec(memory_space=pltpu.VMEM)] * 4,
        out_specs=(hbm,) * 4,
        scratch_shapes=[dma((8,))],
        name="store",
    )(*[pltpu.with_memory_space_constraint(r, pltpu.VMEM) for r in results])
    return tuple(r.reshape(2 * SPAN, r.shape[2]) for r in results)


def solution(mesh):
    split = P("seq", "grp")
    return jax.shard_map(
        functools.partial(shards, mesh.shape["seq"]),
        mesh=mesh,
        in_specs=(split, split, split, split, P(), P()),
        out_specs=(split, split, split, split),
        check_vma=False,
    )
```

```python
import functools
import math

import jax
import jax.numpy as jnp
from jax import lax
from jax.experimental import pallas as pl
from jax.experimental.pallas import tpu as pltpu
from jax.sharding import PartitionSpec as P

MESH = pl.DeviceIdType.MESH
SPAN = 128
DIM = 128
GROUP = 4
F32 = jnp.float32
BF16 = jnp.bfloat16
NT = (((1,), (1,)), ((), ()))
NN = (((1,), (0,)), ((), ()))
ROOT = 1.0 / math.sqrt(DIM)
PIECE = 32


def dot(a, b, dims):
    return lax.dot_general(a, b, dims, preferred_element_type=F32)


def pick(values, wanted):
    index = jnp.int32(0)
    for i, value in enumerate(values):
        index = jnp.where(value == wanted, i, index)
    return index


def every_head(x, heads):
    return jnp.concatenate([x] * heads, axis=1)


def spans(x):
    return x.reshape(x.shape[0] // SPAN, SPAN, x.shape[1])


def fold(x, reduce):
    return reduce(x.reshape(x.shape[0] // 8, 8, x.shape[1]), axis=0)


def main_kernel(
    count, q, g, k, v, lens, assign, attn, dq, dk, dv,
    lens_v, assign_s, padded, qslot, gslot, kown, vown, kprev, vprev, qr, gr, qt, gt,
    ko, vo, kot, vot, kp, vp, kpt, vpt, bias, expo, dpo, pb, sb, oto, stat,
    part_p, part_o, sum_send, sum_near, far_send_buf, far_buf, own_send, own_near,
    o_mine, o_send, o_near, q_mine, q_send, q_near,
    loc_sem, far_ks, far_kr, far_vs, far_vr, rel_ks, rel_kr, rel_vs, rel_vr,
    near_s, near_r, p_s, p_r, f_s, f_r, b_s, b_r, o_s, o_r, oq_s, oq_r,
):
    me = lax.axis_index("seq")
    grp = lax.axis_index("grp")
    core = lax.rem(me, 2)
    other = 1 - core
    chip = me // 2
    beside = me + 1 - 2 * core
    has_prev = chip > 0
    has_next = chip < count // 2 - 1
    before = jnp.where(has_prev, me - 2, me)
    after = jnp.where(has_next, me + 2, me)
    width = q.shape[2] // 2
    heads = width // DIM

    def remote(src, dst, send, recv, device):
        return pltpu.make_async_remote_copy(
            src_ref=src, dst_ref=dst, send_sem=send, recv_sem=recv,
            device_id=(device, grp), device_id_type=MESH,
        )

    def columns(which):
        return pl.ds(pl.multiple_of(which * width, width), width)

    own_slots = pl.ds(2 * core, 2)
    local = [
        pltpu.make_async_copy(k, kown.at[own_slots], loc_sem.at[0]),
        pltpu.make_async_copy(v, vown.at[own_slots], loc_sem.at[1]),
        pltpu.make_async_copy(lens, lens_v, loc_sem.at[2]),
        pltpu.make_async_copy(assign, assign_s, loc_sem.at[3]),
        pltpu.make_async_copy(q.at[:, :, columns(core)], qslot.at[own_slots], loc_sem.at[4]),
        pltpu.make_async_copy(g.at[:, :, columns(core)], gslot.at[own_slots], loc_sem.at[5]),
    ]
    far_k = [remote(k.at[a], kprev.at[2 * core + a], far_ks.at[a], far_kr.at[a], after)
             for a in range(2)]
    far_v = [remote(v.at[a], vprev.at[2 * core + a], far_vs.at[a], far_vr.at[a], after)
             for a in range(2)]
    relay_k = [remote(kprev.at[2 * core + a], kprev.at[2 * core + a], rel_ks.at[a], rel_kr.at[a],
                      beside) for a in range(2)]
    relay_v = [remote(vprev.at[2 * core + a], vprev.at[2 * core + a], rel_vs.at[a], rel_vr.at[a],
                      beside) for a in range(2)]
    near = [
        remote(k, kown.at[own_slots], near_s.at[0], near_r.at[0], beside),
        remote(v, vown.at[own_slots], near_s.at[1], near_r.at[1], beside),
        remote(q.at[:, :, columns(other)], qslot.at[own_slots], near_s.at[2], near_r.at[2], beside),
        remote(g.at[:, :, columns(other)], gslot.at[own_slots], near_s.at[3], near_r.at[3], beside),
    ]

    barrier = pltpu.get_barrier_semaphore()
    pl.semaphore_signal(barrier, inc=1, device_id=(beside, grp), device_id_type=MESH)

    @pl.when(has_prev)
    def _():
        pl.semaphore_signal(barrier, inc=1, device_id=(before, grp), device_id_type=MESH)

    @pl.when(has_next)
    def _():
        pl.semaphore_signal(barrier, inc=1, device_id=(after, grp), device_id_type=MESH)

    for copy in local:
        copy.start()
    pl.semaphore_wait(
        barrier, 1 + has_prev.astype(jnp.int32) + has_next.astype(jnp.int32))

    @pl.when(has_next)
    def _():
        for copy in far_k + far_v:
            copy.start()

    for copy in near[:2]:
        copy.start()

    docs = lens_v.shape[0]
    wide = padded.shape[1]
    padded[...] = jnp.zeros_like(padded)
    local[2].wait()
    padded[0:1, 0:docs] = lens_v[...].reshape(1, docs)
    length = padded[...]
    high = length >> 8
    low = length - (high << 8)
    row8 = lax.broadcasted_iota(jnp.int32, (8, wide), 0)
    both = jnp.where(row8 == 1, pltpu.roll(low, 1, 0), high).astype(F32).astype(BF16)
    until = lax.broadcasted_iota(jnp.int32, (wide, wide), 0)
    upto = lax.broadcasted_iota(jnp.int32, (wide, wide), 1)
    lower = jnp.where(upto <= until, 1.0, 0.0).astype(BF16)
    sums = dot(lower, both, NT)
    base = chip * (GROUP * SPAN)
    ends = sums[:, 0:1] * 256.0 + sums[:, 1:2] - base.astype(F32)
    least = -base.astype(F32)
    key_row = lax.broadcasted_iota(jnp.int32, (SPAN, SPAN), 0).astype(F32)
    query_col = lax.broadcasted_iota(jnp.int32, (SPAN, SPAN), 1).astype(F32)
    for j in range(GROUP):
        pos = query_col[0:1] + float(j * SPAN)
        start = jnp.max(jnp.where(ends <= pos, ends, least), axis=0, keepdims=True)
        for b in range(GROUP + 1):
            key = b if b <= j else b - 1 - GROUP
            ok = key_row + float(key * SPAN) >= start
            if b == j:
                ok = ok & (key_row <= query_col)
            bias[j, b * SPAN : (b + 1) * SPAN] = jnp.where(ok, 0.0, -1e30)

    for copy in near[2:]:
        copy.start()

    local[3].wait()
    back = jnp.maximum(chip - 1, 0)
    here = [assign_s[s % 2, 2 * chip + s // 2] & (GROUP - 1) for s in range(GROUP)]
    there = [assign_s[s % 2, 2 * back + s // 2] & (GROUP - 1) for s in range(GROUP)]
    for copy in (local[0], local[1], local[4], local[5]):
        copy.wait()
    for copy in near:
        copy.wait_recv()
    for j in range(GROUP):
        slot = pick(here, j)
        rows = slice(j * SPAN, (j + 1) * SPAN)
        kb = kown[slot]
        vb = vown[slot]
        ko[rows] = kb
        vo[rows] = vb
        kot[:, rows] = kb.T
        vot[:, rows] = vb.T
        qb = qslot[slot]
        gb = gslot[slot]
        for h in range(heads):
            cols = slice(h * DIM, (h + 1) * DIM)
            qr[j, cols] = qb[:, cols]
            gr[j, cols] = gb[:, cols]
            qt[j, :, cols] = qb[:, cols].T
            gt[j, :, cols] = gb[:, cols].T

    scale = ROOT * math.log2(math.e)
    part_p[...] = jnp.zeros_like(part_p)
    part_o[...] = jnp.zeros_like(part_o)

    def scores(keys, j, first, n):
        s = dot(keys, qt[j], NN)
        top = None
        for at in range(0, n, PIECE):
            rows = slice(first + at, first + at + PIECE)
            piece = s[at : at + PIECE] * scale + every_head(bias[j, rows], heads)
            expo[j, rows] = piece
            top = fold(piece, jnp.max) if top is None else jnp.maximum(top, fold(piece, jnp.max))
        return jnp.max(top, axis=0, keepdims=True)

    def exponentials(j, first, n, top, low=None):
        total = None
        for at in range(0, n, PIECE):
            rows = slice(first + at, first + at + PIECE)
            e = jnp.exp2(expo[j, rows] - top)
            expo[j, rows] = e
            if low is not None:
                low[j, rows] = e.astype(BF16)
            total = fold(e, jnp.sum) if total is None else total + fold(e, jnp.sum)
        return jnp.sum(total, axis=0, keepdims=True)

    tops = []
    for j in range(GROUP):
        n = (j + 1) * SPAN
        tops.append(scores(ko[0:n], j, 0, n))
        dpo[j, 0:n] = dot(vo[0:n], gt[j], NN)
    for j in range(GROUP):
        n = (j + 1) * SPAN
        stat[j, 0:1] = tops[j]
        stat[j, 1:2] = exponentials(j, 0, n, tops[j], pb)
        oto[j] = dot(vot[:, 0:n], pb[j, 0:n], NN)

    @pl.when(has_prev)
    def _():
        for a in range(2):
            far_k[a].wait_recv()
            relay_k[a].start()
        for a in range(2):
            relay_k[a].wait_recv()

    @pl.when(jnp.logical_not(has_prev))
    def _():
        kprev[...] = jnp.zeros_like(kprev)
        vprev[...] = jnp.zeros_like(vprev)

    for i in range(GROUP):
        rows = slice(i * SPAN, (i + 1) * SPAN)
        kb = kprev[pick(there, i)]
        kp[rows] = kb
        kpt[:, rows] = kb.T

    tops = []
    for j in range(GROUP):
        top = scores(kp[j * SPAN :], j, (j + 1) * SPAN, (GROUP - j) * SPAN)
        tops.append(jnp.maximum(stat[j, 0:1], top))
    norms = []
    alphas = []
    for j in range(GROUP):
        total = exponentials(j, (j + 1) * SPAN, (GROUP - j) * SPAN, tops[j])
        shrink = jnp.exp2(stat[j, 0:1] - tops[j])
        r = 1.0 / (stat[j, 1:2] * shrink + total)
        norms.append(r)
        alphas.append(shrink * r)
        if j == 1:

            @pl.when(has_prev)
            def _():
                for a in range(2):
                    far_v[a].wait_recv()
                    relay_v[a].start()

    for j in range(GROUP):
        for at in range((j + 1) * SPAN, expo.shape[1], PIECE):
            rows = slice(at, at + PIECE)
            pr = expo[j, rows] * norms[j]
            expo[j, rows] = pr
            pb[j, rows] = pr.astype(BF16)

    @pl.when(has_prev)
    def _():
        for a in range(2):
            relay_v[a].wait_recv()

    for i in range(GROUP):
        rows = slice(i * SPAN, (i + 1) * SPAN)
        vb = vprev[pick(there, i)]
        vp[rows] = vb
        vpt[:, rows] = vb.T

    deltas = []

    def finish_out(j):
        out = oto[j] * alphas[j] + dot(vpt[:, j * SPAN :], pb[j, (j + 1) * SPAN :], NN)
        deltas.append(jnp.sum(out * gt[j].astype(F32), axis=0, keepdims=True))
        out = out.astype(BF16)
        for h in range(heads):
            cols = slice(h * DIM, (h + 1) * DIM)
            o_mine[j, :, cols] = out[:, cols].T

    def prev_dprobs(j):
        return dot(vp[j * SPAN :], gt[j], NN)

    def prev_grads(j, dp):
        at = (j + 1) * SPAN
        for p in range(0, dp.shape[0], PIECE):
            rows = slice(at + p, at + p + PIECE)
            sb[j, rows] = (expo[j, rows] * (dp[p : p + PIECE] - deltas[j])).astype(BF16)
        part_p[j:, :, 0:DIM] += spans(dot(sb[j, at:], qr[j], NN) * ROOT)
        part_p[j:, :, DIM:] += spans(dot(pb[j, at:], gr[j], NN))

    def mine_of(spans, a):
        return jnp.where(core == 0, spans[a], spans[2 + a])

    def theirs_of(spans, a):
        return jnp.where(core == 0, spans[2 + a], spans[a])

    swap_out = remote(o_send, o_near, oq_s.at[0], oq_r.at[0], beside)
    swap_dq = remote(q_send, q_near, oq_s.at[1], oq_r.at[1], beside)
    swap_p = [remote(sum_send.at[r], sum_near.at[r], p_s.at[r], p_r.at[r], beside)
              for r in range(2)]
    far_p = [remote(far_send_buf.at[r], far_buf.at[2 * r + core], f_s.at[r], f_r.at[r], before)
             for r in range(2)]
    relay_p = [remote(far_buf.at[2 * r + core], far_buf.at[2 * r + core], b_s.at[r], b_r.at[r],
                      beside) for r in range(2)]

    def swap_round(r):
        sum_send[r] = part_p[2 * r + other].astype(BF16)
        swap_p[r].start()

    def far_round(r):
        swap_p[r].wait_recv()
        far_send_buf[r] = (part_p[2 * r + core] + sum_near[r].astype(F32)).astype(BF16)

        @pl.when(has_prev)
        def _():
            far_p[r].start()

    for j in range(GROUP):
        finish_out(j)
    for a in range(2):
        o_send[a] = o_mine[theirs_of(here, a)]
    swap_out.start()

    dp = prev_dprobs(0)
    for j in range(GROUP):
        next_dp = prev_dprobs(j + 1) if j < GROUP - 1 else None
        prev_grads(j, dp)
        dp = next_dp
        if j == 1:
            swap_round(0)
        if j == 2:
            far_round(0)
    swap_round(1)

    def own_dscores(j):
        for at in range(0, (j + 1) * SPAN, PIECE):
            rows = slice(at, at + PIECE)
            pr = expo[j, rows] * alphas[j]
            pb[j, rows] = pr.astype(BF16)
            sb[j, rows] = (pr * (dpo[j, rows] - deltas[j])).astype(BF16)

    def query_grads(j):
        own = slice(0, (j + 1) * SPAN)
        at = (j + 1) * SPAN
        dqt = dot(kot[:, own], sb[j, own], NN) + dot(kpt[:, j * SPAN :], sb[j, at:], NN)
        dqt = (dqt * ROOT).astype(BF16)
        for h in range(heads):
            cols = slice(h * DIM, (h + 1) * DIM)
            q_mine[j, :, cols] = dqt[:, cols].T

    def own_grads(j):
        own = slice(0, (j + 1) * SPAN)
        part_o[0 : j + 1, :, 0:DIM] += spans(dot(sb[j, own], qr[j], NN) * ROOT)
        part_o[0 : j + 1, :, DIM:] += spans(dot(pb[j, own], gr[j], NN))

    own_dscores(0)
    own_dscores(1)
    query_grads(0)
    far_round(1)
    own_dscores(2)
    query_grads(1)
    own_dscores(3)
    query_grads(2)
    query_grads(3)
    for a in range(2):
        q_send[a] = q_mine[theirs_of(here, a)]
    swap_dq.start()

    @pl.when(has_next)
    def _():
        for r in range(2):
            far_p[r].wait_recv()
            relay_p[r].start()

    for j in range(GROUP):
        own_grads(j)

    swap_o = [remote(own_send.at[a], own_near.at[a], o_s.at[a], o_r.at[a], beside)
              for a in range(2)]
    for a in range(2):
        own_send[a] = part_o[theirs_of(here, a)].astype(BF16)
        swap_o[a].start()

    for a in range(2):
        j = mine_of(here, a)
        attn[a, :, columns(core)] = o_mine[j]
        dq[a, :, columns(core)] = q_mine[j]
    swap_out.wait_recv()
    for a in range(2):
        attn[a, :, columns(other)] = o_near[a]
    swap_dq.wait_recv()
    for a in range(2):
        dq[a, :, columns(other)] = q_near[a]

    @pl.when(jnp.logical_not(has_next))
    def _():
        far_buf[...] = jnp.zeros_like(far_buf)

    @pl.when(has_next)
    def _():
        for r in range(2):
            relay_p[r].wait_recv()

    for a in range(2):
        swap_o[a].wait_recv()
        span = mine_of(here, a)
        total = part_o[span] + own_near[a].astype(F32) + far_buf[span].astype(F32)
        dk[a] = total[:, 0:DIM].astype(BF16)
        dv[a] = total[:, DIM:].astype(BF16)

    for copy in near + swap_p + [swap_out, swap_dq] + swap_o:
        copy.wait_send()

    @pl.when(has_next)
    def _():
        for copy in far_k + far_v + relay_p:
            copy.wait_send()

    @pl.when(has_prev)
    def _():
        for copy in relay_k + relay_v + far_p:
            copy.wait_send()


def store_kernel(*refs):
    n = (len(refs) - 1) // 2
    sem = refs[2 * n]
    copies = []
    for i in range(n):
        for a in range(2):
            copies.append(
                pltpu.make_async_copy(refs[i].at[a], refs[n + i].at[a], sem.at[len(copies)]))
    for copy in copies:
        copy.start()
    for copy in copies:
        copy.wait()


def shards(count, queries, keys, values, grad_out, lengths, assign):
    width = queries.shape[1]
    half = width // 2
    docs = lengths.shape[0]
    wide = -(-docs // 128) * 128
    hbm = pl.BlockSpec(memory_space=pltpu.HBM)
    vmem = pl.BlockSpec(memory_space=pltpu.VMEM)
    dma = pltpu.SemaphoreType.DMA
    shape = jax.ShapeDtypeStruct
    keyed = GROUP * SPAN
    seen = keyed + SPAN
    outs = (
        shape((2, SPAN, width), BF16),
        shape((2, SPAN, width), BF16),
        shape((2, SPAN, DIM), BF16),
        shape((2, SPAN, DIM), BF16),
    )
    results = pl.pallas_call(
        functools.partial(main_kernel, count),
        out_shape=outs,
        in_specs=[hbm] * 6,
        out_specs=(vmem,) * 4,
        scratch_shapes=[
            pltpu.VMEM((docs,), jnp.int32),
            pltpu.SMEM(assign.shape[::-1], jnp.int32),
            pltpu.VMEM((8, wide), jnp.int32),
            pltpu.VMEM((GROUP, SPAN, half), BF16),
            pltpu.VMEM((GROUP, SPAN, half), BF16),
            pltpu.VMEM((GROUP, SPAN, DIM), BF16),
            pltpu.VMEM((GROUP, SPAN, DIM), BF16),
            pltpu.VMEM((GROUP, SPAN, DIM), BF16),
            pltpu.VMEM((GROUP, SPAN, DIM), BF16),
            pltpu.VMEM((GROUP, half, DIM), BF16),
            pltpu.VMEM((GROUP, half, DIM), BF16),
            pltpu.VMEM((GROUP, DIM, half), BF16),
            pltpu.VMEM((GROUP, DIM, half), BF16),
            pltpu.VMEM((keyed, DIM), BF16),
            pltpu.VMEM((keyed, DIM), BF16),
            pltpu.VMEM((DIM, keyed), BF16),
            pltpu.VMEM((DIM, keyed), BF16),
            pltpu.VMEM((keyed, DIM), BF16),
            pltpu.VMEM((keyed, DIM), BF16),
            pltpu.VMEM((DIM, keyed), BF16),
            pltpu.VMEM((DIM, keyed), BF16),
            pltpu.VMEM((GROUP, seen, SPAN), F32),
            pltpu.VMEM((GROUP, seen, half), F32),
            pltpu.VMEM((GROUP, keyed, half), F32),
            pltpu.VMEM((GROUP, seen, half), BF16),
            pltpu.VMEM((GROUP, seen, half), BF16),
            pltpu.VMEM((GROUP, DIM, half), F32),
            pltpu.VMEM((GROUP, 8, half), F32),
            pltpu.VMEM((GROUP, SPAN, 2 * DIM), F32),
            pltpu.VMEM((GROUP, SPAN, 2 * DIM), F32),
            pltpu.VMEM((2, SPAN, 2 * DIM), BF16),
            pltpu.VMEM((2, SPAN, 2 * DIM), BF16),
            pltpu.VMEM((2, SPAN, 2 * DIM), BF16),
            pltpu.VMEM((GROUP, SPAN, 2 * DIM), BF16),
            pltpu.VMEM((2, SPAN, 2 * DIM), BF16),
            pltpu.VMEM((2, SPAN, 2 * DIM), BF16),
            pltpu.VMEM((GROUP, SPAN, half), BF16),
            pltpu.VMEM((2, SPAN, half), BF16),
            pltpu.VMEM((2, SPAN, half), BF16),
            pltpu.VMEM((GROUP, SPAN, half), BF16),
            pltpu.VMEM((2, SPAN, half), BF16),
            pltpu.VMEM((2, SPAN, half), BF16),
            dma((6,)),
            dma((2,)), dma((2,)), dma((2,)), dma((2,)),
            dma((2,)), dma((2,)), dma((2,)), dma((2,)),
            dma((4,)), dma((4,)),
            dma((2,)), dma((2,)), dma((2,)), dma((2,)), dma((2,)), dma((2,)),
            dma((2,)), dma((2,)), dma((2,)), dma((2,)),
        ],
        compiler_params=pltpu.CompilerParams(
            collective_id=0, has_side_effects=True, vmem_limit_bytes=40 * 2**20),
        name="attend",
    )(*[
        pltpu.with_memory_space_constraint(x, pltpu.HBM)
        for x in (
            queries.reshape(2, SPAN, width), grad_out.reshape(2, SPAN, width),
            keys.reshape(2, SPAN, DIM), values.reshape(2, SPAN, DIM), lengths, assign.T,
        )
    ])
    results = pl.pallas_call(
        store_kernel,
        out_shape=outs,
        in_specs=[pl.BlockSpec(memory_space=pltpu.VMEM)] * 4,
        out_specs=(hbm,) * 4,
        scratch_shapes=[dma((8,))],
        name="store",
    )(*[pltpu.with_memory_space_constraint(r, pltpu.VMEM) for r in results])
    return tuple(r.reshape(2 * SPAN, r.shape[2]) for r in results)


def solution(mesh):
    split = P("seq", "grp")
    return jax.shard_map(
        functools.partial(shards, mesh.shape["seq"]),
        mesh=mesh,
        in_specs=(split, split, split, split, P(), P()),
        out_specs=(split, split, split, split),
        check_vma=False,
    )
```

```python
import functools
import math

import jax
import jax.numpy as jnp
from jax import lax
from jax.experimental import pallas as pl
from jax.experimental.pallas import tpu as pltpu
from jax.sharding import PartitionSpec as P

MESH = pl.DeviceIdType.MESH
SPAN = 128
DIM = 128
GROUP = 4
F32 = jnp.float32
BF16 = jnp.bfloat16
NT = (((1,), (1,)), ((), ()))
NN = (((1,), (0,)), ((), ()))
TN = (((0,), (0,)), ((), ()))
ROOT = 1.0 / math.sqrt(DIM)
PIECE = 32


def dot(a, b, dims):
    return lax.dot_general(a, b, dims, preferred_element_type=F32)


def pick(values, wanted):
    index = jnp.int32(0)
    for i, value in enumerate(values):
        index = jnp.where(value == wanted, i, index)
    return index


def every_head(x, heads):
    return jnp.concatenate([x] * heads, axis=1)


def spans(x):
    return x.reshape(x.shape[0] // SPAN, SPAN, x.shape[1])


def fold(x, reduce):
    return reduce(x.reshape(x.shape[0] // 8, 8, x.shape[1]), axis=0)


def main_kernel(
    count, q, g, k, v, lens, assign, attn, dq, dk, dv,
    lens_v, assign_s, padded, qslot, gslot, kown, vown, kprev, vprev, qr, gr, qt, gt,
    ko, vo, kot, vot, kp, vp, kpt, vpt, bias, expo, dpo, pb, sb, oto, stat,
    part_p, part_o, sum_send, sum_near, far_send_buf, far_buf, own_send, own_near,
    o_mine, o_send, o_near, q_mine, q_send, q_near,
    loc_sem, far_ks, far_kr, far_vs, far_vr, rel_ks, rel_kr, rel_vs, rel_vr,
    near_s, near_r, p_s, p_r, f_s, f_r, o_s, o_r, oq_s, oq_r,
):
    me = lax.axis_index("seq")
    grp = lax.axis_index("grp")
    core = lax.rem(me, 2)
    other = 1 - core
    chip = me // 2
    beside = me + 1 - 2 * core
    has_prev = chip > 0
    has_next = chip < count // 2 - 1
    before = jnp.where(has_prev, me - 2, me)
    after = jnp.where(has_next, me + 2, me)
    width = q.shape[2] // 2
    heads = width // DIM

    def remote(src, dst, send, recv, device):
        return pltpu.make_async_remote_copy(
            src_ref=src, dst_ref=dst, send_sem=send, recv_sem=recv,
            device_id=(device, grp), device_id_type=MESH,
        )

    def columns(which):
        return pl.ds(pl.multiple_of(which * width, width), width)

    own_slots = pl.ds(2 * core, 2)
    local = [
        pltpu.make_async_copy(k, kown.at[own_slots], loc_sem.at[0]),
        pltpu.make_async_copy(v, vown.at[own_slots], loc_sem.at[1]),
        pltpu.make_async_copy(lens, lens_v, loc_sem.at[2]),
        pltpu.make_async_copy(assign, assign_s, loc_sem.at[3]),
        pltpu.make_async_copy(q.at[:, :, columns(core)], qslot.at[own_slots], loc_sem.at[4]),
        pltpu.make_async_copy(g.at[:, :, columns(core)], gslot.at[own_slots], loc_sem.at[5]),
    ]
    far_k = [remote(k.at[a], kprev.at[2 * core + a], far_ks.at[a], far_kr.at[a], after)
             for a in range(2)]
    far_v = [remote(v.at[a], vprev.at[2 * core + a], far_vs.at[a], far_vr.at[a], after)
             for a in range(2)]
    relay_k = [remote(kprev.at[2 * core + a], kprev.at[2 * core + a], rel_ks.at[a], rel_kr.at[a],
                      beside) for a in range(2)]
    relay_v = [remote(vprev.at[2 * core + a], vprev.at[2 * core + a], rel_vs.at[a], rel_vr.at[a],
                      beside) for a in range(2)]
    near = [
        remote(k, kown.at[own_slots], near_s.at[0], near_r.at[0], beside),
        remote(v, vown.at[own_slots], near_s.at[1], near_r.at[1], beside),
        remote(q.at[:, :, columns(other)], qslot.at[own_slots], near_s.at[2], near_r.at[2], beside),
        remote(g.at[:, :, columns(other)], gslot.at[own_slots], near_s.at[3], near_r.at[3], beside),
    ]

    barrier = pltpu.get_barrier_semaphore()
    pl.semaphore_signal(barrier, inc=1, device_id=(beside, grp), device_id_type=MESH)

    @pl.when(has_prev)
    def _():
        pl.semaphore_signal(barrier, inc=1, device_id=(before, grp), device_id_type=MESH)

    @pl.when(has_next)
    def _():
        pl.semaphore_signal(barrier, inc=1, device_id=(after, grp), device_id_type=MESH)

    for copy in local:
        copy.start()
    pl.semaphore_wait(
        barrier, 1 + has_prev.astype(jnp.int32) + has_next.astype(jnp.int32))

    @pl.when(has_next)
    def _():
        for copy in far_k + far_v:
            copy.start()

    for copy in near[:2]:
        copy.start()

    docs = lens_v.shape[0]
    wide = padded.shape[1]
    padded[...] = jnp.zeros_like(padded)
    local[2].wait()
    padded[0:1, 0:docs] = lens_v[...].reshape(1, docs)
    length = padded[...]
    high = length >> 8
    low = length - (high << 8)
    row8 = lax.broadcasted_iota(jnp.int32, (8, wide), 0)
    both = jnp.where(row8 == 1, pltpu.roll(low, 1, 0), high).astype(F32).astype(BF16)
    until = lax.broadcasted_iota(jnp.int32, (wide, wide), 0)
    upto = lax.broadcasted_iota(jnp.int32, (wide, wide), 1)
    lower = jnp.where(upto <= until, 1.0, 0.0).astype(BF16)
    sums = dot(lower, both, NT)
    base = chip * (GROUP * SPAN)
    ends = sums[:, 0:1] * 256.0 + sums[:, 1:2] - base.astype(F32)
    least = -base.astype(F32)
    key_row = lax.broadcasted_iota(jnp.int32, (SPAN, SPAN), 0).astype(F32)
    query_col = lax.broadcasted_iota(jnp.int32, (SPAN, SPAN), 1).astype(F32)
    for j in range(GROUP):
        pos = query_col[0:1] + float(j * SPAN)
        start = jnp.max(jnp.where(ends <= pos, ends, least), axis=0, keepdims=True)
        for b in range(GROUP + 1):
            key = b if b <= j else b - 1 - GROUP
            ok = key_row + float(key * SPAN) >= start
            if b == j:
                ok = ok & (key_row <= query_col)
            bias[j, b * SPAN : (b + 1) * SPAN] = jnp.where(ok, 0.0, -1e30)

    for copy in near[2:]:
        copy.start()

    local[3].wait()
    back = jnp.maximum(chip - 1, 0)
    here = [assign_s[s % 2, 2 * chip + s // 2] & (GROUP - 1) for s in range(GROUP)]
    there = [assign_s[s % 2, 2 * back + s // 2] & (GROUP - 1) for s in range(GROUP)]
    for copy in (local[0], local[1], local[4], local[5]):
        copy.wait()
    for copy in near:
        copy.wait_recv()
    for j in range(GROUP):
        slot = pick(here, j)
        rows = slice(j * SPAN, (j + 1) * SPAN)
        kb = kown[slot]
        vb = vown[slot]
        ko[rows] = kb
        vo[rows] = vb
        kot[:, rows] = kb.T
        vot[:, rows] = vb.T
        qb = qslot[slot]
        gb = gslot[slot]
        for h in range(heads):
            cols = slice(h * DIM, (h + 1) * DIM)
            qr[j, cols] = qb[:, cols]
            gr[j, cols] = gb[:, cols]
            qt[j, :, cols] = qb[:, cols].T
            gt[j, :, cols] = gb[:, cols].T

    scale = ROOT * math.log2(math.e)
    part_p[...] = jnp.zeros_like(part_p)
    part_o[...] = jnp.zeros_like(part_o)

    def scores(keys, j, first, n):
        s = dot(keys, qt[j], NN)
        top = None
        for at in range(0, n, PIECE):
            rows = slice(first + at, first + at + PIECE)
            piece = s[at : at + PIECE] * scale + every_head(bias[j, rows], heads)
            expo[j, rows] = piece
            top = fold(piece, jnp.max) if top is None else jnp.maximum(top, fold(piece, jnp.max))
        return jnp.max(top, axis=0, keepdims=True)

    def exponentials(j, first, n, top, low=None):
        total = None
        for at in range(0, n, PIECE):
            rows = slice(first + at, first + at + PIECE)
            e = jnp.exp2(expo[j, rows] - top)
            expo[j, rows] = e
            if low is not None:
                low[j, rows] = e.astype(BF16)
            total = fold(e, jnp.sum) if total is None else total + fold(e, jnp.sum)
        return jnp.sum(total, axis=0, keepdims=True)

    tops = []
    for j in range(GROUP):
        n = (j + 1) * SPAN
        tops.append(scores(ko[0:n], j, 0, n))
        dpo[j, 0:n] = dot(vo[0:n], gt[j], NN)
    for j in range(GROUP):
        n = (j + 1) * SPAN
        stat[j, 0:1] = tops[j]
        stat[j, 1:2] = exponentials(j, 0, n, tops[j], pb)
        oto[j] = dot(vot[:, 0:n], pb[j, 0:n], NN)

    @pl.when(has_prev)
    def _():
        for a in range(2):
            far_k[a].wait_recv()
            relay_k[a].start()
        for a in range(2):
            relay_k[a].wait_recv()

    @pl.when(jnp.logical_not(has_prev))
    def _():
        kprev[...] = jnp.zeros_like(kprev)
        vprev[...] = jnp.zeros_like(vprev)

    for i in range(GROUP):
        rows = slice(i * SPAN, (i + 1) * SPAN)
        kb = kprev[pick(there, i)]
        kp[rows] = kb
        kpt[:, rows] = kb.T

    tops = []
    for j in range(GROUP):
        top = scores(kp[j * SPAN :], j, (j + 1) * SPAN, (GROUP - j) * SPAN)
        tops.append(jnp.maximum(stat[j, 0:1], top))
    norms = []
    alphas = []
    for j in range(GROUP):
        total = exponentials(j, (j + 1) * SPAN, (GROUP - j) * SPAN, tops[j])
        shrink = jnp.exp2(stat[j, 0:1] - tops[j])
        r = 1.0 / (stat[j, 1:2] * shrink + total)
        norms.append(r)
        alphas.append(shrink * r)
        if j == 1:

            @pl.when(has_prev)
            def _():
                for a in range(2):
                    far_v[a].wait_recv()
                    relay_v[a].start()

    for j in range(GROUP):
        for at in range((j + 1) * SPAN, expo.shape[1], PIECE):
            rows = slice(at, at + PIECE)
            pr = expo[j, rows] * norms[j]
            expo[j, rows] = pr
            pb[j, rows] = pr.astype(BF16)

    @pl.when(has_prev)
    def _():
        for a in range(2):
            relay_v[a].wait_recv()

    for i in range(GROUP):
        rows = slice(i * SPAN, (i + 1) * SPAN)
        vb = vprev[pick(there, i)]
        vp[rows] = vb
        vpt[:, rows] = vb.T

    deltas = []

    def finish_out(j):
        out = oto[j] * alphas[j] + dot(vpt[:, j * SPAN :], pb[j, (j + 1) * SPAN :], NN)
        deltas.append(jnp.sum(out * gt[j].astype(F32), axis=0, keepdims=True))
        out = out.astype(BF16)
        for h in range(heads):
            cols = slice(h * DIM, (h + 1) * DIM)
            o_mine[j, :, cols] = out[:, cols].T

    def prev_dprobs(j):
        return dot(vp[j * SPAN :], gt[j], NN)

    def prev_grads(j, dp):
        at = (j + 1) * SPAN
        for p in range(0, dp.shape[0], PIECE):
            rows = slice(at + p, at + p + PIECE)
            sb[j, rows] = (expo[j, rows] * (dp[p : p + PIECE] - deltas[j])).astype(BF16)
        part_p[j:, :, 0:DIM] += spans(dot(sb[j, at:], qr[j], NN) * ROOT)
        part_p[j:, :, DIM:] += spans(dot(pb[j, at:], gr[j], NN))

    finish_out(0)
    dp = prev_dprobs(0)
    for j in range(1, GROUP):
        finish_out(j)
        next_dp = prev_dprobs(j)
        prev_grads(j - 1, dp)
        dp = next_dp
    prev_grads(GROUP - 1, dp)

    def mine_of(spans, a):
        return jnp.where(core == 0, spans[a], spans[2 + a])

    def theirs_of(spans, a):
        return jnp.where(core == 0, spans[2 + a], spans[a])

    swap_p = [remote(sum_send.at[a], sum_near.at[a], p_s.at[a], p_r.at[a], beside)
              for a in range(2)]
    far_p = [remote(far_send_buf.at[a], far_buf.at[a], f_s.at[a], f_r.at[a], before)
             for a in range(2)]
    for a in range(2):
        sum_send[a] = part_p[theirs_of(there, a)].astype(BF16)
        swap_p[a].start()

    swap_out = remote(o_send, o_near, oq_s.at[0], oq_r.at[0], beside)
    swap_dq = remote(q_send, q_near, oq_s.at[1], oq_r.at[1], beside)
    for a in range(2):
        o_send[a] = o_mine[theirs_of(here, a)]
    swap_out.start()

    def own_dscores(j):
        for at in range(0, (j + 1) * SPAN, PIECE):
            rows = slice(at, at + PIECE)
            pr = expo[j, rows] * alphas[j]
            pb[j, rows] = pr.astype(BF16)
            sb[j, rows] = (pr * (dpo[j, rows] - deltas[j])).astype(BF16)

    def query_grads(j):
        own = slice(0, (j + 1) * SPAN)
        at = (j + 1) * SPAN
        grad = dot(sb[j, own], ko[own], TN) + dot(sb[j, at:], kp[j * SPAN :], TN)
        grad = (grad * ROOT).astype(BF16)
        for h in range(heads):
            cols = slice(h * DIM, (h + 1) * DIM)
            q_mine[j, :, cols] = grad[cols]

    def own_grads(j):
        own = slice(0, (j + 1) * SPAN)
        part_o[0 : j + 1, :, 0:DIM] += spans(dot(sb[j, own], qr[j], NN) * ROOT)
        part_o[0 : j + 1, :, DIM:] += spans(dot(pb[j, own], gr[j], NN))

    own_dscores(0)
    for j in range(1, GROUP):
        own_dscores(j)
        query_grads(j - 1)
    query_grads(GROUP - 1)
    for a in range(2):
        q_send[a] = q_mine[theirs_of(here, a)]
    swap_dq.start()

    for a in range(2):
        swap_p[a].wait_recv()
        far_send_buf[a] = (
            part_p[mine_of(there, a)] + sum_near[a].astype(F32)).astype(BF16)

        @pl.when(has_prev)
        def _(a=a):
            far_p[a].start()

    for j in range(GROUP):
        own_grads(j)

    swap_o = [remote(own_send.at[a], own_near.at[a], o_s.at[a], o_r.at[a], beside)
              for a in range(2)]
    for a in range(2):
        own_send[a] = part_o[theirs_of(here, a)].astype(BF16)
        swap_o[a].start()

    for a in range(2):
        j = mine_of(here, a)
        attn[a, :, columns(core)] = o_mine[j]
        dq[a, :, columns(core)] = q_mine[j]
    swap_out.wait_recv()
    for a in range(2):
        attn[a, :, columns(other)] = o_near[a]
    swap_dq.wait_recv()
    for a in range(2):
        dq[a, :, columns(other)] = q_near[a]

    @pl.when(jnp.logical_not(has_next))
    def _():
        far_buf[...] = jnp.zeros_like(far_buf)

    for a in range(2):
        swap_o[a].wait_recv()

        @pl.when(has_next)
        def _(a=a):
            far_p[a].wait_recv()

        total = part_o[mine_of(here, a)] + own_near[a].astype(F32) + far_buf[a].astype(F32)
        dk[a] = total[:, 0:DIM].astype(BF16)
        dv[a] = total[:, DIM:].astype(BF16)

    for copy in near + swap_p + [swap_out, swap_dq] + swap_o:
        copy.wait_send()

    @pl.when(has_next)
    def _():
        for copy in far_k + far_v:
            copy.wait_send()

    @pl.when(has_prev)
    def _():
        for copy in relay_k + relay_v + far_p:
            copy.wait_send()


def store_kernel(*refs):
    n = (len(refs) - 1) // 2
    sem = refs[2 * n]
    copies = []
    for i in range(n):
        for a in range(2):
            copies.append(
                pltpu.make_async_copy(refs[i].at[a], refs[n + i].at[a], sem.at[len(copies)]))
    for copy in copies:
        copy.start()
    for copy in copies:
        copy.wait()


def shards(count, queries, keys, values, grad_out, lengths, assign):
    width = queries.shape[1]
    half = width // 2
    docs = lengths.shape[0]
    wide = -(-docs // 128) * 128
    hbm = pl.BlockSpec(memory_space=pltpu.HBM)
    vmem = pl.BlockSpec(memory_space=pltpu.VMEM)
    dma = pltpu.SemaphoreType.DMA
    shape = jax.ShapeDtypeStruct
    keyed = GROUP * SPAN
    seen = keyed + SPAN
    outs = (
        shape((2, SPAN, width), BF16),
        shape((2, SPAN, width), BF16),
        shape((2, SPAN, DIM), BF16),
        shape((2, SPAN, DIM), BF16),
    )
    results = pl.pallas_call(
        functools.partial(main_kernel, count),
        out_shape=outs,
        in_specs=[hbm] * 6,
        out_specs=(vmem,) * 4,
        scratch_shapes=[
            pltpu.VMEM((docs,), jnp.int32),
            pltpu.SMEM(assign.shape[::-1], jnp.int32),
            pltpu.VMEM((8, wide), jnp.int32),
            pltpu.VMEM((GROUP, SPAN, half), BF16),
            pltpu.VMEM((GROUP, SPAN, half), BF16),
            pltpu.VMEM((GROUP, SPAN, DIM), BF16),
            pltpu.VMEM((GROUP, SPAN, DIM), BF16),
            pltpu.VMEM((GROUP, SPAN, DIM), BF16),
            pltpu.VMEM((GROUP, SPAN, DIM), BF16),
            pltpu.VMEM((GROUP, half, DIM), BF16),
            pltpu.VMEM((GROUP, half, DIM), BF16),
            pltpu.VMEM((GROUP, DIM, half), BF16),
            pltpu.VMEM((GROUP, DIM, half), BF16),
            pltpu.VMEM((keyed, DIM), BF16),
            pltpu.VMEM((keyed, DIM), BF16),
            pltpu.VMEM((DIM, keyed), BF16),
            pltpu.VMEM((DIM, keyed), BF16),
            pltpu.VMEM((keyed, DIM), BF16),
            pltpu.VMEM((keyed, DIM), BF16),
            pltpu.VMEM((DIM, keyed), BF16),
            pltpu.VMEM((DIM, keyed), BF16),
            pltpu.VMEM((GROUP, seen, SPAN), F32),
            pltpu.VMEM((GROUP, seen, half), F32),
            pltpu.VMEM((GROUP, keyed, half), F32),
            pltpu.VMEM((GROUP, seen, half), BF16),
            pltpu.VMEM((GROUP, seen, half), BF16),
            pltpu.VMEM((GROUP, DIM, half), F32),
            pltpu.VMEM((GROUP, 8, half), F32),
            pltpu.VMEM((GROUP, SPAN, 2 * DIM), F32),
            pltpu.VMEM((GROUP, SPAN, 2 * DIM), F32),
            pltpu.VMEM((2, SPAN, 2 * DIM), BF16),
            pltpu.VMEM((2, SPAN, 2 * DIM), BF16),
            pltpu.VMEM((2, SPAN, 2 * DIM), BF16),
            pltpu.VMEM((2, SPAN, 2 * DIM), BF16),
            pltpu.VMEM((2, SPAN, 2 * DIM), BF16),
            pltpu.VMEM((2, SPAN, 2 * DIM), BF16),
            pltpu.VMEM((GROUP, SPAN, half), BF16),
            pltpu.VMEM((2, SPAN, half), BF16),
            pltpu.VMEM((2, SPAN, half), BF16),
            pltpu.VMEM((GROUP, SPAN, half), BF16),
            pltpu.VMEM((2, SPAN, half), BF16),
            pltpu.VMEM((2, SPAN, half), BF16),
            dma((6,)),
            dma((2,)), dma((2,)), dma((2,)), dma((2,)),
            dma((2,)), dma((2,)), dma((2,)), dma((2,)),
            dma((4,)), dma((4,)),
            dma((2,)), dma((2,)), dma((2,)), dma((2,)), dma((2,)), dma((2,)),
            dma((2,)), dma((2,)),
        ],
        compiler_params=pltpu.CompilerParams(
            collective_id=0, has_side_effects=True, vmem_limit_bytes=40 * 2**20),
        name="attend",
    )(*[
        pltpu.with_memory_space_constraint(x, pltpu.HBM)
        for x in (
            queries.reshape(2, SPAN, width), grad_out.reshape(2, SPAN, width),
            keys.reshape(2, SPAN, DIM), values.reshape(2, SPAN, DIM), lengths, assign.T,
        )
    ])
    results = pl.pallas_call(
        store_kernel,
        out_shape=outs,
        in_specs=[pl.BlockSpec(memory_space=pltpu.VMEM)] * 4,
        out_specs=(hbm,) * 4,
        scratch_shapes=[dma((8,))],
        name="store",
    )(*[pltpu.with_memory_space_constraint(r, pltpu.VMEM) for r in results])
    return tuple(r.reshape(2 * SPAN, r.shape[2]) for r in results)


def solution(mesh):
    split = P("seq", "grp")
    return jax.shard_map(
        functools.partial(shards, mesh.shape["seq"]),
        mesh=mesh,
        in_specs=(split, split, split, split, P(), P()),
        out_specs=(split, split, split, split),
        check_vma=False,
    )
```

```python
import functools
import math

import jax
import jax.numpy as jnp
from jax import lax
from jax.experimental import pallas as pl
from jax.experimental.pallas import tpu as pltpu
from jax.sharding import PartitionSpec as P

MESH = pl.DeviceIdType.MESH
SPAN = 128
DIM = 128
GROUP = 4
F32 = jnp.float32
BF16 = jnp.bfloat16
NT = (((1,), (1,)), ((), ()))
NN = (((1,), (0,)), ((), ()))
TN = (((0,), (0,)), ((), ()))
ROOT = 1.0 / math.sqrt(DIM)
PIECE = 32


def dot(a, b, dims):
    return lax.dot_general(a, b, dims, preferred_element_type=F32)


def pick(values, wanted):
    index = jnp.int32(0)
    for i, value in enumerate(values):
        index = jnp.where(value == wanted, i, index)
    return index


def every_head(x, heads):
    return jnp.concatenate([x] * heads, axis=1)


def spans(x):
    return x.reshape(x.shape[0] // SPAN, SPAN, x.shape[1])


def fold(x, reduce):
    return reduce(x.reshape(x.shape[0] // 8, 8, x.shape[1]), axis=0)


def main_kernel(
    count, q, g, k, v, lens, assign, attn, dq, dk, dv,
    lens_v, assign_s, padded, qslot, gslot, kown, vown, kprev, vprev, qr, gr, qt, gt,
    ko, vo, kot, vot, kp, vp, kpt, vpt, bias, expo, dpo, pb, sb, oto, stat,
    part_p, part_o, sum_send, sum_near, far_send_buf, far_buf, own_send, own_near,
    o_mine, o_send, o_near, q_mine, q_send, q_near,
    loc_sem, far_ks, far_kr, far_vs, far_vr, rel_ks, rel_kr, rel_vs, rel_vr,
    near_s, near_r, p_s, p_r, f_s, f_r, b_s, b_r, o_s, o_r, oq_s, oq_r,
):
    me = lax.axis_index("seq")
    grp = lax.axis_index("grp")
    core = lax.rem(me, 2)
    other = 1 - core
    chip = me // 2
    beside = me + 1 - 2 * core
    has_prev = chip > 0
    has_next = chip < count // 2 - 1
    before = jnp.where(has_prev, me - 2, me)
    after = jnp.where(has_next, me + 2, me)
    width = q.shape[2] // 2
    heads = width // DIM

    def remote(src, dst, send, recv, device):
        return pltpu.make_async_remote_copy(
            src_ref=src, dst_ref=dst, send_sem=send, recv_sem=recv,
            device_id=(device, grp), device_id_type=MESH,
        )

    def columns(which):
        return pl.ds(pl.multiple_of(which * width, width), width)

    own_slots = pl.ds(2 * core, 2)
    local = [
        pltpu.make_async_copy(k, kown.at[own_slots], loc_sem.at[0]),
        pltpu.make_async_copy(v, vown.at[own_slots], loc_sem.at[1]),
        pltpu.make_async_copy(lens, lens_v, loc_sem.at[2]),
        pltpu.make_async_copy(assign, assign_s, loc_sem.at[3]),
        pltpu.make_async_copy(q.at[:, :, columns(core)], qslot.at[own_slots], loc_sem.at[4]),
        pltpu.make_async_copy(g.at[:, :, columns(core)], gslot.at[own_slots], loc_sem.at[5]),
    ]
    far_k = [remote(k.at[a], kprev.at[2 * core + a], far_ks.at[a], far_kr.at[a], after)
             for a in range(2)]
    far_v = [remote(v.at[a], vprev.at[2 * core + a], far_vs.at[a], far_vr.at[a], after)
             for a in range(2)]
    relay_k = [remote(kprev.at[2 * core + a], kprev.at[2 * core + a], rel_ks.at[a], rel_kr.at[a],
                      beside) for a in range(2)]
    relay_v = [remote(vprev.at[2 * core + a], vprev.at[2 * core + a], rel_vs.at[a], rel_vr.at[a],
                      beside) for a in range(2)]
    near = [
        remote(k, kown.at[own_slots], near_s.at[0], near_r.at[0], beside),
        remote(v, vown.at[own_slots], near_s.at[1], near_r.at[1], beside),
        remote(q.at[:, :, columns(other)], qslot.at[own_slots], near_s.at[2], near_r.at[2], beside),
        remote(g.at[:, :, columns(other)], gslot.at[own_slots], near_s.at[3], near_r.at[3], beside),
    ]

    barrier = pltpu.get_barrier_semaphore()
    pl.semaphore_signal(barrier, inc=1, device_id=(beside, grp), device_id_type=MESH)

    @pl.when(has_prev)
    def _():
        pl.semaphore_signal(barrier, inc=1, device_id=(before, grp), device_id_type=MESH)

    @pl.when(has_next)
    def _():
        pl.semaphore_signal(barrier, inc=1, device_id=(after, grp), device_id_type=MESH)

    for copy in local:
        copy.start()
    pl.semaphore_wait(
        barrier, 1 + has_prev.astype(jnp.int32) + has_next.astype(jnp.int32))

    @pl.when(has_next)
    def _():
        for copy in far_k + far_v:
            copy.start()

    for copy in near[:2]:
        copy.start()

    docs = lens_v.shape[0]
    wide = padded.shape[1]
    padded[...] = jnp.zeros_like(padded)
    local[2].wait()
    padded[0:1, 0:docs] = lens_v[...].reshape(1, docs)
    length = padded[...]
    high = length >> 8
    low = length - (high << 8)
    row8 = lax.broadcasted_iota(jnp.int32, (8, wide), 0)
    both = jnp.where(row8 == 1, pltpu.roll(low, 1, 0), high).astype(F32).astype(BF16)
    until = lax.broadcasted_iota(jnp.int32, (wide, wide), 0)
    upto = lax.broadcasted_iota(jnp.int32, (wide, wide), 1)
    lower = jnp.where(upto <= until, 1.0, 0.0).astype(BF16)
    sums = dot(lower, both, NT)
    base = chip * (GROUP * SPAN)
    ends = sums[:, 0:1] * 256.0 + sums[:, 1:2] - base.astype(F32)
    least = -base.astype(F32)
    key_row = lax.broadcasted_iota(jnp.int32, (SPAN, SPAN), 0).astype(F32)
    query_col = lax.broadcasted_iota(jnp.int32, (SPAN, SPAN), 1).astype(F32)
    for j in range(GROUP):
        pos = query_col[0:1] + float(j * SPAN)
        start = jnp.max(jnp.where(ends <= pos, ends, least), axis=0, keepdims=True)
        for b in range(GROUP + 1):
            key = b if b <= j else b - 1 - GROUP
            ok = key_row + float(key * SPAN) >= start
            if b == j:
                ok = ok & (key_row <= query_col)
            bias[j, b * SPAN : (b + 1) * SPAN] = jnp.where(ok, 0.0, -1e30)

    for copy in near[2:]:
        copy.start()

    local[3].wait()
    back = jnp.maximum(chip - 1, 0)
    here = [assign_s[s % 2, 2 * chip + s // 2] & (GROUP - 1) for s in range(GROUP)]
    there = [assign_s[s % 2, 2 * back + s // 2] & (GROUP - 1) for s in range(GROUP)]
    for copy in (local[0], local[1], local[4], local[5]):
        copy.wait()
    for copy in near:
        copy.wait_recv()
    for j in range(GROUP):
        slot = pick(here, j)
        rows = slice(j * SPAN, (j + 1) * SPAN)
        kb = kown[slot]
        vb = vown[slot]
        ko[rows] = kb
        vo[rows] = vb
        kot[:, rows] = kb.T
        vot[:, rows] = vb.T
        qb = qslot[slot]
        gb = gslot[slot]
        for h in range(heads):
            cols = slice(h * DIM, (h + 1) * DIM)
            qr[j, cols] = qb[:, cols]
            gr[j, cols] = gb[:, cols]
            qt[j, :, cols] = qb[:, cols].T
            gt[j, :, cols] = gb[:, cols].T

    scale = ROOT * math.log2(math.e)
    part_p[...] = jnp.zeros_like(part_p)
    part_o[...] = jnp.zeros_like(part_o)

    def scores(keys, j, first, n):
        s = dot(keys, qt[j], NN)
        top = None
        for at in range(0, n, PIECE):
            rows = slice(first + at, first + at + PIECE)
            piece = s[at : at + PIECE] * scale + every_head(bias[j, rows], heads)
            expo[j, rows] = piece
            top = fold(piece, jnp.max) if top is None else jnp.maximum(top, fold(piece, jnp.max))
        return jnp.max(top, axis=0, keepdims=True)

    def exponentials(j, first, n, top):
        total = jnp.zeros((8, width), F32)
        for at in range(0, n, PIECE):
            rows = slice(first + at, first + at + PIECE)
            e = jnp.exp2(expo[j, rows] - top)
            expo[j, rows] = e
            total = total + fold(e, jnp.sum)
        return jnp.sum(total, axis=0, keepdims=True)

    def weighted(j, first, dp):
        total = jnp.zeros((8, width), F32)
        for at in range(0, dp.shape[0], PIECE):
            rows = slice(first + at, first + at + PIECE)
            total = total + fold(expo[j, rows] * dp[at : at + PIECE], jnp.sum)
        return jnp.sum(total, axis=0, keepdims=True)

    tops = []
    for j in range(GROUP):
        n = (j + 1) * SPAN
        tops.append(scores(ko[0:n], j, 0, n))
        dpo[j, 0:n] = dot(vo[0:n], gt[j], NN)
    for j in range(GROUP):
        n = (j + 1) * SPAN
        stat[j, 0:1] = tops[j]
        stat[j, 1:2] = exponentials(j, 0, n, tops[j])
        stat[j, 2:3] = weighted(j, 0, dpo[j, 0:n])
        oto[j] = dot(vot[:, 0:n], expo[j, 0:n].astype(BF16), NN)

    @pl.when(has_prev)
    def _():
        for a in range(2):
            far_k[a].wait_recv()
            relay_k[a].start()
        for a in range(2):
            relay_k[a].wait_recv()

    @pl.when(jnp.logical_not(has_prev))
    def _():
        kprev[...] = jnp.zeros_like(kprev)
        vprev[...] = jnp.zeros_like(vprev)

    for i in range(GROUP):
        rows = slice(i * SPAN, (i + 1) * SPAN)
        kb = kprev[pick(there, i)]
        kp[rows] = kb
        kpt[:, rows] = kb.T

    tops = []
    for j in range(GROUP):
        top = scores(kp[j * SPAN :], j, (j + 1) * SPAN, (GROUP - j) * SPAN)
        tops.append(jnp.maximum(stat[j, 0:1], top))
    norms = []
    alphas = []
    for j in range(GROUP):
        total = exponentials(j, (j + 1) * SPAN, (GROUP - j) * SPAN, tops[j])
        shrink = jnp.exp2(stat[j, 0:1] - tops[j])
        r = 1.0 / (stat[j, 1:2] * shrink + total)
        norms.append(r)
        alphas.append(shrink * r)
        if j == 1:

            @pl.when(has_prev)
            def _():
                for a in range(2):
                    far_v[a].wait_recv()
                    relay_v[a].start()

    @pl.when(has_prev)
    def _():
        for a in range(2):
            relay_v[a].wait_recv()

    for i in range(GROUP):
        rows = slice(i * SPAN, (i + 1) * SPAN)
        vb = vprev[pick(there, i)]
        vp[rows] = vb
        vpt[:, rows] = vb.T

    def mine_of(spans, a):
        return jnp.where(core == 0, spans[a], spans[2 + a])

    def theirs_of(spans, a):
        return jnp.where(core == 0, spans[2 + a], spans[a])

    my_pair = pl.ds(2 * core, 2)
    swap_p = remote(sum_send, sum_near, p_s.at[0], p_r.at[0], beside)
    far_p = remote(far_send_buf, far_buf.at[my_pair], f_s.at[0], f_r.at[0], before)
    relay_p = remote(far_buf.at[my_pair], far_buf.at[my_pair], b_s.at[0], b_r.at[0], beside)

    def give(pair):
        sum_send[...] = part_p[2 * pair : 2 * pair + 2].astype(BF16)
        swap_p.start()

    def send_back(pair):
        swap_p.wait_recv()
        for i in range(2):
            far_send_buf[i] = (part_p[2 * pair + i] + sum_near[i].astype(F32)).astype(BF16)

        @pl.when(has_prev)
        def _():
            far_p.start()

    deltas = []

    def prev_grads(j, dp):
        at = (j + 1) * SPAN
        delta = alphas[j] * stat[j, 2:3] + norms[j] * weighted(j, at, dp)
        deltas.append(delta)
        for p in range(0, dp.shape[0], PIECE):
            rows = slice(at + p, at + p + PIECE)
            pr = expo[j, rows] * norms[j]
            pb[j, rows] = pr.astype(BF16)
            sb[j, rows] = (pr * (dp[p : p + PIECE] - delta)).astype(BF16)
        part_p[j:, :, 0:DIM] += spans(dot(sb[j, at:], qr[j], NN) * ROOT)
        part_p[j:, :, DIM:] += spans(dot(pb[j, at:], gr[j], NN))

    dp = dot(vp[...], gt[0], NN)
    for j in range(GROUP):
        next_dp = dot(vp[(j + 1) * SPAN :], gt[j + 1], NN) if j < GROUP - 1 else None
        prev_grads(j, dp)
        dp = next_dp
        if j == 1:

            @pl.when(core == 1)
            def _():
                give(0)

    @pl.when(core == 0)
    def _():
        give(1)
        send_back(0)

    swap_out = remote(o_send, o_near, oq_s.at[0], oq_r.at[0], beside)
    swap_dq = remote(q_send, q_near, oq_s.at[1], oq_r.at[1], beside)
    for j in range(GROUP):
        out = oto[j] * alphas[j] + dot(vpt[:, j * SPAN :], pb[j, (j + 1) * SPAN :], NN)
        out = out.astype(BF16)
        for h in range(heads):
            cols = slice(h * DIM, (h + 1) * DIM)
            o_mine[j, :, cols] = out[:, cols].T
    for a in range(2):
        o_send[a] = o_mine[theirs_of(here, a)]
    swap_out.start()

    @pl.when(core == 1)
    def _():
        send_back(1)

    def own_dscores(j):
        for at in range(0, (j + 1) * SPAN, PIECE):
            rows = slice(at, at + PIECE)
            pr = expo[j, rows] * alphas[j]
            pb[j, rows] = pr.astype(BF16)
            sb[j, rows] = (pr * (dpo[j, rows] - deltas[j])).astype(BF16)

    def query_grads(j):
        own = slice(0, (j + 1) * SPAN)
        at = (j + 1) * SPAN
        grad = dot(sb[j, own], ko[own], TN) + dot(sb[j, at:], kp[j * SPAN :], TN)
        grad = (grad * ROOT).astype(BF16)
        for h in range(heads):
            cols = slice(h * DIM, (h + 1) * DIM)
            q_mine[j, :, cols] = grad[cols]

    def own_grads(j):
        own = slice(0, (j + 1) * SPAN)
        part_o[0 : j + 1, :, 0:DIM] += spans(dot(sb[j, own], qr[j], NN) * ROOT)
        part_o[0 : j + 1, :, DIM:] += spans(dot(pb[j, own], gr[j], NN))

    own_dscores(0)
    for j in range(1, GROUP):
        own_dscores(j)
        query_grads(j - 1)
    query_grads(GROUP - 1)
    for a in range(2):
        q_send[a] = q_mine[theirs_of(here, a)]
    swap_dq.start()

    @pl.when(has_next)
    def _():
        far_p.wait_recv()
        relay_p.start()

    for j in range(GROUP):
        own_grads(j)

    swap_o = [remote(own_send.at[a], own_near.at[a], o_s.at[a], o_r.at[a], beside)
              for a in range(2)]
    for a in range(2):
        own_send[a] = part_o[theirs_of(here, a)].astype(BF16)
        swap_o[a].start()

    for a in range(2):
        j = mine_of(here, a)
        attn[a, :, columns(core)] = o_mine[j]
        dq[a, :, columns(core)] = q_mine[j]
    swap_out.wait_recv()
    for a in range(2):
        attn[a, :, columns(other)] = o_near[a]
    swap_dq.wait_recv()
    for a in range(2):
        dq[a, :, columns(other)] = q_near[a]

    @pl.when(jnp.logical_not(has_next))
    def _():
        far_buf[...] = jnp.zeros_like(far_buf)

    @pl.when(has_next)
    def _():
        relay_p.wait_recv()

    for a in range(2):
        swap_o[a].wait_recv()
        span = mine_of(here, a)
        total = part_o[span] + own_near[a].astype(F32) + far_buf[span].astype(F32)
        dk[a] = total[:, 0:DIM].astype(BF16)
        dv[a] = total[:, DIM:].astype(BF16)

    for copy in near + [swap_p, swap_out, swap_dq] + swap_o:
        copy.wait_send()

    @pl.when(has_next)
    def _():
        for copy in far_k + far_v + [relay_p]:
            copy.wait_send()

    @pl.when(has_prev)
    def _():
        for copy in relay_k + relay_v + [far_p]:
            copy.wait_send()


def store_kernel(*refs):
    n = (len(refs) - 1) // 2
    sem = refs[2 * n]
    copies = []
    for i in range(n):
        for a in range(2):
            copies.append(
                pltpu.make_async_copy(refs[i].at[a], refs[n + i].at[a], sem.at[len(copies)]))
    for copy in copies:
        copy.start()
    for copy in copies:
        copy.wait()


def shards(count, queries, keys, values, grad_out, lengths, assign):
    width = queries.shape[1]
    half = width // 2
    docs = lengths.shape[0]
    wide = -(-docs // 128) * 128
    hbm = pl.BlockSpec(memory_space=pltpu.HBM)
    vmem = pl.BlockSpec(memory_space=pltpu.VMEM)
    dma = pltpu.SemaphoreType.DMA
    shape = jax.ShapeDtypeStruct
    keyed = GROUP * SPAN
    seen = keyed + SPAN
    outs = (
        shape((2, SPAN, width), BF16),
        shape((2, SPAN, width), BF16),
        shape((2, SPAN, DIM), BF16),
        shape((2, SPAN, DIM), BF16),
    )
    results = pl.pallas_call(
        functools.partial(main_kernel, count),
        out_shape=outs,
        in_specs=[hbm] * 6,
        out_specs=(vmem,) * 4,
        scratch_shapes=[
            pltpu.VMEM((docs,), jnp.int32),
            pltpu.SMEM(assign.shape[::-1], jnp.int32),
            pltpu.VMEM((8, wide), jnp.int32),
            pltpu.VMEM((GROUP, SPAN, half), BF16),
            pltpu.VMEM((GROUP, SPAN, half), BF16),
            pltpu.VMEM((GROUP, SPAN, DIM), BF16),
            pltpu.VMEM((GROUP, SPAN, DIM), BF16),
            pltpu.VMEM((GROUP, SPAN, DIM), BF16),
            pltpu.VMEM((GROUP, SPAN, DIM), BF16),
            pltpu.VMEM((GROUP, half, DIM), BF16),
            pltpu.VMEM((GROUP, half, DIM), BF16),
            pltpu.VMEM((GROUP, DIM, half), BF16),
            pltpu.VMEM((GROUP, DIM, half), BF16),
            pltpu.VMEM((keyed, DIM), BF16),
            pltpu.VMEM((keyed, DIM), BF16),
            pltpu.VMEM((DIM, keyed), BF16),
            pltpu.VMEM((DIM, keyed), BF16),
            pltpu.VMEM((keyed, DIM), BF16),
            pltpu.VMEM((keyed, DIM), BF16),
            pltpu.VMEM((DIM, keyed), BF16),
            pltpu.VMEM((DIM, keyed), BF16),
            pltpu.VMEM((GROUP, seen, SPAN), F32),
            pltpu.VMEM((GROUP, seen, half), F32),
            pltpu.VMEM((GROUP, keyed, half), F32),
            pltpu.VMEM((GROUP, seen, half), BF16),
            pltpu.VMEM((GROUP, seen, half), BF16),
            pltpu.VMEM((GROUP, DIM, half), F32),
            pltpu.VMEM((GROUP, 8, half), F32),
            pltpu.VMEM((GROUP, SPAN, 2 * DIM), F32),
            pltpu.VMEM((GROUP, SPAN, 2 * DIM), F32),
            pltpu.VMEM((2, SPAN, 2 * DIM), BF16),
            pltpu.VMEM((2, SPAN, 2 * DIM), BF16),
            pltpu.VMEM((2, SPAN, 2 * DIM), BF16),
            pltpu.VMEM((GROUP, SPAN, 2 * DIM), BF16),
            pltpu.VMEM((2, SPAN, 2 * DIM), BF16),
            pltpu.VMEM((2, SPAN, 2 * DIM), BF16),
            pltpu.VMEM((GROUP, SPAN, half), BF16),
            pltpu.VMEM((2, SPAN, half), BF16),
            pltpu.VMEM((2, SPAN, half), BF16),
            pltpu.VMEM((GROUP, SPAN, half), BF16),
            pltpu.VMEM((2, SPAN, half), BF16),
            pltpu.VMEM((2, SPAN, half), BF16),
            dma((6,)),
            dma((2,)), dma((2,)), dma((2,)), dma((2,)),
            dma((2,)), dma((2,)), dma((2,)), dma((2,)),
            dma((4,)), dma((4,)),
            dma((1,)), dma((1,)), dma((1,)), dma((1,)), dma((1,)), dma((1,)),
            dma((2,)), dma((2,)), dma((2,)), dma((2,)),
        ],
        compiler_params=pltpu.CompilerParams(
            collective_id=0, has_side_effects=True, vmem_limit_bytes=40 * 2**20),
        name="attend",
    )(*[
        pltpu.with_memory_space_constraint(x, pltpu.HBM)
        for x in (
            queries.reshape(2, SPAN, width), grad_out.reshape(2, SPAN, width),
            keys.reshape(2, SPAN, DIM), values.reshape(2, SPAN, DIM), lengths, assign.T,
        )
    ])
    results = pl.pallas_call(
        store_kernel,
        out_shape=outs,
        in_specs=[pl.BlockSpec(memory_space=pltpu.VMEM)] * 4,
        out_specs=(hbm,) * 4,
        scratch_shapes=[dma((8,))],
        name="store",
    )(*[pltpu.with_memory_space_constraint(r, pltpu.VMEM) for r in results])
    return tuple(r.reshape(2 * SPAN, r.shape[2]) for r in results)


def solution(mesh):
    split = P("seq", "grp")
    return jax.shard_map(
        functools.partial(shards, mesh.shape["seq"]),
        mesh=mesh,
        in_specs=(split, split, split, split, P(), P()),
        out_specs=(split, split, split, split),
        check_vma=False,
    )
```

```python
import functools
import math

import jax
import jax.numpy as jnp
from jax import lax
from jax.experimental import pallas as pl
from jax.experimental.pallas import tpu as pltpu
from jax.sharding import PartitionSpec as P

MESH = pl.DeviceIdType.MESH
SPAN = 128
DIM = 128
GROUP = 4
F32 = jnp.float32
BF16 = jnp.bfloat16
NT = (((1,), (1,)), ((), ()))
NN = (((1,), (0,)), ((), ()))
TN = (((0,), (0,)), ((), ()))
ROOT = 1.0 / math.sqrt(DIM)
FAR = 64
BACK = 32
PIECE = 32


def dot(a, b, dims):
    return lax.dot_general(a, b, dims, preferred_element_type=F32)


def pick(values, wanted):
    index = jnp.int32(0)
    for i, value in enumerate(values):
        index = jnp.where(value == wanted, i, index)
    return index


def every_head(x, heads):
    return jnp.concatenate([x] * heads, axis=1)


def spans(x):
    return x.reshape(x.shape[0] // SPAN, SPAN, x.shape[1])


def fold(x, reduce):
    return reduce(x.reshape(x.shape[0] // 8, 8, x.shape[1]), axis=0)


def main_kernel(
    count, q, g, k, v, lens, assign, attn, dq, dk, dv,
    lens_v, assign_s, padded, qslot, gslot, kown, vown, kprev, vprev, qr, gr, qt, gt,
    ko, vo, kot, vot, kp, vp, kpt, vpt, bias, expo, dpo, pb, sb, oto, stat,
    part_p, part_o, sum_send, sum_near, far_send_buf, far_buf, own_send, own_near,
    o_mine, o_send, o_near, q_mine, q_send, q_near,
    loc_sem, far_ks, far_kr, far_vs, far_vr, rel_ks, rel_kr, rel_vs, rel_vr,
    near_s, near_r, p_s, p_r, f_s, f_r, o_s, o_r, oq_s, oq_r,
):
    me = lax.axis_index("seq")
    grp = lax.axis_index("grp")
    core = lax.rem(me, 2)
    other = 1 - core
    chip = me // 2
    beside = me + 1 - 2 * core
    has_prev = chip > 0
    has_next = chip < count // 2 - 1
    before = jnp.where(has_prev, me - 2, me)
    after = jnp.where(has_next, me + 2, me)
    width = q.shape[2] // 2
    heads = width // DIM

    def remote(src, dst, send, recv, device):
        return pltpu.make_async_remote_copy(
            src_ref=src, dst_ref=dst, send_sem=send, recv_sem=recv,
            device_id=(device, grp), device_id_type=MESH,
        )

    def columns(which):
        return pl.ds(pl.multiple_of(which * width, width), width)

    own_slots = pl.ds(2 * core, 2)
    local = [
        pltpu.make_async_copy(k, kown.at[own_slots], loc_sem.at[0]),
        pltpu.make_async_copy(v, vown.at[own_slots], loc_sem.at[1]),
        pltpu.make_async_copy(lens, lens_v, loc_sem.at[2]),
        pltpu.make_async_copy(assign, assign_s, loc_sem.at[3]),
        pltpu.make_async_copy(q.at[:, :, columns(core)], qslot.at[own_slots], loc_sem.at[4]),
        pltpu.make_async_copy(g.at[:, :, columns(core)], gslot.at[own_slots], loc_sem.at[5]),
    ]
    def pieces(ref, span):
        return [ref.at[span, pl.ds(at, FAR)] for at in range(0, SPAN, FAR)]

    def far_copies(src, dst, send, recv):
        ends = [(x, y) for a in range(2) for x, y in zip(pieces(src, a), pieces(dst, 2 * core + a))]
        return [remote(x, y, send.at[i], recv.at[i], after) for i, (x, y) in enumerate(ends)]

    def relay_copies(dst, send, recv):
        ends = [x for a in range(2) for x in pieces(dst, 2 * core + a)]
        return [remote(x, x, send.at[i], recv.at[i], beside) for i, x in enumerate(ends)]

    far_k = far_copies(k, kprev, far_ks, far_kr)
    far_v = far_copies(v, vprev, far_vs, far_vr)
    relay_k = relay_copies(kprev, rel_ks, rel_kr)
    relay_v = relay_copies(vprev, rel_vs, rel_vr)
    near = [
        remote(k, kown.at[own_slots], near_s.at[0], near_r.at[0], beside),
        remote(v, vown.at[own_slots], near_s.at[1], near_r.at[1], beside),
        remote(q.at[:, :, columns(other)], qslot.at[own_slots], near_s.at[2], near_r.at[2], beside),
        remote(g.at[:, :, columns(other)], gslot.at[own_slots], near_s.at[3], near_r.at[3], beside),
    ]

    barrier = pltpu.get_barrier_semaphore()
    pl.semaphore_signal(barrier, inc=1, device_id=(beside, grp), device_id_type=MESH)

    @pl.when(has_prev)
    def _():
        pl.semaphore_signal(barrier, inc=1, device_id=(before, grp), device_id_type=MESH)

    @pl.when(has_next)
    def _():
        pl.semaphore_signal(barrier, inc=1, device_id=(after, grp), device_id_type=MESH)

    for copy in local:
        copy.start()
    pl.semaphore_wait(
        barrier, 1 + has_prev.astype(jnp.int32) + has_next.astype(jnp.int32))

    @pl.when(has_next)
    def _():
        for copy in far_k + far_v:
            copy.start()

    for copy in near[:2]:
        copy.start()

    docs = lens_v.shape[0]
    wide = padded.shape[1]
    padded[...] = jnp.zeros_like(padded)
    local[2].wait()
    padded[0:1, 0:docs] = lens_v[...].reshape(1, docs)
    length = padded[...]
    high = length >> 8
    low = length - (high << 8)
    row8 = lax.broadcasted_iota(jnp.int32, (8, wide), 0)
    both = jnp.where(row8 == 1, pltpu.roll(low, 1, 0), high).astype(F32).astype(BF16)
    until = lax.broadcasted_iota(jnp.int32, (wide, wide), 0)
    upto = lax.broadcasted_iota(jnp.int32, (wide, wide), 1)
    lower = jnp.where(upto <= until, 1.0, 0.0).astype(BF16)
    sums = dot(lower, both, NT)
    base = chip * (GROUP * SPAN)
    ends = sums[:, 0:1] * 256.0 + sums[:, 1:2] - base.astype(F32)
    least = -base.astype(F32)
    key_row = lax.broadcasted_iota(jnp.int32, (SPAN, SPAN), 0).astype(F32)
    query_col = lax.broadcasted_iota(jnp.int32, (SPAN, SPAN), 1).astype(F32)
    for j in range(GROUP):
        pos = query_col[0:1] + float(j * SPAN)
        start = jnp.max(jnp.where(ends <= pos, ends, least), axis=0, keepdims=True)
        for b in range(GROUP + 1):
            key = b if b <= j else b - 1 - GROUP
            ok = key_row + float(key * SPAN) >= start
            if b == j:
                ok = ok & (key_row <= query_col)
            bias[j, b * SPAN : (b + 1) * SPAN] = jnp.where(ok, 0.0, -1e30)

    for copy in near[2:]:
        copy.start()

    local[3].wait()
    back = jnp.maximum(chip - 1, 0)
    here = [assign_s[s % 2, 2 * chip + s // 2] & (GROUP - 1) for s in range(GROUP)]
    there = [assign_s[s % 2, 2 * back + s // 2] & (GROUP - 1) for s in range(GROUP)]
    for copy in (local[0], local[1], local[4], local[5]):
        copy.wait()
    for copy in near:
        copy.wait_recv()
    for j in range(GROUP):
        slot = pick(here, j)
        rows = slice(j * SPAN, (j + 1) * SPAN)
        kb = kown[slot]
        vb = vown[slot]
        ko[rows] = kb
        vo[rows] = vb
        kot[:, rows] = kb.T
        vot[:, rows] = vb.T
        qb = qslot[slot]
        gb = gslot[slot]
        for h in range(heads):
            cols = slice(h * DIM, (h + 1) * DIM)
            qr[j, cols] = qb[:, cols]
            gr[j, cols] = gb[:, cols]
            qt[j, :, cols] = qb[:, cols].T
            gt[j, :, cols] = gb[:, cols].T

    scale = ROOT * math.log2(math.e)
    part_p[...] = jnp.zeros_like(part_p)
    part_o[...] = jnp.zeros_like(part_o)

    def scores(keys, j, first, n):
        s = dot(keys, qt[j], NN)
        top = None
        for at in range(0, n, PIECE):
            rows = slice(first + at, first + at + PIECE)
            piece = s[at : at + PIECE] * scale + every_head(bias[j, rows], heads)
            expo[j, rows] = piece
            top = fold(piece, jnp.max) if top is None else jnp.maximum(top, fold(piece, jnp.max))
        return jnp.max(top, axis=0, keepdims=True)

    def exponentials(j, first, n, top, low=None):
        total = None
        for at in range(0, n, PIECE):
            rows = slice(first + at, first + at + PIECE)
            e = jnp.exp2(expo[j, rows] - top)
            expo[j, rows] = e
            if low is not None:
                low[j, rows] = e.astype(BF16)
            total = fold(e, jnp.sum) if total is None else total + fold(e, jnp.sum)
        return jnp.sum(total, axis=0, keepdims=True)

    tops = []
    for j in range(GROUP):
        n = (j + 1) * SPAN
        tops.append(scores(ko[0:n], j, 0, n))
        dpo[j, 0:n] = dot(vo[0:n], gt[j], NN)
    for j in range(GROUP):
        n = (j + 1) * SPAN
        stat[j, 0:1] = tops[j]
        stat[j, 1:2] = exponentials(j, 0, n, tops[j], pb)
        oto[j] = dot(vot[:, 0:n], pb[j, 0:n], NN)

    @pl.when(has_prev)
    def _():
        for far, relay in zip(far_k, relay_k):
            far.wait_recv()
            relay.start()
        for relay in relay_k:
            relay.wait_recv()

    @pl.when(jnp.logical_not(has_prev))
    def _():
        kprev[...] = jnp.zeros_like(kprev)
        vprev[...] = jnp.zeros_like(vprev)

    for i in range(GROUP):
        rows = slice(i * SPAN, (i + 1) * SPAN)
        kb = kprev[pick(there, i)]
        kp[rows] = kb
        kpt[:, rows] = kb.T

    tops = []
    for j in range(GROUP):
        top = scores(kp[j * SPAN :], j, (j + 1) * SPAN, (GROUP - j) * SPAN)
        tops.append(jnp.maximum(stat[j, 0:1], top))
    norms = []
    alphas = []
    for j in range(GROUP):
        total = exponentials(j, (j + 1) * SPAN, (GROUP - j) * SPAN, tops[j])
        shrink = jnp.exp2(stat[j, 0:1] - tops[j])
        r = 1.0 / (stat[j, 1:2] * shrink + total)
        norms.append(r)
        alphas.append(shrink * r)
        if j == 1:

            @pl.when(has_prev)
            def _():
                for far, relay in zip(far_v, relay_v):
                    far.wait_recv()
                    relay.start()

    for j in range(GROUP):
        for at in range((j + 1) * SPAN, expo.shape[1], PIECE):
            rows = slice(at, at + PIECE)
            pr = expo[j, rows] * norms[j]
            expo[j, rows] = pr
            pb[j, rows] = pr.astype(BF16)

    @pl.when(has_prev)
    def _():
        for relay in relay_v:
            relay.wait_recv()

    for i in range(GROUP):
        rows = slice(i * SPAN, (i + 1) * SPAN)
        vb = vprev[pick(there, i)]
        vp[rows] = vb
        vpt[:, rows] = vb.T

    deltas = []

    def finish_out(j):
        out = oto[j] * alphas[j] + dot(vpt[:, j * SPAN :], pb[j, (j + 1) * SPAN :], NN)
        deltas.append(jnp.sum(out * gt[j].astype(F32), axis=0, keepdims=True))
        out = out.astype(BF16)
        for h in range(heads):
            cols = slice(h * DIM, (h + 1) * DIM)
            o_mine[j, :, cols] = out[:, cols].T

    def prev_dprobs(j):
        return dot(vp[j * SPAN :], gt[j], NN)

    def prev_grads(j, dp):
        at = (j + 1) * SPAN
        for p in range(0, dp.shape[0], PIECE):
            rows = slice(at + p, at + p + PIECE)
            sb[j, rows] = (expo[j, rows] * (dp[p : p + PIECE] - deltas[j])).astype(BF16)
        part_p[j:, :, 0:DIM] += spans(dot(sb[j, at:], qr[j], NN) * ROOT)
        part_p[j:, :, DIM:] += spans(dot(pb[j, at:], gr[j], NN))

    finish_out(0)
    dp = prev_dprobs(0)
    for j in range(1, GROUP):
        finish_out(j)
        next_dp = prev_dprobs(j)
        prev_grads(j - 1, dp)
        dp = next_dp
    prev_grads(GROUP - 1, dp)

    def mine_of(spans, a):
        return jnp.where(core == 0, spans[a], spans[2 + a])

    def theirs_of(spans, a):
        return jnp.where(core == 0, spans[2 + a], spans[a])

    swap_p = [remote(sum_send.at[a], sum_near.at[a], p_s.at[a], p_r.at[a], beside)
              for a in range(2)]
    far_p = [
        remote(far_send_buf.at[a, pl.ds(at, BACK)], far_buf.at[a, pl.ds(at, BACK)],
               f_s.at[a, at // BACK], f_r.at[a, at // BACK], before)
        for a in range(2) for at in range(0, SPAN, BACK)
    ]
    for a in range(2):
        sum_send[a] = part_p[theirs_of(there, a)].astype(BF16)
        swap_p[a].start()

    swap_out = remote(o_send, o_near, oq_s.at[0], oq_r.at[0], beside)
    swap_dq = remote(q_send, q_near, oq_s.at[1], oq_r.at[1], beside)
    for a in range(2):
        o_send[a] = o_mine[theirs_of(here, a)]
    swap_out.start()

    def own_dscores(j):
        for at in range(0, (j + 1) * SPAN, PIECE):
            rows = slice(at, at + PIECE)
            pr = expo[j, rows] * alphas[j]
            pb[j, rows] = pr.astype(BF16)
            sb[j, rows] = (pr * (dpo[j, rows] - deltas[j])).astype(BF16)

    def query_grads(j):
        own = slice(0, (j + 1) * SPAN)
        at = (j + 1) * SPAN
        grad = dot(sb[j, own], ko[own], TN) + dot(sb[j, at:], kp[j * SPAN :], TN)
        grad = (grad * ROOT).astype(BF16)
        for h in range(heads):
            cols = slice(h * DIM, (h + 1) * DIM)
            q_mine[j, :, cols] = grad[cols]

    def own_grads(j):
        own = slice(0, (j + 1) * SPAN)
        part_o[0 : j + 1, :, 0:DIM] += spans(dot(sb[j, own], qr[j], NN) * ROOT)
        part_o[0 : j + 1, :, DIM:] += spans(dot(pb[j, own], gr[j], NN))

    own_dscores(0)
    for j in range(1, GROUP):
        own_dscores(j)
        query_grads(j - 1)
    query_grads(GROUP - 1)
    for a in range(2):
        q_send[a] = q_mine[theirs_of(here, a)]
    swap_dq.start()

    for a in range(2):
        swap_p[a].wait_recv()
        far_send_buf[a] = (
            part_p[mine_of(there, a)] + sum_near[a].astype(F32)).astype(BF16)

        @pl.when(has_prev)
        def _(a=a):
            for copy in far_p[a * (SPAN // BACK) : (a + 1) * (SPAN // BACK)]:
                copy.start()

    for j in range(GROUP):
        own_grads(j)

    swap_o = [remote(own_send.at[a], own_near.at[a], o_s.at[a], o_r.at[a], beside)
              for a in range(2)]
    for a in range(2):
        own_send[a] = part_o[theirs_of(here, a)].astype(BF16)
        swap_o[a].start()

    for a in range(2):
        j = mine_of(here, a)
        attn[a, :, columns(core)] = o_mine[j]
        dq[a, :, columns(core)] = q_mine[j]
    swap_out.wait_recv()
    for a in range(2):
        attn[a, :, columns(other)] = o_near[a]
    swap_dq.wait_recv()
    for a in range(2):
        dq[a, :, columns(other)] = q_near[a]

    @pl.when(jnp.logical_not(has_next))
    def _():
        far_buf[...] = jnp.zeros_like(far_buf)

    for a in range(2):
        swap_o[a].wait_recv()

        @pl.when(has_next)
        def _(a=a):
            for copy in far_p[a * (SPAN // BACK) : (a + 1) * (SPAN // BACK)]:
                copy.wait_recv()

        total = part_o[mine_of(here, a)] + own_near[a].astype(F32) + far_buf[a].astype(F32)
        dk[a] = total[:, 0:DIM].astype(BF16)
        dv[a] = total[:, DIM:].astype(BF16)

    for copy in near + swap_p + [swap_out, swap_dq] + swap_o:
        copy.wait_send()

    @pl.when(has_next)
    def _():
        for copy in far_k + far_v:
            copy.wait_send()

    @pl.when(has_prev)
    def _():
        for copy in relay_k + relay_v + far_p:
            copy.wait_send()


def store_kernel(*refs):
    n = (len(refs) - 1) // 2
    sem = refs[2 * n]
    copies = []
    for i in range(n):
        for a in range(2):
            copies.append(
                pltpu.make_async_copy(refs[i].at[a], refs[n + i].at[a], sem.at[len(copies)]))
    for copy in copies:
        copy.start()
    for copy in copies:
        copy.wait()


def shards(count, queries, keys, values, grad_out, lengths, assign):
    width = queries.shape[1]
    half = width // 2
    docs = lengths.shape[0]
    wide = -(-docs // 128) * 128
    hbm = pl.BlockSpec(memory_space=pltpu.HBM)
    vmem = pl.BlockSpec(memory_space=pltpu.VMEM)
    dma = pltpu.SemaphoreType.DMA
    shape = jax.ShapeDtypeStruct
    keyed = GROUP * SPAN
    seen = keyed + SPAN
    moves = 2 * SPAN // FAR
    outs = (
        shape((2, SPAN, width), BF16),
        shape((2, SPAN, width), BF16),
        shape((2, SPAN, DIM), BF16),
        shape((2, SPAN, DIM), BF16),
    )
    results = pl.pallas_call(
        functools.partial(main_kernel, count),
        out_shape=outs,
        in_specs=[hbm] * 6,
        out_specs=(vmem,) * 4,
        scratch_shapes=[
            pltpu.VMEM((docs,), jnp.int32),
            pltpu.SMEM(assign.shape[::-1], jnp.int32),
            pltpu.VMEM((8, wide), jnp.int32),
            pltpu.VMEM((GROUP, SPAN, half), BF16),
            pltpu.VMEM((GROUP, SPAN, half), BF16),
            pltpu.VMEM((GROUP, SPAN, DIM), BF16),
            pltpu.VMEM((GROUP, SPAN, DIM), BF16),
            pltpu.VMEM((GROUP, SPAN, DIM), BF16),
            pltpu.VMEM((GROUP, SPAN, DIM), BF16),
            pltpu.VMEM((GROUP, half, DIM), BF16),
            pltpu.VMEM((GROUP, half, DIM), BF16),
            pltpu.VMEM((GROUP, DIM, half), BF16),
            pltpu.VMEM((GROUP, DIM, half), BF16),
            pltpu.VMEM((keyed, DIM), BF16),
            pltpu.VMEM((keyed, DIM), BF16),
            pltpu.VMEM((DIM, keyed), BF16),
            pltpu.VMEM((DIM, keyed), BF16),
            pltpu.VMEM((keyed, DIM), BF16),
            pltpu.VMEM((keyed, DIM), BF16),
            pltpu.VMEM((DIM, keyed), BF16),
            pltpu.VMEM((DIM, keyed), BF16),
            pltpu.VMEM((GROUP, seen, SPAN), F32),
            pltpu.VMEM((GROUP, seen, half), F32),
            pltpu.VMEM((GROUP, keyed, half), F32),
            pltpu.VMEM((GROUP, seen, half), BF16),
            pltpu.VMEM((GROUP, seen, half), BF16),
            pltpu.VMEM((GROUP, DIM, half), F32),
            pltpu.VMEM((GROUP, 8, half), F32),
            pltpu.VMEM((GROUP, SPAN, 2 * DIM), F32),
            pltpu.VMEM((GROUP, SPAN, 2 * DIM), F32),
            pltpu.VMEM((2, SPAN, 2 * DIM), BF16),
            pltpu.VMEM((2, SPAN, 2 * DIM), BF16),
            pltpu.VMEM((2, SPAN, 2 * DIM), BF16),
            pltpu.VMEM((2, SPAN, 2 * DIM), BF16),
            pltpu.VMEM((2, SPAN, 2 * DIM), BF16),
            pltpu.VMEM((2, SPAN, 2 * DIM), BF16),
            pltpu.VMEM((GROUP, SPAN, half), BF16),
            pltpu.VMEM((2, SPAN, half), BF16),
            pltpu.VMEM((2, SPAN, half), BF16),
            pltpu.VMEM((GROUP, SPAN, half), BF16),
            pltpu.VMEM((2, SPAN, half), BF16),
            pltpu.VMEM((2, SPAN, half), BF16),
            dma((6,)),
            dma((moves,)), dma((moves,)), dma((moves,)), dma((moves,)),
            dma((moves,)), dma((moves,)), dma((moves,)), dma((moves,)),
            dma((4,)), dma((4,)),
            dma((2,)), dma((2,)), dma((2, SPAN // BACK)), dma((2, SPAN // BACK)),
            dma((2,)), dma((2,)),
            dma((2,)), dma((2,)),
        ],
        compiler_params=pltpu.CompilerParams(
            collective_id=0, has_side_effects=True, vmem_limit_bytes=40 * 2**20),
        name="attend",
    )(*[
        pltpu.with_memory_space_constraint(x, pltpu.HBM)
        for x in (
            queries.reshape(2, SPAN, width), grad_out.reshape(2, SPAN, width),
            keys.reshape(2, SPAN, DIM), values.reshape(2, SPAN, DIM), lengths, assign.T,
        )
    ])
    results = pl.pallas_call(
        store_kernel,
        out_shape=outs,
        in_specs=[pl.BlockSpec(memory_space=pltpu.VMEM)] * 4,
        out_specs=(hbm,) * 4,
        scratch_shapes=[dma((8,))],
        name="store",
    )(*[pltpu.with_memory_space_constraint(r, pltpu.VMEM) for r in results])
    return tuple(r.reshape(2 * SPAN, r.shape[2]) for r in results)


def solution(mesh):
    split = P("seq", "grp")
    return jax.shard_map(
        functools.partial(shards, mesh.shape["seq"]),
        mesh=mesh,
        in_specs=(split, split, split, split, P(), P()),
        out_specs=(split, split, split, split),
        check_vma=False,
    )
```

```python
import functools
import math

import jax
import jax.numpy as jnp
from jax import lax
from jax.experimental import pallas as pl
from jax.experimental.pallas import tpu as pltpu
from jax.sharding import PartitionSpec as P

MESH = pl.DeviceIdType.MESH
SPAN = 128
DIM = 128
GROUP = 4
F32 = jnp.float32
BF16 = jnp.bfloat16
NT = (((1,), (1,)), ((), ()))
NN = (((1,), (0,)), ((), ()))
TN = (((0,), (0,)), ((), ()))
ROOT = 1.0 / math.sqrt(DIM)
PIECE = 32


def dot(a, b, dims):
    return lax.dot_general(a, b, dims, preferred_element_type=F32)


def pick(values, wanted):
    index = jnp.int32(0)
    for i, value in enumerate(values):
        index = jnp.where(value == wanted, i, index)
    return index


def every_head(x, heads):
    return jnp.concatenate([x] * heads, axis=1)


def spans(x):
    return x.reshape(x.shape[0] // SPAN, SPAN, x.shape[1])


def fold(x, reduce):
    return reduce(x.reshape(x.shape[0] // 8, 8, x.shape[1]), axis=0)


def main_kernel(
    count, q, g, k, v, lens, assign, attn, dq, dk, dv,
    lens_v, assign_s, padded, qslot, gslot, kown, vown, kprev, vprev, qr, gr, qt, gt,
    ko, vo, kot, vot, kp, vp, kpt, vpt, bias, expo, dpo, pb, sb, oto, stat,
    part_p, part_o, sum_send, sum_near, far_send_buf, far_buf, own_send, own_near,
    o_mine, o_send, o_near, q_mine, q_send, q_near,
    arrived, loc_sem, far_ks, far_kr, far_vs, far_vr, rel_ks, rel_kr, rel_vs, rel_vr,
    near_s, near_r, p_s, p_r, f_s, f_r, o_s, o_r, oq_s, oq_r,
):
    me = lax.axis_index("seq")
    grp = lax.axis_index("grp")
    core = lax.rem(me, 2)
    other = 1 - core
    chip = me // 2
    beside = me + 1 - 2 * core
    has_prev = chip > 0
    has_next = chip < count // 2 - 1
    before = jnp.where(has_prev, me - 2, me)
    after = jnp.where(has_next, me + 2, me)
    width = q.shape[2] // 2
    heads = width // DIM

    def remote(src, dst, send, recv, device):
        return pltpu.make_async_remote_copy(
            src_ref=src, dst_ref=dst, send_sem=send, recv_sem=recv,
            device_id=(device, grp), device_id_type=MESH,
        )

    def columns(which):
        return pl.ds(pl.multiple_of(which * width, width), width)

    own_slots = pl.ds(2 * core, 2)
    local = [
        pltpu.make_async_copy(k, kown.at[own_slots], loc_sem.at[0]),
        pltpu.make_async_copy(v, vown.at[own_slots], loc_sem.at[1]),
        pltpu.make_async_copy(lens, lens_v, loc_sem.at[2]),
        pltpu.make_async_copy(assign, assign_s, loc_sem.at[3]),
        pltpu.make_async_copy(q.at[:, :, columns(core)], qslot.at[own_slots], loc_sem.at[4]),
        pltpu.make_async_copy(g.at[:, :, columns(core)], gslot.at[own_slots], loc_sem.at[5]),
    ]
    far_k = [remote(k.at[a], kprev.at[2 * core + a], far_ks.at[a], far_kr.at[a], after)
             for a in range(2)]
    far_v = [remote(v.at[a], vprev.at[2 * core + a], far_vs.at[a], far_vr.at[a], after)
             for a in range(2)]
    relay_k = [remote(kprev.at[2 * core + a], kprev.at[2 * core + a], rel_ks.at[a], rel_kr.at[a],
                      beside) for a in range(2)]
    relay_v = [remote(vprev.at[2 * core + a], vprev.at[2 * core + a], rel_vs.at[a], rel_vr.at[a],
                      beside) for a in range(2)]
    near = [
        remote(k, kown.at[own_slots], near_s.at[0], near_r.at[0], beside),
        remote(v, vown.at[own_slots], near_s.at[1], near_r.at[1], beside),
        remote(q.at[:, :, columns(other)], qslot.at[own_slots], near_s.at[2], near_r.at[2], beside),
        remote(g.at[:, :, columns(other)], gslot.at[own_slots], near_s.at[3], near_r.at[3], beside),
    ]

    barrier = pltpu.get_barrier_semaphore()
    pl.semaphore_signal(barrier, inc=1, device_id=(beside, grp), device_id_type=MESH)

    @pl.when(has_prev)
    def _():
        pl.semaphore_signal(barrier, inc=1, device_id=(before, grp), device_id_type=MESH)

    for copy in local:
        copy.start()
    pl.semaphore_wait(barrier, 1 + has_next.astype(jnp.int32))

    @pl.when(has_next)
    def _():
        pl.semaphore_signal(arrived, inc=1, device_id=(after, grp), device_id_type=MESH)
        for copy in far_k + far_v:
            copy.start()

    for copy in near[:2]:
        copy.start()

    docs = lens_v.shape[0]
    wide = padded.shape[1]
    padded[...] = jnp.zeros_like(padded)
    local[2].wait()
    padded[0:1, 0:docs] = lens_v[...].reshape(1, docs)
    length = padded[...]
    high = length >> 8
    low = length - (high << 8)
    row8 = lax.broadcasted_iota(jnp.int32, (8, wide), 0)
    both = jnp.where(row8 == 1, pltpu.roll(low, 1, 0), high).astype(F32).astype(BF16)
    until = lax.broadcasted_iota(jnp.int32, (wide, wide), 0)
    upto = lax.broadcasted_iota(jnp.int32, (wide, wide), 1)
    lower = jnp.where(upto <= until, 1.0, 0.0).astype(BF16)
    sums = dot(lower, both, NT)
    base = chip * (GROUP * SPAN)
    ends = sums[:, 0:1] * 256.0 + sums[:, 1:2] - base.astype(F32)
    least = -base.astype(F32)
    key_row = lax.broadcasted_iota(jnp.int32, (SPAN, SPAN), 0).astype(F32)
    query_col = lax.broadcasted_iota(jnp.int32, (SPAN, SPAN), 1).astype(F32)
    for j in range(GROUP):
        pos = query_col[0:1] + float(j * SPAN)
        start = jnp.max(jnp.where(ends <= pos, ends, least), axis=0, keepdims=True)
        for b in range(GROUP + 1):
            key = b if b <= j else b - 1 - GROUP
            ok = key_row + float(key * SPAN) >= start
            if b == j:
                ok = ok & (key_row <= query_col)
            bias[j, b * SPAN : (b + 1) * SPAN] = jnp.where(ok, 0.0, -1e30)

    for copy in near[2:]:
        copy.start()

    local[3].wait()
    back = jnp.maximum(chip - 1, 0)
    here = [assign_s[s % 2, 2 * chip + s // 2] & (GROUP - 1) for s in range(GROUP)]
    there = [assign_s[s % 2, 2 * back + s // 2] & (GROUP - 1) for s in range(GROUP)]
    for copy in (local[0], local[1], local[4], local[5]):
        copy.wait()
    for copy in near:
        copy.wait_recv()
    for j in range(GROUP):
        slot = pick(here, j)
        rows = slice(j * SPAN, (j + 1) * SPAN)
        kb = kown[slot]
        vb = vown[slot]
        ko[rows] = kb
        vo[rows] = vb
        kot[:, rows] = kb.T
        vot[:, rows] = vb.T
        qb = qslot[slot]
        gb = gslot[slot]
        for h in range(heads):
            cols = slice(h * DIM, (h + 1) * DIM)
            qr[j, cols] = qb[:, cols]
            gr[j, cols] = gb[:, cols]
            qt[j, :, cols] = qb[:, cols].T
            gt[j, :, cols] = gb[:, cols].T

    scale = ROOT * math.log2(math.e)
    part_p[...] = jnp.zeros_like(part_p)
    part_o[...] = jnp.zeros_like(part_o)

    def scores(keys, j, first, n):
        s = dot(keys, qt[j], NN)
        top = None
        for at in range(0, n, PIECE):
            rows = slice(first + at, first + at + PIECE)
            piece = s[at : at + PIECE] * scale + every_head(bias[j, rows], heads)
            expo[j, rows] = piece
            top = fold(piece, jnp.max) if top is None else jnp.maximum(top, fold(piece, jnp.max))
        return jnp.max(top, axis=0, keepdims=True)

    def exponentials(j, first, n, top, low=None):
        total = None
        for at in range(0, n, PIECE):
            rows = slice(first + at, first + at + PIECE)
            e = jnp.exp2(expo[j, rows] - top)
            expo[j, rows] = e
            if low is not None:
                low[j, rows] = e.astype(BF16)
            total = fold(e, jnp.sum) if total is None else total + fold(e, jnp.sum)
        return jnp.sum(total, axis=0, keepdims=True)

    tops = []
    for j in range(GROUP):
        n = (j + 1) * SPAN
        tops.append(scores(ko[0:n], j, 0, n))
        dpo[j, 0:n] = dot(vo[0:n], gt[j], NN)
    for j in range(GROUP):
        n = (j + 1) * SPAN
        stat[j, 0:1] = tops[j]
        stat[j, 1:2] = exponentials(j, 0, n, tops[j], pb)
        oto[j] = dot(vot[:, 0:n], pb[j, 0:n], NN)

    @pl.when(has_prev)
    def _():
        pl.semaphore_wait(arrived, 1)
        for a in range(2):
            far_k[a].wait_recv()
            relay_k[a].start()
        for a in range(2):
            relay_k[a].wait_recv()

    @pl.when(jnp.logical_not(has_prev))
    def _():
        kprev[...] = jnp.zeros_like(kprev)
        vprev[...] = jnp.zeros_like(vprev)

    for i in range(GROUP):
        rows = slice(i * SPAN, (i + 1) * SPAN)
        kb = kprev[pick(there, i)]
        kp[rows] = kb
        kpt[:, rows] = kb.T

    tops = []
    for j in range(GROUP):
        top = scores(kp[j * SPAN :], j, (j + 1) * SPAN, (GROUP - j) * SPAN)
        tops.append(jnp.maximum(stat[j, 0:1], top))
    norms = []
    alphas = []
    for j in range(GROUP):
        total = exponentials(j, (j + 1) * SPAN, (GROUP - j) * SPAN, tops[j])
        shrink = jnp.exp2(stat[j, 0:1] - tops[j])
        r = 1.0 / (stat[j, 1:2] * shrink + total)
        norms.append(r)
        alphas.append(shrink * r)
        if j == 1:

            @pl.when(has_prev)
            def _():
                for a in range(2):
                    far_v[a].wait_recv()
                    relay_v[a].start()

    for j in range(GROUP):
        for at in range((j + 1) * SPAN, expo.shape[1], PIECE):
            rows = slice(at, at + PIECE)
            pr = expo[j, rows] * norms[j]
            expo[j, rows] = pr
            pb[j, rows] = pr.astype(BF16)

    @pl.when(has_prev)
    def _():
        for a in range(2):
            relay_v[a].wait_recv()

    for i in range(GROUP):
        rows = slice(i * SPAN, (i + 1) * SPAN)
        vb = vprev[pick(there, i)]
        vp[rows] = vb
        vpt[:, rows] = vb.T

    deltas = []

    def finish_out(j):
        out = oto[j] * alphas[j] + dot(vpt[:, j * SPAN :], pb[j, (j + 1) * SPAN :], NN)
        deltas.append(jnp.sum(out * gt[j].astype(F32), axis=0, keepdims=True))
        out = out.astype(BF16)
        for h in range(heads):
            cols = slice(h * DIM, (h + 1) * DIM)
            o_mine[j, :, cols] = out[:, cols].T

    def prev_dprobs(j):
        return dot(vp[j * SPAN :], gt[j], NN)

    def prev_grads(j, dp):
        at = (j + 1) * SPAN
        for p in range(0, dp.shape[0], PIECE):
            rows = slice(at + p, at + p + PIECE)
            sb[j, rows] = (expo[j, rows] * (dp[p : p + PIECE] - deltas[j])).astype(BF16)
        part_p[j:, :, 0:DIM] += spans(dot(sb[j, at:], qr[j], NN) * ROOT)
        part_p[j:, :, DIM:] += spans(dot(pb[j, at:], gr[j], NN))

    finish_out(0)
    dp = prev_dprobs(0)
    for j in range(1, GROUP):
        finish_out(j)
        next_dp = prev_dprobs(j)
        prev_grads(j - 1, dp)
        dp = next_dp
    prev_grads(GROUP - 1, dp)

    def mine_of(spans, a):
        return jnp.where(core == 0, spans[a], spans[2 + a])

    def theirs_of(spans, a):
        return jnp.where(core == 0, spans[2 + a], spans[a])

    swap_p = [remote(sum_send.at[a], sum_near.at[a], p_s.at[a], p_r.at[a], beside)
              for a in range(2)]
    far_p = [remote(far_send_buf.at[a], far_buf.at[a], f_s.at[a], f_r.at[a], before)
             for a in range(2)]
    for a in range(2):
        sum_send[a] = part_p[theirs_of(there, a)].astype(BF16)
        swap_p[a].start()

    swap_out = remote(o_send, o_near, oq_s.at[0], oq_r.at[0], beside)
    swap_dq = remote(q_send, q_near, oq_s.at[1], oq_r.at[1], beside)
    for a in range(2):
        o_send[a] = o_mine[theirs_of(here, a)]
    swap_out.start()

    def own_dscores(j):
        for at in range(0, (j + 1) * SPAN, PIECE):
            rows = slice(at, at + PIECE)
            pr = expo[j, rows] * alphas[j]
            pb[j, rows] = pr.astype(BF16)
            sb[j, rows] = (pr * (dpo[j, rows] - deltas[j])).astype(BF16)

    def query_grads(j):
        own = slice(0, (j + 1) * SPAN)
        at = (j + 1) * SPAN
        grad = dot(sb[j, own], ko[own], TN) + dot(sb[j, at:], kp[j * SPAN :], TN)
        grad = (grad * ROOT).astype(BF16)
        for h in range(heads):
            cols = slice(h * DIM, (h + 1) * DIM)
            q_mine[j, :, cols] = grad[cols]

    def own_grads(j):
        own = slice(0, (j + 1) * SPAN)
        part_o[0 : j + 1, :, 0:DIM] += spans(dot(sb[j, own], qr[j], NN) * ROOT)
        part_o[0 : j + 1, :, DIM:] += spans(dot(pb[j, own], gr[j], NN))

    own_dscores(0)
    for j in range(1, GROUP):
        own_dscores(j)
        query_grads(j - 1)
    query_grads(GROUP - 1)
    for a in range(2):
        q_send[a] = q_mine[theirs_of(here, a)]
    swap_dq.start()

    for a in range(2):
        swap_p[a].wait_recv()
        far_send_buf[a] = (
            part_p[mine_of(there, a)] + sum_near[a].astype(F32)).astype(BF16)

        @pl.when(has_prev)
        def _(a=a):
            far_p[a].start()

    for j in range(GROUP):
        own_grads(j)

    swap_o = [remote(own_send.at[a], own_near.at[a], o_s.at[a], o_r.at[a], beside)
              for a in range(2)]
    for a in range(2):
        own_send[a] = part_o[theirs_of(here, a)].astype(BF16)
        swap_o[a].start()

    for a in range(2):
        j = mine_of(here, a)
        attn[a, :, columns(core)] = o_mine[j]
        dq[a, :, columns(core)] = q_mine[j]
    swap_out.wait_recv()
    for a in range(2):
        attn[a, :, columns(other)] = o_near[a]
    swap_dq.wait_recv()
    for a in range(2):
        dq[a, :, columns(other)] = q_near[a]

    @pl.when(jnp.logical_not(has_next))
    def _():
        far_buf[...] = jnp.zeros_like(far_buf)

    for a in range(2):
        swap_o[a].wait_recv()

        @pl.when(has_next)
        def _(a=a):
            far_p[a].wait_recv()

        total = part_o[mine_of(here, a)] + own_near[a].astype(F32) + far_buf[a].astype(F32)
        dk[a] = total[:, 0:DIM].astype(BF16)
        dv[a] = total[:, DIM:].astype(BF16)

    for copy in near + swap_p + [swap_out, swap_dq] + swap_o:
        copy.wait_send()

    @pl.when(has_next)
    def _():
        for copy in far_k + far_v:
            copy.wait_send()

    @pl.when(has_prev)
    def _():
        for copy in relay_k + relay_v + far_p:
            copy.wait_send()


def store_kernel(*refs):
    n = (len(refs) - 1) // 2
    sem = refs[2 * n]
    copies = []
    for i in range(n):
        for a in range(2):
            copies.append(
                pltpu.make_async_copy(refs[i].at[a], refs[n + i].at[a], sem.at[len(copies)]))
    for copy in copies:
        copy.start()
    for copy in copies:
        copy.wait()


def shards(count, queries, keys, values, grad_out, lengths, assign):
    width = queries.shape[1]
    half = width // 2
    docs = lengths.shape[0]
    wide = -(-docs // 128) * 128
    hbm = pl.BlockSpec(memory_space=pltpu.HBM)
    vmem = pl.BlockSpec(memory_space=pltpu.VMEM)
    dma = pltpu.SemaphoreType.DMA
    shape = jax.ShapeDtypeStruct
    keyed = GROUP * SPAN
    seen = keyed + SPAN
    outs = (
        shape((2, SPAN, width), BF16),
        shape((2, SPAN, width), BF16),
        shape((2, SPAN, DIM), BF16),
        shape((2, SPAN, DIM), BF16),
    )
    results = pl.pallas_call(
        functools.partial(main_kernel, count),
        out_shape=outs,
        in_specs=[hbm] * 6,
        out_specs=(vmem,) * 4,
        scratch_shapes=[
            pltpu.VMEM((docs,), jnp.int32),
            pltpu.SMEM(assign.shape[::-1], jnp.int32),
            pltpu.VMEM((8, wide), jnp.int32),
            pltpu.VMEM((GROUP, SPAN, half), BF16),
            pltpu.VMEM((GROUP, SPAN, half), BF16),
            pltpu.VMEM((GROUP, SPAN, DIM), BF16),
            pltpu.VMEM((GROUP, SPAN, DIM), BF16),
            pltpu.VMEM((GROUP, SPAN, DIM), BF16),
            pltpu.VMEM((GROUP, SPAN, DIM), BF16),
            pltpu.VMEM((GROUP, half, DIM), BF16),
            pltpu.VMEM((GROUP, half, DIM), BF16),
            pltpu.VMEM((GROUP, DIM, half), BF16),
            pltpu.VMEM((GROUP, DIM, half), BF16),
            pltpu.VMEM((keyed, DIM), BF16),
            pltpu.VMEM((keyed, DIM), BF16),
            pltpu.VMEM((DIM, keyed), BF16),
            pltpu.VMEM((DIM, keyed), BF16),
            pltpu.VMEM((keyed, DIM), BF16),
            pltpu.VMEM((keyed, DIM), BF16),
            pltpu.VMEM((DIM, keyed), BF16),
            pltpu.VMEM((DIM, keyed), BF16),
            pltpu.VMEM((GROUP, seen, SPAN), F32),
            pltpu.VMEM((GROUP, seen, half), F32),
            pltpu.VMEM((GROUP, keyed, half), F32),
            pltpu.VMEM((GROUP, seen, half), BF16),
            pltpu.VMEM((GROUP, seen, half), BF16),
            pltpu.VMEM((GROUP, DIM, half), F32),
            pltpu.VMEM((GROUP, 8, half), F32),
            pltpu.VMEM((GROUP, SPAN, 2 * DIM), F32),
            pltpu.VMEM((GROUP, SPAN, 2 * DIM), F32),
            pltpu.VMEM((2, SPAN, 2 * DIM), BF16),
            pltpu.VMEM((2, SPAN, 2 * DIM), BF16),
            pltpu.VMEM((2, SPAN, 2 * DIM), BF16),
            pltpu.VMEM((2, SPAN, 2 * DIM), BF16),
            pltpu.VMEM((2, SPAN, 2 * DIM), BF16),
            pltpu.VMEM((2, SPAN, 2 * DIM), BF16),
            pltpu.VMEM((GROUP, SPAN, half), BF16),
            pltpu.VMEM((2, SPAN, half), BF16),
            pltpu.VMEM((2, SPAN, half), BF16),
            pltpu.VMEM((GROUP, SPAN, half), BF16),
            pltpu.VMEM((2, SPAN, half), BF16),
            pltpu.VMEM((2, SPAN, half), BF16),
            pltpu.SemaphoreType.REGULAR,
            dma((6,)),
            dma((2,)), dma((2,)), dma((2,)), dma((2,)),
            dma((2,)), dma((2,)), dma((2,)), dma((2,)),
            dma((4,)), dma((4,)),
            dma((2,)), dma((2,)), dma((2,)), dma((2,)), dma((2,)), dma((2,)),
            dma((2,)), dma((2,)),
        ],
        compiler_params=pltpu.CompilerParams(
            collective_id=0, has_side_effects=True, vmem_limit_bytes=40 * 2**20),
        name="attend",
    )(*[
        pltpu.with_memory_space_constraint(x, pltpu.HBM)
        for x in (
            queries.reshape(2, SPAN, width), grad_out.reshape(2, SPAN, width),
            keys.reshape(2, SPAN, DIM), values.reshape(2, SPAN, DIM), lengths, assign.T,
        )
    ])
    results = pl.pallas_call(
        store_kernel,
        out_shape=outs,
        in_specs=[pl.BlockSpec(memory_space=pltpu.VMEM)] * 4,
        out_specs=(hbm,) * 4,
        scratch_shapes=[dma((8,))],
        name="store",
    )(*[pltpu.with_memory_space_constraint(r, pltpu.VMEM) for r in results])
    return tuple(r.reshape(2 * SPAN, r.shape[2]) for r in results)


def solution(mesh):
    split = P("seq", "grp")
    return jax.shard_map(
        functools.partial(shards, mesh.shape["seq"]),
        mesh=mesh,
        in_specs=(split, split, split, split, P(), P()),
        out_specs=(split, split, split, split),
        check_vma=False,
    )
```

```python
import functools
import math

import jax
import jax.numpy as jnp
from jax import lax
from jax.experimental import pallas as pl
from jax.experimental.pallas import tpu as pltpu
from jax.sharding import PartitionSpec as P

MESH = pl.DeviceIdType.MESH
SPAN = 128
DIM = 128
GROUP = 4
F32 = jnp.float32
BF16 = jnp.bfloat16
NT = (((1,), (1,)), ((), ()))
NN = (((1,), (0,)), ((), ()))
TN = (((0,), (0,)), ((), ()))
ROOT = 1.0 / math.sqrt(DIM)
PIECE = 32


def dot(a, b, dims):
    return lax.dot_general(a, b, dims, preferred_element_type=F32)


def pick(values, wanted):
    index = jnp.int32(0)
    for i, value in enumerate(values):
        index = jnp.where(value == wanted, i, index)
    return index


def every_head(x, heads):
    return jnp.concatenate([x] * heads, axis=1)


def spans(x):
    return x.reshape(x.shape[0] // SPAN, SPAN, x.shape[1])


def fold(x, reduce):
    return reduce(x.reshape(x.shape[0] // 8, 8, x.shape[1]), axis=0)


def main_kernel(
    count, q, g, k, v, lens, assign, attn, dq, dk, dv,
    lens_v, assign_s, padded, qslot, gslot, kown, vown, kprev, vprev, qr, gr, qt, gt,
    ko, vo, vot, kp, vp, vpt, bias, expo, dpo, pb, sb, oto, stat,
    part_p, part_o, sum_send, sum_near, far_send_buf, far_buf, own_send, own_near,
    o_mine, o_send, o_near, q_mine, q_send, q_near,
    arrived, loc_sem, far_ks, far_kr, far_vs, far_vr, rel_ks, rel_kr, rel_vs, rel_vr,
    near_s, near_r, p_s, p_r, f_s, f_r, o_s, o_r, oq_s, oq_r,
):
    me = lax.axis_index("seq")
    grp = lax.axis_index("grp")
    core = lax.rem(me, 2)
    other = 1 - core
    chip = me // 2
    beside = me + 1 - 2 * core
    has_prev = chip > 0
    has_next = chip < count // 2 - 1
    before = jnp.where(has_prev, me - 2, me)
    after = jnp.where(has_next, me + 2, me)
    width = q.shape[2] // 2
    heads = width // DIM

    def remote(src, dst, send, recv, device):
        return pltpu.make_async_remote_copy(
            src_ref=src, dst_ref=dst, send_sem=send, recv_sem=recv,
            device_id=(device, grp), device_id_type=MESH,
        )

    def columns(which):
        return pl.ds(pl.multiple_of(which * width, width), width)

    own_slots = pl.ds(2 * core, 2)
    local = [
        pltpu.make_async_copy(k, kown.at[own_slots], loc_sem.at[0]),
        pltpu.make_async_copy(v, vown.at[own_slots], loc_sem.at[1]),
        pltpu.make_async_copy(lens, lens_v, loc_sem.at[2]),
        pltpu.make_async_copy(assign, assign_s, loc_sem.at[3]),
        pltpu.make_async_copy(q.at[:, :, columns(core)], qslot.at[own_slots], loc_sem.at[4]),
        pltpu.make_async_copy(g.at[:, :, columns(core)], gslot.at[own_slots], loc_sem.at[5]),
    ]
    far_k = [remote(k.at[a], kprev.at[2 * core + a], far_ks.at[a], far_kr.at[a], after)
             for a in range(2)]
    far_v = [remote(v.at[a], vprev.at[2 * core + a], far_vs.at[a], far_vr.at[a], after)
             for a in range(2)]
    relay_k = [remote(kprev.at[2 * core + a], kprev.at[2 * core + a], rel_ks.at[a], rel_kr.at[a],
                      beside) for a in range(2)]
    relay_v = [remote(vprev.at[2 * core + a], vprev.at[2 * core + a], rel_vs.at[a], rel_vr.at[a],
                      beside) for a in range(2)]
    near = [
        remote(k, kown.at[own_slots], near_s.at[0], near_r.at[0], beside),
        remote(v, vown.at[own_slots], near_s.at[1], near_r.at[1], beside),
        remote(q.at[:, :, columns(other)], qslot.at[own_slots], near_s.at[2], near_r.at[2], beside),
        remote(g.at[:, :, columns(other)], gslot.at[own_slots], near_s.at[3], near_r.at[3], beside),
    ]

    barrier = pltpu.get_barrier_semaphore()
    pl.semaphore_signal(barrier, inc=1, device_id=(beside, grp), device_id_type=MESH)

    @pl.when(has_prev)
    def _():
        pl.semaphore_signal(barrier, inc=1, device_id=(before, grp), device_id_type=MESH)

    for copy in local[:4]:
        copy.start()
    pl.semaphore_wait(barrier, 1 + has_next.astype(jnp.int32))

    @pl.when(has_next)
    def _():
        pl.semaphore_signal(arrived, inc=1, device_id=(after, grp), device_id_type=MESH)
        for copy in far_k + far_v:
            copy.start()

    for copy in near[:2] + local[4:]:
        copy.start()

    docs = lens_v.shape[0]
    wide = padded.shape[1]
    padded[...] = jnp.zeros_like(padded)
    local[2].wait()
    padded[0:1, 0:docs] = lens_v[...].reshape(1, docs)
    length = padded[...]
    high = length >> 8
    low = length - (high << 8)
    row8 = lax.broadcasted_iota(jnp.int32, (8, wide), 0)
    both = jnp.where(row8 == 1, pltpu.roll(low, 1, 0), high).astype(F32).astype(BF16)
    until = lax.broadcasted_iota(jnp.int32, (wide, wide), 0)
    upto = lax.broadcasted_iota(jnp.int32, (wide, wide), 1)
    lower = jnp.where(upto <= until, 1.0, 0.0).astype(BF16)
    sums = dot(lower, both, NT)
    base = chip * (GROUP * SPAN)
    ends = sums[:, 0:1] * 256.0 + sums[:, 1:2] - base.astype(F32)
    least = -base.astype(F32)
    key_row = lax.broadcasted_iota(jnp.int32, (SPAN, SPAN), 0).astype(F32)
    query_col = lax.broadcasted_iota(jnp.int32, (SPAN, SPAN), 1).astype(F32)
    for j in range(GROUP):
        pos = query_col[0:1] + float(j * SPAN)
        start = jnp.max(jnp.where(ends <= pos, ends, least), axis=0, keepdims=True)
        for b in range(GROUP + 1):
            key = b if b <= j else b - 1 - GROUP
            ok = key_row + float(key * SPAN) >= start
            if b == j:
                ok = ok & (key_row <= query_col)
            bias[j, b * SPAN : (b + 1) * SPAN] = jnp.where(ok, 0.0, -1e30)

    for copy in near[2:]:
        copy.start()

    local[3].wait()
    back = jnp.maximum(chip - 1, 0)
    here = [assign_s[s % 2, 2 * chip + s // 2] & (GROUP - 1) for s in range(GROUP)]
    there = [assign_s[s % 2, 2 * back + s // 2] & (GROUP - 1) for s in range(GROUP)]
    for copy in (local[0], local[1], local[4], local[5]):
        copy.wait()
    for copy in near:
        copy.wait_recv()
    for j in range(GROUP):
        slot = pick(here, j)
        rows = slice(j * SPAN, (j + 1) * SPAN)
        kb = kown[slot]
        vb = vown[slot]
        ko[rows] = kb
        vo[rows] = vb
        vot[:, rows] = vb.T
        qb = qslot[slot]
        gb = gslot[slot]
        for h in range(heads):
            cols = slice(h * DIM, (h + 1) * DIM)
            qr[j, cols] = qb[:, cols]
            gr[j, cols] = gb[:, cols]
            qt[j, :, cols] = qb[:, cols].T
            gt[j, :, cols] = gb[:, cols].T

    scale = ROOT * math.log2(math.e)
    part_p[...] = jnp.zeros_like(part_p)
    part_o[...] = jnp.zeros_like(part_o)

    def scores(keys, j, first, n):
        s = dot(keys, qt[j], NN)
        top = None
        for at in range(0, n, PIECE):
            rows = slice(first + at, first + at + PIECE)
            piece = s[at : at + PIECE] * scale + every_head(bias[j, rows], heads)
            expo[j, rows] = piece
            top = fold(piece, jnp.max) if top is None else jnp.maximum(top, fold(piece, jnp.max))
        return jnp.max(top, axis=0, keepdims=True)

    def exponentials(j, first, n, top):
        total = jnp.zeros((8, width), F32)
        for at in range(0, n, PIECE):
            rows = slice(first + at, first + at + PIECE)
            e = jnp.exp2(expo[j, rows] - top)
            expo[j, rows] = e
            total = total + fold(e, jnp.sum)
        return jnp.sum(total, axis=0, keepdims=True)

    def weighted(j, first, dp):
        total = jnp.zeros((8, width), F32)
        for at in range(0, dp.shape[0], PIECE):
            rows = slice(first + at, first + at + PIECE)
            total = total + fold(expo[j, rows] * dp[at : at + PIECE], jnp.sum)
        return jnp.sum(total, axis=0, keepdims=True)

    tops = []
    for j in range(GROUP):
        n = (j + 1) * SPAN
        tops.append(scores(ko[0:n], j, 0, n))
        dpo[j, 0:n] = dot(vo[0:n], gt[j], NN)
    for j in range(GROUP):
        n = (j + 1) * SPAN
        stat[j, 0:1] = tops[j]
        stat[j, 1:2] = exponentials(j, 0, n, tops[j])
        stat[j, 2:3] = weighted(j, 0, dpo[j, 0:n])
        oto[j] = dot(vot[:, 0:n], expo[j, 0:n].astype(BF16), NN)

    @pl.when(has_prev)
    def _():
        pl.semaphore_wait(arrived, 1)
        for a in range(2):
            far_k[a].wait_recv()
            relay_k[a].start()
        for a in range(2):
            relay_k[a].wait_recv()

    @pl.when(jnp.logical_not(has_prev))
    def _():
        kprev[...] = jnp.zeros_like(kprev)
        vprev[...] = jnp.zeros_like(vprev)

    for i in range(GROUP):
        rows = slice(i * SPAN, (i + 1) * SPAN)
        kb = kprev[pick(there, i)]
        kp[rows] = kb

    tops = []
    for j in range(GROUP):
        top = scores(kp[j * SPAN :], j, (j + 1) * SPAN, (GROUP - j) * SPAN)
        tops.append(jnp.maximum(stat[j, 0:1], top))
    norms = []
    alphas = []
    for j in range(GROUP):
        total = exponentials(j, (j + 1) * SPAN, (GROUP - j) * SPAN, tops[j])
        shrink = jnp.exp2(stat[j, 0:1] - tops[j])
        r = 1.0 / (stat[j, 1:2] * shrink + total)
        norms.append(r)
        alphas.append(shrink * r)
        if j == 1:

            @pl.when(has_prev)
            def _():
                for a in range(2):
                    far_v[a].wait_recv()
                    relay_v[a].start()

    @pl.when(has_prev)
    def _():
        for a in range(2):
            relay_v[a].wait_recv()

    for i in range(GROUP):
        rows = slice(i * SPAN, (i + 1) * SPAN)
        vb = vprev[pick(there, i)]
        vp[rows] = vb

    deltas = []

    def prev_grads(j, dp):
        at = (j + 1) * SPAN
        delta = alphas[j] * stat[j, 2:3] + norms[j] * weighted(j, at, dp)
        deltas.append(delta)
        for p in range(0, dp.shape[0], PIECE):
            rows = slice(at + p, at + p + PIECE)
            pr = expo[j, rows] * norms[j]
            pb[j, rows] = pr.astype(BF16)
            sb[j, rows] = (pr * (dp[p : p + PIECE] - delta)).astype(BF16)
        part_p[j:, :, 0:DIM] += spans(dot(sb[j, at:], qr[j], NN) * ROOT)
        part_p[j:, :, DIM:] += spans(dot(pb[j, at:], gr[j], NN))

    dp = dot(vp[...], gt[0], NN)
    for j in range(GROUP):
        next_dp = dot(vp[(j + 1) * SPAN :], gt[j + 1], NN) if j < GROUP - 1 else None
        prev_grads(j, dp)
        dp = next_dp

    def mine_of(spans, a):
        return jnp.where(core == 0, spans[a], spans[2 + a])

    def theirs_of(spans, a):
        return jnp.where(core == 0, spans[2 + a], spans[a])

    swap_p = [remote(sum_send.at[a], sum_near.at[a], p_s.at[a], p_r.at[a], beside)
              for a in range(2)]
    far_p = [remote(far_send_buf.at[a], far_buf.at[a], f_s.at[a], f_r.at[a], before)
             for a in range(2)]
    for a in range(2):
        sum_send[a] = part_p[theirs_of(there, a)].astype(BF16)
        swap_p[a].start()

    swap_out = remote(o_send, o_near, oq_s.at[0], oq_r.at[0], beside)
    swap_dq = remote(q_send, q_near, oq_s.at[1], oq_r.at[1], beside)
    vpt[...] = vp[...].T
    for j in range(GROUP):
        out = oto[j] * alphas[j] + dot(vpt[:, j * SPAN :], pb[j, (j + 1) * SPAN :], NN)
        out = out.astype(BF16)
        for h in range(heads):
            cols = slice(h * DIM, (h + 1) * DIM)
            o_mine[j, :, cols] = out[:, cols].T
    for a in range(2):
        o_send[a] = o_mine[theirs_of(here, a)]
    swap_out.start()

    for a in range(2):
        swap_p[a].wait_recv()
        far_send_buf[a] = (
            part_p[mine_of(there, a)] + sum_near[a].astype(F32)).astype(BF16)

        @pl.when(has_prev)
        def _(a=a):
            far_p[a].start()

    def own_dscores(j):
        for at in range(0, (j + 1) * SPAN, PIECE):
            rows = slice(at, at + PIECE)
            pr = expo[j, rows] * alphas[j]
            pb[j, rows] = pr.astype(BF16)
            sb[j, rows] = (pr * (dpo[j, rows] - deltas[j])).astype(BF16)

    def query_grads(j):
        own = slice(0, (j + 1) * SPAN)
        at = (j + 1) * SPAN
        grad = dot(sb[j, own], ko[own], TN) + dot(sb[j, at:], kp[j * SPAN :], TN)
        grad = (grad * ROOT).astype(BF16)
        for h in range(heads):
            cols = slice(h * DIM, (h + 1) * DIM)
            q_mine[j, :, cols] = grad[cols]

    def own_grads(j):
        own = slice(0, (j + 1) * SPAN)
        part_o[0 : j + 1, :, 0:DIM] += spans(dot(sb[j, own], qr[j], NN) * ROOT)
        part_o[0 : j + 1, :, DIM:] += spans(dot(pb[j, own], gr[j], NN))

    own_dscores(0)
    for j in range(1, GROUP):
        own_dscores(j)
        query_grads(j - 1)
    query_grads(GROUP - 1)
    for a in range(2):
        q_send[a] = q_mine[theirs_of(here, a)]
    swap_dq.start()

    for j in range(GROUP):
        own_grads(j)

    swap_o = [remote(own_send.at[a], own_near.at[a], o_s.at[a], o_r.at[a], beside)
              for a in range(2)]
    for a in range(2):
        own_send[a] = part_o[theirs_of(here, a)].astype(BF16)
        swap_o[a].start()

    for a in range(2):
        j = mine_of(here, a)
        attn[a, :, columns(core)] = o_mine[j]
        dq[a, :, columns(core)] = q_mine[j]
    swap_out.wait_recv()
    for a in range(2):
        attn[a, :, columns(other)] = o_near[a]
    swap_dq.wait_recv()
    for a in range(2):
        dq[a, :, columns(other)] = q_near[a]

    @pl.when(jnp.logical_not(has_next))
    def _():
        far_buf[...] = jnp.zeros_like(far_buf)

    for a in range(2):
        swap_o[a].wait_recv()

        @pl.when(has_next)
        def _(a=a):
            far_p[a].wait_recv()

        total = part_o[mine_of(here, a)] + own_near[a].astype(F32) + far_buf[a].astype(F32)
        dk[a] = total[:, 0:DIM].astype(BF16)
        dv[a] = total[:, DIM:].astype(BF16)

    for copy in near + swap_p + [swap_out, swap_dq] + swap_o:
        copy.wait_send()

    @pl.when(has_next)
    def _():
        for copy in far_k + far_v:
            copy.wait_send()

    @pl.when(has_prev)
    def _():
        for copy in relay_k + relay_v + far_p:
            copy.wait_send()


def store_kernel(*refs):
    n = (len(refs) - 1) // 2
    sem = refs[2 * n]
    copies = []
    for i in range(n):
        for a in range(2):
            copies.append(
                pltpu.make_async_copy(refs[i].at[a], refs[n + i].at[a], sem.at[len(copies)]))
    for copy in copies:
        copy.start()
    for copy in copies:
        copy.wait()


def shards(count, queries, keys, values, grad_out, lengths, assign):
    width = queries.shape[1]
    half = width // 2
    docs = lengths.shape[0]
    wide = -(-docs // 128) * 128
    hbm = pl.BlockSpec(memory_space=pltpu.HBM)
    vmem = pl.BlockSpec(memory_space=pltpu.VMEM)
    dma = pltpu.SemaphoreType.DMA
    shape = jax.ShapeDtypeStruct
    keyed = GROUP * SPAN
    seen = keyed + SPAN
    outs = (
        shape((2, SPAN, width), BF16),
        shape((2, SPAN, width), BF16),
        shape((2, SPAN, DIM), BF16),
        shape((2, SPAN, DIM), BF16),
    )
    results = pl.pallas_call(
        functools.partial(main_kernel, count),
        out_shape=outs,
        in_specs=[hbm] * 6,
        out_specs=(vmem,) * 4,
        scratch_shapes=[
            pltpu.VMEM((docs,), jnp.int32),
            pltpu.SMEM(assign.shape[::-1], jnp.int32),
            pltpu.VMEM((8, wide), jnp.int32),
            pltpu.VMEM((GROUP, SPAN, half), BF16),
            pltpu.VMEM((GROUP, SPAN, half), BF16),
            pltpu.VMEM((GROUP, SPAN, DIM), BF16),
            pltpu.VMEM((GROUP, SPAN, DIM), BF16),
            pltpu.VMEM((GROUP, SPAN, DIM), BF16),
            pltpu.VMEM((GROUP, SPAN, DIM), BF16),
            pltpu.VMEM((GROUP, half, DIM), BF16),
            pltpu.VMEM((GROUP, half, DIM), BF16),
            pltpu.VMEM((GROUP, DIM, half), BF16),
            pltpu.VMEM((GROUP, DIM, half), BF16),
            pltpu.VMEM((keyed, DIM), BF16),
            pltpu.VMEM((keyed, DIM), BF16),
            pltpu.VMEM((DIM, keyed), BF16),
            pltpu.VMEM((keyed, DIM), BF16),
            pltpu.VMEM((keyed, DIM), BF16),
            pltpu.VMEM((DIM, keyed), BF16),
            pltpu.VMEM((GROUP, seen, SPAN), F32),
            pltpu.VMEM((GROUP, seen, half), F32),
            pltpu.VMEM((GROUP, keyed, half), F32),
            pltpu.VMEM((GROUP, seen, half), BF16),
            pltpu.VMEM((GROUP, seen, half), BF16),
            pltpu.VMEM((GROUP, DIM, half), F32),
            pltpu.VMEM((GROUP, 8, half), F32),
            pltpu.VMEM((GROUP, SPAN, 2 * DIM), F32),
            pltpu.VMEM((GROUP, SPAN, 2 * DIM), F32),
            pltpu.VMEM((2, SPAN, 2 * DIM), BF16),
            pltpu.VMEM((2, SPAN, 2 * DIM), BF16),
            pltpu.VMEM((2, SPAN, 2 * DIM), BF16),
            pltpu.VMEM((2, SPAN, 2 * DIM), BF16),
            pltpu.VMEM((2, SPAN, 2 * DIM), BF16),
            pltpu.VMEM((2, SPAN, 2 * DIM), BF16),
            pltpu.VMEM((GROUP, SPAN, half), BF16),
            pltpu.VMEM((2, SPAN, half), BF16),
            pltpu.VMEM((2, SPAN, half), BF16),
            pltpu.VMEM((GROUP, SPAN, half), BF16),
            pltpu.VMEM((2, SPAN, half), BF16),
            pltpu.VMEM((2, SPAN, half), BF16),
            pltpu.SemaphoreType.REGULAR,
            dma((6,)),
            dma((2,)), dma((2,)), dma((2,)), dma((2,)),
            dma((2,)), dma((2,)), dma((2,)), dma((2,)),
            dma((4,)), dma((4,)),
            dma((2,)), dma((2,)), dma((2,)), dma((2,)), dma((2,)), dma((2,)),
            dma((2,)), dma((2,)),
        ],
        compiler_params=pltpu.CompilerParams(
            collective_id=0, has_side_effects=True, vmem_limit_bytes=40 * 2**20),
        name="attend",
    )(*[
        pltpu.with_memory_space_constraint(x, pltpu.HBM)
        for x in (
            queries.reshape(2, SPAN, width), grad_out.reshape(2, SPAN, width),
            keys.reshape(2, SPAN, DIM), values.reshape(2, SPAN, DIM), lengths, assign.T,
        )
    ])
    results = pl.pallas_call(
        store_kernel,
        out_shape=outs,
        in_specs=[pl.BlockSpec(memory_space=pltpu.VMEM)] * 4,
        out_specs=(hbm,) * 4,
        scratch_shapes=[dma((8,))],
        name="store",
    )(*[pltpu.with_memory_space_constraint(r, pltpu.VMEM) for r in results])
    return tuple(r.reshape(2 * SPAN, r.shape[2]) for r in results)


def solution(mesh):
    split = P("seq", "grp")
    return jax.shard_map(
        functools.partial(shards, mesh.shape["seq"]),
        mesh=mesh,
        in_specs=(split, split, split, split, P(), P()),
        out_specs=(split, split, split, split),
        check_vma=False,
    )
```

```python
import functools
import math

import jax
import jax.numpy as jnp
from jax import lax
from jax.experimental import pallas as pl
from jax.experimental.pallas import tpu as pltpu
from jax.sharding import PartitionSpec as P

MESH = pl.DeviceIdType.MESH
SPAN = 128
DIM = 128
GROUP = 4
F32 = jnp.float32
BF16 = jnp.bfloat16
NT = (((1,), (1,)), ((), ()))
NN = (((1,), (0,)), ((), ()))
TN = (((0,), (0,)), ((), ()))
ROOT = 1.0 / math.sqrt(DIM)
PIECE = 32


def dot(a, b, dims):
    return lax.dot_general(a, b, dims, preferred_element_type=F32)


def pick(values, wanted):
    index = jnp.int32(0)
    for i, value in enumerate(values):
        index = jnp.where(value == wanted, i, index)
    return index


def every_head(x, heads):
    return jnp.concatenate([x] * heads, axis=1)


def spans(x):
    return x.reshape(x.shape[0] // SPAN, SPAN, x.shape[1])


def fold(x, reduce):
    return reduce(x.reshape(x.shape[0] // 8, 8, x.shape[1]), axis=0)


def main_kernel(
    count, q, g, k, v, lens, assign, attn, dq, dk, dv,
    lens_v, assign_s, padded, qslot, gslot, kown, vown, kprev, vprev, qr, gr, qt, gt,
    ko, vo, kot, vot, kp, vp, kpt, vpt, bias, expo, dpo, pb, sb, oto, stat,
    part_p, part_o, sum_send, sum_near, far_send_buf, far_buf, own_send, own_near,
    o_mine, o_send, o_near, q_mine, q_send, q_near,
    arrived, loc_sem, far_ks, far_kr, far_vs, far_vr, rel_ks, rel_kr, rel_vs, rel_vr,
    near_s, near_r, p_s, p_r, f_s, f_r, o_s, o_r, oq_s, oq_r,
):
    me = lax.axis_index("seq")
    grp = lax.axis_index("grp")
    core = lax.rem(me, 2)
    other = 1 - core
    chip = me // 2
    beside = me + 1 - 2 * core
    has_prev = chip > 0
    has_next = chip < count // 2 - 1
    before = jnp.where(has_prev, me - 2, me)
    after = jnp.where(has_next, me + 2, me)
    width = q.shape[2] // 2
    heads = width // DIM

    def remote(src, dst, send, recv, device):
        return pltpu.make_async_remote_copy(
            src_ref=src, dst_ref=dst, send_sem=send, recv_sem=recv,
            device_id=(device, grp), device_id_type=MESH,
        )

    def columns(which):
        return pl.ds(pl.multiple_of(which * width, width), width)

    own_slots = pl.ds(2 * core, 2)
    local = [
        pltpu.make_async_copy(k, kown.at[own_slots], loc_sem.at[0]),
        pltpu.make_async_copy(v, vown.at[own_slots], loc_sem.at[1]),
        pltpu.make_async_copy(lens, lens_v, loc_sem.at[2]),
        pltpu.make_async_copy(assign, assign_s, loc_sem.at[3]),
        pltpu.make_async_copy(q.at[:, :, columns(core)], qslot.at[own_slots], loc_sem.at[4]),
        pltpu.make_async_copy(g.at[:, :, columns(core)], gslot.at[own_slots], loc_sem.at[5]),
    ]
    far_k = [remote(k.at[a], kprev.at[2 * core + a], far_ks.at[a], far_kr.at[a], after)
             for a in range(2)]
    far_v = [remote(v.at[a], vprev.at[2 * core + a], far_vs.at[a], far_vr.at[a], after)
             for a in range(2)]
    relay_k = [remote(kprev.at[2 * core + a], kprev.at[2 * core + a], rel_ks.at[a], rel_kr.at[a],
                      beside) for a in range(2)]
    relay_v = [remote(vprev.at[2 * core + a], vprev.at[2 * core + a], rel_vs.at[a], rel_vr.at[a],
                      beside) for a in range(2)]
    near = [
        remote(k, kown.at[own_slots], near_s.at[0], near_r.at[0], beside),
        remote(v, vown.at[own_slots], near_s.at[1], near_r.at[1], beside),
        remote(q.at[:, :, columns(other)], qslot.at[own_slots], near_s.at[2], near_r.at[2], beside),
        remote(g.at[:, :, columns(other)], gslot.at[own_slots], near_s.at[3], near_r.at[3], beside),
    ]

    barrier = pltpu.get_barrier_semaphore()
    pl.semaphore_signal(barrier, inc=1, device_id=(beside, grp), device_id_type=MESH)

    @pl.when(has_prev)
    def _():
        pl.semaphore_signal(barrier, inc=1, device_id=(before, grp), device_id_type=MESH)

    for copy in local[:4]:
        copy.start()
    pl.semaphore_wait(barrier, 1 + has_next.astype(jnp.int32))

    @pl.when(has_next)
    def _():
        pl.semaphore_signal(arrived, inc=1, device_id=(after, grp), device_id_type=MESH)
        for copy in far_k:
            copy.start()

    for copy in near[:2] + local[4:]:
        copy.start()

    docs = lens_v.shape[0]
    wide = padded.shape[1]
    padded[...] = jnp.zeros_like(padded)
    local[2].wait()
    padded[0:1, 0:docs] = lens_v[...].reshape(1, docs)
    length = padded[...]
    high = length >> 8
    low = length - (high << 8)
    row8 = lax.broadcasted_iota(jnp.int32, (8, wide), 0)
    both = jnp.where(row8 == 1, pltpu.roll(low, 1, 0), high).astype(F32).astype(BF16)
    until = lax.broadcasted_iota(jnp.int32, (wide, wide), 0)
    upto = lax.broadcasted_iota(jnp.int32, (wide, wide), 1)
    lower = jnp.where(upto <= until, 1.0, 0.0).astype(BF16)
    sums = dot(lower, both, NT)
    base = chip * (GROUP * SPAN)
    ends = sums[:, 0:1] * 256.0 + sums[:, 1:2] - base.astype(F32)
    least = -base.astype(F32)
    key_row = lax.broadcasted_iota(jnp.int32, (SPAN, SPAN), 0).astype(F32)
    query_col = lax.broadcasted_iota(jnp.int32, (SPAN, SPAN), 1).astype(F32)
    for j in range(GROUP):
        if j == 2:

            @pl.when(has_next)
            def _():
                for copy in far_v:
                    copy.start()

        pos = query_col[0:1] + float(j * SPAN)
        start = jnp.max(jnp.where(ends <= pos, ends, least), axis=0, keepdims=True)
        for b in range(GROUP + 1):
            key = b if b <= j else b - 1 - GROUP
            ok = key_row + float(key * SPAN) >= start
            if b == j:
                ok = ok & (key_row <= query_col)
            bias[j, b * SPAN : (b + 1) * SPAN] = jnp.where(ok, 0.0, -1e30)

    for copy in near[2:]:
        copy.start()

    local[3].wait()
    back = jnp.maximum(chip - 1, 0)
    here = [assign_s[s % 2, 2 * chip + s // 2] & (GROUP - 1) for s in range(GROUP)]
    there = [assign_s[s % 2, 2 * back + s // 2] & (GROUP - 1) for s in range(GROUP)]
    for copy in (local[0], local[1], local[4], local[5]):
        copy.wait()
    for copy in near:
        copy.wait_recv()
    for j in range(GROUP):
        slot = pick(here, j)
        rows = slice(j * SPAN, (j + 1) * SPAN)
        kb = kown[slot]
        vb = vown[slot]
        ko[rows] = kb
        vo[rows] = vb
        kot[:, rows] = kb.T
        vot[:, rows] = vb.T
        qb = qslot[slot]
        gb = gslot[slot]
        for h in range(heads):
            cols = slice(h * DIM, (h + 1) * DIM)
            qr[j, cols] = qb[:, cols]
            gr[j, cols] = gb[:, cols]
            qt[j, :, cols] = qb[:, cols].T
            gt[j, :, cols] = gb[:, cols].T

    scale = ROOT * math.log2(math.e)
    part_p[...] = jnp.zeros_like(part_p)
    part_o[...] = jnp.zeros_like(part_o)

    def scores(keys, j, first, n):
        s = dot(keys, qt[j], NN)
        top = None
        for at in range(0, n, PIECE):
            rows = slice(first + at, first + at + PIECE)
            piece = s[at : at + PIECE] * scale + every_head(bias[j, rows], heads)
            expo[j, rows] = piece
            top = fold(piece, jnp.max) if top is None else jnp.maximum(top, fold(piece, jnp.max))
        return jnp.max(top, axis=0, keepdims=True)

    def exponentials(j, first, n, top, low=None):
        total = None
        for at in range(0, n, PIECE):
            rows = slice(first + at, first + at + PIECE)
            e = jnp.exp2(expo[j, rows] - top)
            expo[j, rows] = e
            if low is not None:
                low[j, rows] = e.astype(BF16)
            total = fold(e, jnp.sum) if total is None else total + fold(e, jnp.sum)
        return jnp.sum(total, axis=0, keepdims=True)

    tops = []
    for j in range(GROUP):
        n = (j + 1) * SPAN
        tops.append(scores(ko[0:n], j, 0, n))
        dpo[j, 0:n] = dot(vo[0:n], gt[j], NN)
    for j in range(GROUP):
        n = (j + 1) * SPAN
        stat[j, 0:1] = tops[j]
        stat[j, 1:2] = exponentials(j, 0, n, tops[j], pb)
        oto[j] = dot(vot[:, 0:n], pb[j, 0:n], NN)

    @pl.when(has_prev)
    def _():
        pl.semaphore_wait(arrived, 1)
        for a in range(2):
            far_k[a].wait_recv()
            relay_k[a].start()
        for a in range(2):
            relay_k[a].wait_recv()

    @pl.when(jnp.logical_not(has_prev))
    def _():
        kprev[...] = jnp.zeros_like(kprev)
        vprev[...] = jnp.zeros_like(vprev)

    for i in range(GROUP):
        rows = slice(i * SPAN, (i + 1) * SPAN)
        kb = kprev[pick(there, i)]
        kp[rows] = kb
        kpt[:, rows] = kb.T

    tops = []
    for j in range(GROUP):
        top = scores(kp[j * SPAN :], j, (j + 1) * SPAN, (GROUP - j) * SPAN)
        tops.append(jnp.maximum(stat[j, 0:1], top))
    norms = []
    alphas = []
    for j in range(GROUP):
        total = exponentials(j, (j + 1) * SPAN, (GROUP - j) * SPAN, tops[j])
        shrink = jnp.exp2(stat[j, 0:1] - tops[j])
        r = 1.0 / (stat[j, 1:2] * shrink + total)
        norms.append(r)
        alphas.append(shrink * r)
        if j == 1:

            @pl.when(has_prev)
            def _():
                for a in range(2):
                    far_v[a].wait_recv()
                    relay_v[a].start()

    for j in range(GROUP):
        for at in range((j + 1) * SPAN, expo.shape[1], PIECE):
            rows = slice(at, at + PIECE)
            pr = expo[j, rows] * norms[j]
            expo[j, rows] = pr
            pb[j, rows] = pr.astype(BF16)

    @pl.when(has_prev)
    def _():
        for a in range(2):
            relay_v[a].wait_recv()

    for i in range(GROUP):
        rows = slice(i * SPAN, (i + 1) * SPAN)
        vb = vprev[pick(there, i)]
        vp[rows] = vb
        vpt[:, rows] = vb.T

    deltas = []

    def finish_out(j):
        out = oto[j] * alphas[j] + dot(vpt[:, j * SPAN :], pb[j, (j + 1) * SPAN :], NN)
        deltas.append(jnp.sum(out * gt[j].astype(F32), axis=0, keepdims=True))
        out = out.astype(BF16)
        for h in range(heads):
            cols = slice(h * DIM, (h + 1) * DIM)
            o_mine[j, :, cols] = out[:, cols].T

    def prev_dprobs(j):
        return dot(vp[j * SPAN :], gt[j], NN)

    def prev_grads(j, dp):
        at = (j + 1) * SPAN
        for p in range(0, dp.shape[0], PIECE):
            rows = slice(at + p, at + p + PIECE)
            sb[j, rows] = (expo[j, rows] * (dp[p : p + PIECE] - deltas[j])).astype(BF16)
        part_p[j:, :, 0:DIM] += spans(dot(sb[j, at:], qr[j], NN) * ROOT)
        part_p[j:, :, DIM:] += spans(dot(pb[j, at:], gr[j], NN))

    finish_out(0)
    dp = prev_dprobs(0)
    for j in range(1, GROUP):
        finish_out(j)
        next_dp = prev_dprobs(j)
        prev_grads(j - 1, dp)
        dp = next_dp
    prev_grads(GROUP - 1, dp)

    def mine_of(spans, a):
        return jnp.where(core == 0, spans[a], spans[2 + a])

    def theirs_of(spans, a):
        return jnp.where(core == 0, spans[2 + a], spans[a])

    swap_p = [remote(sum_send.at[a], sum_near.at[a], p_s.at[a], p_r.at[a], beside)
              for a in range(2)]
    far_p = [remote(far_send_buf.at[a], far_buf.at[a], f_s.at[a], f_r.at[a], before)
             for a in range(2)]
    for a in range(2):
        sum_send[a] = part_p[theirs_of(there, a)].astype(BF16)
        swap_p[a].start()

    swap_out = remote(o_send, o_near, oq_s.at[0], oq_r.at[0], beside)
    swap_dq = remote(q_send, q_near, oq_s.at[1], oq_r.at[1], beside)
    for a in range(2):
        o_send[a] = o_mine[theirs_of(here, a)]
    swap_out.start()

    def own_dscores(j):
        for at in range(0, (j + 1) * SPAN, PIECE):
            rows = slice(at, at + PIECE)
            pr = expo[j, rows] * alphas[j]
            pb[j, rows] = pr.astype(BF16)
            sb[j, rows] = (pr * (dpo[j, rows] - deltas[j])).astype(BF16)

    def query_grads(j):
        own = slice(0, (j + 1) * SPAN)
        at = (j + 1) * SPAN
        grad = dot(sb[j, own], ko[own], TN) + dot(sb[j, at:], kp[j * SPAN :], TN)
        grad = (grad * ROOT).astype(BF16)
        for h in range(heads):
            cols = slice(h * DIM, (h + 1) * DIM)
            q_mine[j, :, cols] = grad[cols]

    def own_grads(j):
        own = slice(0, (j + 1) * SPAN)
        part_o[0 : j + 1, :, 0:DIM] += spans(dot(sb[j, own], qr[j], NN) * ROOT)
        part_o[0 : j + 1, :, DIM:] += spans(dot(pb[j, own], gr[j], NN))

    own_dscores(0)
    for j in range(1, GROUP):
        own_dscores(j)
        query_grads(j - 1)
    query_grads(GROUP - 1)
    for a in range(2):
        q_send[a] = q_mine[theirs_of(here, a)]
    swap_dq.start()

    for a in range(2):
        swap_p[a].wait_recv()
        far_send_buf[a] = (
            part_p[mine_of(there, a)] + sum_near[a].astype(F32)).astype(BF16)

        @pl.when(has_prev)
        def _(a=a):
            far_p[a].start()

    for j in range(GROUP):
        own_grads(j)

    swap_o = [remote(own_send.at[a], own_near.at[a], o_s.at[a], o_r.at[a], beside)
              for a in range(2)]
    for a in range(2):
        own_send[a] = part_o[theirs_of(here, a)].astype(BF16)
        swap_o[a].start()

    for a in range(2):
        j = mine_of(here, a)
        attn[a, :, columns(core)] = o_mine[j]
        dq[a, :, columns(core)] = q_mine[j]
    swap_out.wait_recv()
    for a in range(2):
        attn[a, :, columns(other)] = o_near[a]
    swap_dq.wait_recv()
    for a in range(2):
        dq[a, :, columns(other)] = q_near[a]

    @pl.when(jnp.logical_not(has_next))
    def _():
        far_buf[...] = jnp.zeros_like(far_buf)

    for a in range(2):
        swap_o[a].wait_recv()

        @pl.when(has_next)
        def _(a=a):
            far_p[a].wait_recv()

        total = part_o[mine_of(here, a)] + own_near[a].astype(F32) + far_buf[a].astype(F32)
        dk[a] = total[:, 0:DIM].astype(BF16)
        dv[a] = total[:, DIM:].astype(BF16)

    for copy in near + swap_p + [swap_out, swap_dq] + swap_o:
        copy.wait_send()

    @pl.when(has_next)
    def _():
        for copy in far_k + far_v:
            copy.wait_send()

    @pl.when(has_prev)
    def _():
        for copy in relay_k + relay_v + far_p:
            copy.wait_send()


def store_kernel(*refs):
    n = (len(refs) - 1) // 2
    sem = refs[2 * n]
    copies = []
    for i in range(n):
        for a in range(2):
            copies.append(
                pltpu.make_async_copy(refs[i].at[a], refs[n + i].at[a], sem.at[len(copies)]))
    for copy in copies:
        copy.start()
    for copy in copies:
        copy.wait()


def shards(count, queries, keys, values, grad_out, lengths, assign):
    width = queries.shape[1]
    half = width // 2
    docs = lengths.shape[0]
    wide = -(-docs // 128) * 128
    hbm = pl.BlockSpec(memory_space=pltpu.HBM)
    vmem = pl.BlockSpec(memory_space=pltpu.VMEM)
    dma = pltpu.SemaphoreType.DMA
    shape = jax.ShapeDtypeStruct
    keyed = GROUP * SPAN
    seen = keyed + SPAN
    outs = (
        shape((2, SPAN, width), BF16),
        shape((2, SPAN, width), BF16),
        shape((2, SPAN, DIM), BF16),
        shape((2, SPAN, DIM), BF16),
    )
    results = pl.pallas_call(
        functools.partial(main_kernel, count),
        out_shape=outs,
        in_specs=[hbm] * 6,
        out_specs=(vmem,) * 4,
        scratch_shapes=[
            pltpu.VMEM((docs,), jnp.int32),
            pltpu.SMEM(assign.shape[::-1], jnp.int32),
            pltpu.VMEM((8, wide), jnp.int32),
            pltpu.VMEM((GROUP, SPAN, half), BF16),
            pltpu.VMEM((GROUP, SPAN, half), BF16),
            pltpu.VMEM((GROUP, SPAN, DIM), BF16),
            pltpu.VMEM((GROUP, SPAN, DIM), BF16),
            pltpu.VMEM((GROUP, SPAN, DIM), BF16),
            pltpu.VMEM((GROUP, SPAN, DIM), BF16),
            pltpu.VMEM((GROUP, half, DIM), BF16),
            pltpu.VMEM((GROUP, half, DIM), BF16),
            pltpu.VMEM((GROUP, DIM, half), BF16),
            pltpu.VMEM((GROUP, DIM, half), BF16),
            pltpu.VMEM((keyed, DIM), BF16),
            pltpu.VMEM((keyed, DIM), BF16),
            pltpu.VMEM((DIM, keyed), BF16),
            pltpu.VMEM((DIM, keyed), BF16),
            pltpu.VMEM((keyed, DIM), BF16),
            pltpu.VMEM((keyed, DIM), BF16),
            pltpu.VMEM((DIM, keyed), BF16),
            pltpu.VMEM((DIM, keyed), BF16),
            pltpu.VMEM((GROUP, seen, SPAN), F32),
            pltpu.VMEM((GROUP, seen, half), F32),
            pltpu.VMEM((GROUP, keyed, half), F32),
            pltpu.VMEM((GROUP, seen, half), BF16),
            pltpu.VMEM((GROUP, seen, half), BF16),
            pltpu.VMEM((GROUP, DIM, half), F32),
            pltpu.VMEM((GROUP, 8, half), F32),
            pltpu.VMEM((GROUP, SPAN, 2 * DIM), F32),
            pltpu.VMEM((GROUP, SPAN, 2 * DIM), F32),
            pltpu.VMEM((2, SPAN, 2 * DIM), BF16),
            pltpu.VMEM((2, SPAN, 2 * DIM), BF16),
            pltpu.VMEM((2, SPAN, 2 * DIM), BF16),
            pltpu.VMEM((2, SPAN, 2 * DIM), BF16),
            pltpu.VMEM((2, SPAN, 2 * DIM), BF16),
            pltpu.VMEM((2, SPAN, 2 * DIM), BF16),
            pltpu.VMEM((GROUP, SPAN, half), BF16),
            pltpu.VMEM((2, SPAN, half), BF16),
            pltpu.VMEM((2, SPAN, half), BF16),
            pltpu.VMEM((GROUP, SPAN, half), BF16),
            pltpu.VMEM((2, SPAN, half), BF16),
            pltpu.VMEM((2, SPAN, half), BF16),
            pltpu.SemaphoreType.REGULAR,
            dma((6,)),
            dma((2,)), dma((2,)), dma((2,)), dma((2,)),
            dma((2,)), dma((2,)), dma((2,)), dma((2,)),
            dma((4,)), dma((4,)),
            dma((2,)), dma((2,)), dma((2,)), dma((2,)), dma((2,)), dma((2,)),
            dma((2,)), dma((2,)),
        ],
        compiler_params=pltpu.CompilerParams(
            collective_id=0, has_side_effects=True, vmem_limit_bytes=40 * 2**20),
        name="attend",
    )(*[
        pltpu.with_memory_space_constraint(x, pltpu.HBM)
        for x in (
            queries.reshape(2, SPAN, width), grad_out.reshape(2, SPAN, width),
            keys.reshape(2, SPAN, DIM), values.reshape(2, SPAN, DIM), lengths, assign.T,
        )
    ])
    results = pl.pallas_call(
        store_kernel,
        out_shape=outs,
        in_specs=[pl.BlockSpec(memory_space=pltpu.VMEM)] * 4,
        out_specs=(hbm,) * 4,
        scratch_shapes=[dma((8,))],
        name="store",
    )(*[pltpu.with_memory_space_constraint(r, pltpu.VMEM) for r in results])
    return tuple(r.reshape(2 * SPAN, r.shape[2]) for r in results)


def solution(mesh):
    split = P("seq", "grp")
    return jax.shard_map(
        functools.partial(shards, mesh.shape["seq"]),
        mesh=mesh,
        in_specs=(split, split, split, split, P(), P()),
        out_specs=(split, split, split, split),
        check_vma=False,
    )
```

```python
import functools
import math

import jax
import jax.numpy as jnp
from jax import lax
from jax.experimental import pallas as pl
from jax.experimental.pallas import tpu as pltpu
from jax.sharding import PartitionSpec as P

MESH = pl.DeviceIdType.MESH
SPAN = 128
DIM = 128
GROUP = 4
F32 = jnp.float32
BF16 = jnp.bfloat16
NT = (((1,), (1,)), ((), ()))
NN = (((1,), (0,)), ((), ()))
TN = (((0,), (0,)), ((), ()))
ROOT = 1.0 / math.sqrt(DIM)
PIECE = 32


def dot(a, b, dims):
    return lax.dot_general(a, b, dims, preferred_element_type=F32)


def pick(values, wanted):
    index = jnp.int32(0)
    for i, value in enumerate(values):
        index = jnp.where(value == wanted, i, index)
    return index


def every_head(x, heads):
    return jnp.concatenate([x] * heads, axis=1)


def spans(x):
    return x.reshape(x.shape[0] // SPAN, SPAN, x.shape[1])


def fold(x, reduce):
    return reduce(x.reshape(x.shape[0] // 8, 8, x.shape[1]), axis=0)


def main_kernel(
    count, q, g, k, v, lens, assign, attn, dq, dk, dv,
    lens_v, assign_s, padded, qslot, gslot, kown, vown, kprev, vprev, qr, gr, qt, gt,
    ko, vo, kot, vot, kp, vp, kpt, vpt, bias, expo, dpo, pb, sb, oto, stat,
    part_p, part_o, sum_send, sum_near, far_send_buf, far_buf, own_send, own_near,
    o_mine, o_send, o_near, q_mine, q_send, q_near,
    arrived, loc_sem, far_ks, far_kr, far_vs, far_vr, rel_ks, rel_kr, rel_vs, rel_vr,
    near_s, near_r, p_s, p_r, f_s, f_r, o_s, o_r, oq_s, oq_r,
):
    me = lax.axis_index("seq")
    grp = lax.axis_index("grp")
    core = lax.rem(me, 2)
    other = 1 - core
    chip = me // 2
    beside = me + 1 - 2 * core
    has_prev = chip > 0
    has_next = chip < count // 2 - 1
    before = jnp.where(has_prev, me - 2, me)
    after = jnp.where(has_next, me + 2, me)
    width = q.shape[2] // 2
    heads = width // DIM

    def remote(src, dst, send, recv, device):
        return pltpu.make_async_remote_copy(
            src_ref=src, dst_ref=dst, send_sem=send, recv_sem=recv,
            device_id=(device, grp), device_id_type=MESH,
        )

    def columns(which):
        return pl.ds(pl.multiple_of(which * width, width), width)

    own_slots = pl.ds(2 * core, 2)
    local = [
        pltpu.make_async_copy(k, kown.at[own_slots], loc_sem.at[0]),
        pltpu.make_async_copy(v, vown.at[own_slots], loc_sem.at[1]),
        pltpu.make_async_copy(lens, lens_v, loc_sem.at[2]),
        pltpu.make_async_copy(assign, assign_s, loc_sem.at[3]),
        pltpu.make_async_copy(q.at[:, :, columns(core)], qslot.at[own_slots], loc_sem.at[4]),
        pltpu.make_async_copy(g.at[:, :, columns(core)], gslot.at[own_slots], loc_sem.at[5]),
    ]
    far_k = [remote(k.at[a], kprev.at[2 * core + a], far_ks.at[a], far_kr.at[a], after)
             for a in range(2)]
    far_v = [remote(v.at[a], vprev.at[2 * core + a], far_vs.at[a], far_vr.at[a], after)
             for a in range(2)]
    relay_k = [remote(kprev.at[2 * core + a], kprev.at[2 * core + a], rel_ks.at[a], rel_kr.at[a],
                      beside) for a in range(2)]
    relay_v = [remote(vprev.at[2 * core + a], vprev.at[2 * core + a], rel_vs.at[a], rel_vr.at[a],
                      beside) for a in range(2)]
    near = [
        remote(k, kown.at[own_slots], near_s.at[0], near_r.at[0], beside),
        remote(v, vown.at[own_slots], near_s.at[1], near_r.at[1], beside),
        remote(q.at[:, :, columns(other)], qslot.at[own_slots], near_s.at[2], near_r.at[2], beside),
        remote(g.at[:, :, columns(other)], gslot.at[own_slots], near_s.at[3], near_r.at[3], beside),
    ]

    barrier = pltpu.get_barrier_semaphore()
    pl.semaphore_signal(barrier, inc=1, device_id=(beside, grp), device_id_type=MESH)

    @pl.when(has_prev)
    def _():
        pl.semaphore_signal(barrier, inc=1, device_id=(before, grp), device_id_type=MESH)

    for copy in local[:4]:
        copy.start()
    pl.semaphore_wait(barrier, 1 + has_next.astype(jnp.int32))

    @pl.when(has_next)
    def _():
        pl.semaphore_signal(arrived, inc=1, device_id=(after, grp), device_id_type=MESH)
        for copy in far_k:
            copy.start()

    for copy in near[:2] + local[4:]:
        copy.start()

    docs = lens_v.shape[0]
    wide = padded.shape[1]
    padded[...] = jnp.zeros_like(padded)
    local[2].wait()
    padded[0:1, 0:docs] = lens_v[...].reshape(1, docs)
    length = padded[...]
    high = length >> 8
    low = length - (high << 8)
    row8 = lax.broadcasted_iota(jnp.int32, (8, wide), 0)
    both = jnp.where(row8 == 1, pltpu.roll(low, 1, 0), high).astype(F32).astype(BF16)
    until = lax.broadcasted_iota(jnp.int32, (wide, wide), 0)
    upto = lax.broadcasted_iota(jnp.int32, (wide, wide), 1)
    lower = jnp.where(upto <= until, 1.0, 0.0).astype(BF16)
    sums = dot(lower, both, NT)
    base = chip * (GROUP * SPAN)
    ends = sums[:, 0:1] * 256.0 + sums[:, 1:2] - base.astype(F32)
    least = -base.astype(F32)
    key_row = lax.broadcasted_iota(jnp.int32, (SPAN, SPAN), 0).astype(F32)
    query_col = lax.broadcasted_iota(jnp.int32, (SPAN, SPAN), 1).astype(F32)
    for j in range(GROUP):
        if j == 2:

            @pl.when(has_next)
            def _():
                for copy in far_v:
                    copy.start()

        pos = query_col[0:1] + float(j * SPAN)
        start = jnp.max(jnp.where(ends <= pos, ends, least), axis=0, keepdims=True)
        for b in range(GROUP + 1):
            key = b if b <= j else b - 1 - GROUP
            ok = key_row + float(key * SPAN) >= start
            if b == j:
                ok = ok & (key_row <= query_col)
            bias[j, b * SPAN : (b + 1) * SPAN] = jnp.where(ok, 0.0, -1e30)

    for copy in near[2:]:
        copy.start()

    local[3].wait()
    back = jnp.maximum(chip - 1, 0)
    here = [assign_s[s % 2, 2 * chip + s // 2] & (GROUP - 1) for s in range(GROUP)]
    there = [assign_s[s % 2, 2 * back + s // 2] & (GROUP - 1) for s in range(GROUP)]
    for copy in (local[0], local[1], local[4], local[5]):
        copy.wait()
    for copy in near:
        copy.wait_recv()
    for j in range(GROUP):
        slot = pick(here, j)
        rows = slice(j * SPAN, (j + 1) * SPAN)
        kb = kown[slot]
        vb = vown[slot]
        ko[rows] = kb
        vo[rows] = vb
        kot[:, rows] = kb.T
        vot[:, rows] = vb.T
        qb = qslot[slot]
        gb = gslot[slot]
        for h in range(heads):
            cols = slice(h * DIM, (h + 1) * DIM)
            qr[j, cols] = qb[:, cols]
            gr[j, cols] = gb[:, cols]
            qt[j, :, cols] = qb[:, cols].T
            gt[j, :, cols] = gb[:, cols].T

    scale = ROOT * math.log2(math.e)
    part_p[...] = jnp.zeros_like(part_p)
    part_o[...] = jnp.zeros_like(part_o)

    def scores(keys, j, first, n):
        s = dot(keys, qt[j], NN)
        top = None
        for at in range(0, n, PIECE):
            rows = slice(first + at, first + at + PIECE)
            piece = s[at : at + PIECE] * scale + every_head(bias[j, rows], heads)
            expo[j, rows] = piece
            top = fold(piece, jnp.max) if top is None else jnp.maximum(top, fold(piece, jnp.max))
        return jnp.max(top, axis=0, keepdims=True)

    def exponentials(j, first, n, top, low=None):
        total = None
        for at in range(0, n, PIECE):
            rows = slice(first + at, first + at + PIECE)
            e = jnp.exp2(expo[j, rows] - top)
            expo[j, rows] = e
            if low is not None:
                low[j, rows] = e.astype(BF16)
            total = fold(e, jnp.sum) if total is None else total + fold(e, jnp.sum)
        return jnp.sum(total, axis=0, keepdims=True)

    tops = []
    for j in range(GROUP):
        n = (j + 1) * SPAN
        tops.append(scores(ko[0:n], j, 0, n))
        dpo[j, 0:n] = dot(vo[0:n], gt[j], NN)
    for j in range(GROUP):
        n = (j + 1) * SPAN
        stat[j, 0:1] = tops[j]
        stat[j, 1:2] = exponentials(j, 0, n, tops[j], pb)
        oto[j] = dot(vot[:, 0:n], pb[j, 0:n], NN)

    @pl.when(has_prev)
    def _():
        pl.semaphore_wait(arrived, 1)
        for a in range(2):
            far_k[a].wait_recv()
            relay_k[a].start()
        for a in range(2):
            relay_k[a].wait_recv()

    @pl.when(jnp.logical_not(has_prev))
    def _():
        kprev[...] = jnp.zeros_like(kprev)
        vprev[...] = jnp.zeros_like(vprev)

    for i in range(GROUP):
        rows = slice(i * SPAN, (i + 1) * SPAN)
        kb = kprev[pick(there, i)]
        kp[rows] = kb
        kpt[:, rows] = kb.T

    tops = []
    for j in range(GROUP):
        top = scores(kp[j * SPAN :], j, (j + 1) * SPAN, (GROUP - j) * SPAN)
        tops.append(jnp.maximum(stat[j, 0:1], top))
    norms = []
    alphas = []
    for j in range(GROUP):
        total = exponentials(j, (j + 1) * SPAN, (GROUP - j) * SPAN, tops[j])
        shrink = jnp.exp2(stat[j, 0:1] - tops[j])
        r = 1.0 / (stat[j, 1:2] * shrink + total)
        norms.append(r)
        alphas.append(shrink * r)
        if j == 1:

            @pl.when(has_prev)
            def _():
                for a in range(2):
                    far_v[a].wait_recv()
                    relay_v[a].start()

    for j in range(GROUP):
        for at in range((j + 1) * SPAN, expo.shape[1], PIECE):
            rows = slice(at, at + PIECE)
            pr = expo[j, rows] * norms[j]
            expo[j, rows] = pr
            pb[j, rows] = pr.astype(BF16)

    for j in range(GROUP):
        own = slice(0, (j + 1) * SPAN)
        part_p[j:, :, DIM:] += spans(dot(pb[j, (j + 1) * SPAN :], gr[j], NN))
        for at in range(0, (j + 1) * SPAN, PIECE):
            rows = slice(at, at + PIECE)
            pr = expo[j, rows] * alphas[j]
            expo[j, rows] = pr
            pb[j, rows] = pr.astype(BF16)
        part_o[0 : j + 1, :, DIM:] += spans(dot(pb[j, own], gr[j], NN))

    @pl.when(has_prev)
    def _():
        for a in range(2):
            relay_v[a].wait_recv()

    for i in range(GROUP):
        rows = slice(i * SPAN, (i + 1) * SPAN)
        vb = vprev[pick(there, i)]
        vp[rows] = vb
        vpt[:, rows] = vb.T

    deltas = []

    def finish_out(j):
        out = oto[j] * alphas[j] + dot(vpt[:, j * SPAN :], pb[j, (j + 1) * SPAN :], NN)
        deltas.append(jnp.sum(out * gt[j].astype(F32), axis=0, keepdims=True))
        out = out.astype(BF16)
        for h in range(heads):
            cols = slice(h * DIM, (h + 1) * DIM)
            o_mine[j, :, cols] = out[:, cols].T

    def prev_dprobs(j):
        return dot(vp[j * SPAN :], gt[j], NN)

    def prev_grads(j, dp):
        at = (j + 1) * SPAN
        for p in range(0, dp.shape[0], PIECE):
            rows = slice(at + p, at + p + PIECE)
            sb[j, rows] = (expo[j, rows] * (dp[p : p + PIECE] - deltas[j])).astype(BF16)
        part_p[j:, :, 0:DIM] += spans(dot(sb[j, at:], qr[j], NN) * ROOT)

    finish_out(0)
    dp = prev_dprobs(0)
    for j in range(1, GROUP):
        finish_out(j)
        next_dp = prev_dprobs(j)
        prev_grads(j - 1, dp)
        dp = next_dp
    prev_grads(GROUP - 1, dp)

    def mine_of(spans, a):
        return jnp.where(core == 0, spans[a], spans[2 + a])

    def theirs_of(spans, a):
        return jnp.where(core == 0, spans[2 + a], spans[a])

    swap_p = [remote(sum_send.at[a], sum_near.at[a], p_s.at[a], p_r.at[a], beside)
              for a in range(2)]
    far_p = [remote(far_send_buf.at[a], far_buf.at[a], f_s.at[a], f_r.at[a], before)
             for a in range(2)]
    for a in range(2):
        sum_send[a] = part_p[theirs_of(there, a)].astype(BF16)
        swap_p[a].start()

    swap_out = remote(o_send, o_near, oq_s.at[0], oq_r.at[0], beside)
    swap_dq = remote(q_send, q_near, oq_s.at[1], oq_r.at[1], beside)
    for a in range(2):
        o_send[a] = o_mine[theirs_of(here, a)]
    swap_out.start()

    def own_dscores(j):
        for at in range(0, (j + 1) * SPAN, PIECE):
            rows = slice(at, at + PIECE)
            sb[j, rows] = (expo[j, rows] * (dpo[j, rows] - deltas[j])).astype(BF16)

    def query_grads(j):
        own = slice(0, (j + 1) * SPAN)
        at = (j + 1) * SPAN
        grad = dot(sb[j, own], ko[own], TN) + dot(sb[j, at:], kp[j * SPAN :], TN)
        grad = (grad * ROOT).astype(BF16)
        for h in range(heads):
            cols = slice(h * DIM, (h + 1) * DIM)
            q_mine[j, :, cols] = grad[cols]

    def own_grads(j):
        own = slice(0, (j + 1) * SPAN)
        part_o[0 : j + 1, :, 0:DIM] += spans(dot(sb[j, own], qr[j], NN) * ROOT)

    own_dscores(0)
    for j in range(1, GROUP):
        own_dscores(j)
        query_grads(j - 1)
    query_grads(GROUP - 1)
    for a in range(2):
        q_send[a] = q_mine[theirs_of(here, a)]
    swap_dq.start()

    for a in range(2):
        swap_p[a].wait_recv()
        far_send_buf[a] = (
            part_p[mine_of(there, a)] + sum_near[a].astype(F32)).astype(BF16)

        @pl.when(has_prev)
        def _(a=a):
            far_p[a].start()

    for j in range(GROUP):
        own_grads(j)

    swap_o = [remote(own_send.at[a], own_near.at[a], o_s.at[a], o_r.at[a], beside)
              for a in range(2)]
    for a in range(2):
        own_send[a] = part_o[theirs_of(here, a)].astype(BF16)
        swap_o[a].start()

    for a in range(2):
        j = mine_of(here, a)
        attn[a, :, columns(core)] = o_mine[j]
        dq[a, :, columns(core)] = q_mine[j]
    swap_out.wait_recv()
    for a in range(2):
        attn[a, :, columns(other)] = o_near[a]
    swap_dq.wait_recv()
    for a in range(2):
        dq[a, :, columns(other)] = q_near[a]

    @pl.when(jnp.logical_not(has_next))
    def _():
        far_buf[...] = jnp.zeros_like(far_buf)

    for a in range(2):
        swap_o[a].wait_recv()

        @pl.when(has_next)
        def _(a=a):
            far_p[a].wait_recv()

        total = part_o[mine_of(here, a)] + own_near[a].astype(F32) + far_buf[a].astype(F32)
        dk[a] = total[:, 0:DIM].astype(BF16)
        dv[a] = total[:, DIM:].astype(BF16)

    for copy in near + swap_p + [swap_out, swap_dq] + swap_o:
        copy.wait_send()

    @pl.when(has_next)
    def _():
        for copy in far_k + far_v:
            copy.wait_send()

    @pl.when(has_prev)
    def _():
        for copy in relay_k + relay_v + far_p:
            copy.wait_send()


def store_kernel(*refs):
    n = (len(refs) - 1) // 2
    sem = refs[2 * n]
    copies = []
    for i in range(n):
        for a in range(2):
            copies.append(
                pltpu.make_async_copy(refs[i].at[a], refs[n + i].at[a], sem.at[len(copies)]))
    for copy in copies:
        copy.start()
    for copy in copies:
        copy.wait()


def shards(count, queries, keys, values, grad_out, lengths, assign):
    width = queries.shape[1]
    half = width // 2
    docs = lengths.shape[0]
    wide = -(-docs // 128) * 128
    hbm = pl.BlockSpec(memory_space=pltpu.HBM)
    vmem = pl.BlockSpec(memory_space=pltpu.VMEM)
    dma = pltpu.SemaphoreType.DMA
    shape = jax.ShapeDtypeStruct
    keyed = GROUP * SPAN
    seen = keyed + SPAN
    outs = (
        shape((2, SPAN, width), BF16),
        shape((2, SPAN, width), BF16),
        shape((2, SPAN, DIM), BF16),
        shape((2, SPAN, DIM), BF16),
    )
    results = pl.pallas_call(
        functools.partial(main_kernel, count),
        out_shape=outs,
        in_specs=[hbm] * 6,
        out_specs=(vmem,) * 4,
        scratch_shapes=[
            pltpu.VMEM((docs,), jnp.int32),
            pltpu.SMEM(assign.shape[::-1], jnp.int32),
            pltpu.VMEM((8, wide), jnp.int32),
            pltpu.VMEM((GROUP, SPAN, half), BF16),
            pltpu.VMEM((GROUP, SPAN, half), BF16),
            pltpu.VMEM((GROUP, SPAN, DIM), BF16),
            pltpu.VMEM((GROUP, SPAN, DIM), BF16),
            pltpu.VMEM((GROUP, SPAN, DIM), BF16),
            pltpu.VMEM((GROUP, SPAN, DIM), BF16),
            pltpu.VMEM((GROUP, half, DIM), BF16),
            pltpu.VMEM((GROUP, half, DIM), BF16),
            pltpu.VMEM((GROUP, DIM, half), BF16),
            pltpu.VMEM((GROUP, DIM, half), BF16),
            pltpu.VMEM((keyed, DIM), BF16),
            pltpu.VMEM((keyed, DIM), BF16),
            pltpu.VMEM((DIM, keyed), BF16),
            pltpu.VMEM((DIM, keyed), BF16),
            pltpu.VMEM((keyed, DIM), BF16),
            pltpu.VMEM((keyed, DIM), BF16),
            pltpu.VMEM((DIM, keyed), BF16),
            pltpu.VMEM((DIM, keyed), BF16),
            pltpu.VMEM((GROUP, seen, SPAN), F32),
            pltpu.VMEM((GROUP, seen, half), F32),
            pltpu.VMEM((GROUP, keyed, half), F32),
            pltpu.VMEM((GROUP, seen, half), BF16),
            pltpu.VMEM((GROUP, seen, half), BF16),
            pltpu.VMEM((GROUP, DIM, half), F32),
            pltpu.VMEM((GROUP, 8, half), F32),
            pltpu.VMEM((GROUP, SPAN, 2 * DIM), F32),
            pltpu.VMEM((GROUP, SPAN, 2 * DIM), F32),
            pltpu.VMEM((2, SPAN, 2 * DIM), BF16),
            pltpu.VMEM((2, SPAN, 2 * DIM), BF16),
            pltpu.VMEM((2, SPAN, 2 * DIM), BF16),
            pltpu.VMEM((2, SPAN, 2 * DIM), BF16),
            pltpu.VMEM((2, SPAN, 2 * DIM), BF16),
            pltpu.VMEM((2, SPAN, 2 * DIM), BF16),
            pltpu.VMEM((GROUP, SPAN, half), BF16),
            pltpu.VMEM((2, SPAN, half), BF16),
            pltpu.VMEM((2, SPAN, half), BF16),
            pltpu.VMEM((GROUP, SPAN, half), BF16),
            pltpu.VMEM((2, SPAN, half), BF16),
            pltpu.VMEM((2, SPAN, half), BF16),
            pltpu.SemaphoreType.REGULAR,
            dma((6,)),
            dma((2,)), dma((2,)), dma((2,)), dma((2,)),
            dma((2,)), dma((2,)), dma((2,)), dma((2,)),
            dma((4,)), dma((4,)),
            dma((2,)), dma((2,)), dma((2,)), dma((2,)), dma((2,)), dma((2,)),
            dma((2,)), dma((2,)),
        ],
        compiler_params=pltpu.CompilerParams(
            collective_id=0, has_side_effects=True, vmem_limit_bytes=40 * 2**20),
        name="attend",
    )(*[
        pltpu.with_memory_space_constraint(x, pltpu.HBM)
        for x in (
            queries.reshape(2, SPAN, width), grad_out.reshape(2, SPAN, width),
            keys.reshape(2, SPAN, DIM), values.reshape(2, SPAN, DIM), lengths, assign.T,
        )
    ])
    results = pl.pallas_call(
        store_kernel,
        out_shape=outs,
        in_specs=[pl.BlockSpec(memory_space=pltpu.VMEM)] * 4,
        out_specs=(hbm,) * 4,
        scratch_shapes=[dma((8,))],
        name="store",
    )(*[pltpu.with_memory_space_constraint(r, pltpu.VMEM) for r in results])
    return tuple(r.reshape(2 * SPAN, r.shape[2]) for r in results)


def solution(mesh):
    split = P("seq", "grp")
    return jax.shard_map(
        functools.partial(shards, mesh.shape["seq"]),
        mesh=mesh,
        in_specs=(split, split, split, split, P(), P()),
        out_specs=(split, split, split, split),
        check_vma=False,
    )
```

```python
import functools
import math

import jax
import jax.numpy as jnp
from jax import lax
from jax.experimental import pallas as pl
from jax.experimental.pallas import tpu as pltpu
from jax.sharding import PartitionSpec as P

MESH = pl.DeviceIdType.MESH
SPAN = 128
DIM = 128
GROUP = 4
F32 = jnp.float32
BF16 = jnp.bfloat16
NT = (((1,), (1,)), ((), ()))
NN = (((1,), (0,)), ((), ()))
TN = (((0,), (0,)), ((), ()))
ROOT = 1.0 / math.sqrt(DIM)
PIECE = 32


def dot(a, b, dims):
    return lax.dot_general(a, b, dims, preferred_element_type=F32)


def pick(values, wanted):
    index = jnp.int32(0)
    for i, value in enumerate(values):
        index = jnp.where(value == wanted, i, index)
    return index


def every_head(x, heads):
    return jnp.concatenate([x] * heads, axis=1)


def spans(x):
    return x.reshape(x.shape[0] // SPAN, SPAN, x.shape[1])


def fold(x, reduce):
    return reduce(x.reshape(x.shape[0] // 8, 8, x.shape[1]), axis=0)


def main_kernel(
    count, q, g, k, v, lens, assign, attn, dq, dk, dv,
    lens_v, assign_s, padded, qslot, gslot, kown, vown, kprev, vprev, qr, gr, qt, gt,
    ko, vo, kot, vot, kp, vp, kpt, vpt, bias, expo, dpo, pb, sb, oto, stat,
    part_p, part_o, sum_send, sum_near, far_send_buf, far_buf, own_send, own_near,
    o_mine, o_send, o_near, q_mine, q_send, q_near,
    arrived, loc_sem, far_ks, far_kr, far_vs, far_vr, rel_ks, rel_kr, rel_vs, rel_vr,
    near_s, near_r, p_s, p_r, f_s, f_r, o_s, o_r, oq_s, oq_r,
):
    me = lax.axis_index("seq")
    grp = lax.axis_index("grp")
    core = lax.rem(me, 2)
    other = 1 - core
    chip = me // 2
    beside = me + 1 - 2 * core
    has_prev = chip > 0
    has_next = chip < count // 2 - 1
    before = jnp.where(has_prev, me - 2, me)
    after = jnp.where(has_next, me + 2, me)
    width = q.shape[2] // 2
    heads = width // DIM

    def remote(src, dst, send, recv, device):
        return pltpu.make_async_remote_copy(
            src_ref=src, dst_ref=dst, send_sem=send, recv_sem=recv,
            device_id=(device, grp), device_id_type=MESH,
        )

    def columns(which):
        return pl.ds(pl.multiple_of(which * width, width), width)

    own_slots = pl.ds(2 * core, 2)
    local = [
        pltpu.make_async_copy(k, kown.at[own_slots], loc_sem.at[0]),
        pltpu.make_async_copy(v, vown.at[own_slots], loc_sem.at[1]),
        pltpu.make_async_copy(lens, lens_v, loc_sem.at[2]),
        pltpu.make_async_copy(assign, assign_s, loc_sem.at[3]),
        pltpu.make_async_copy(q.at[:, :, columns(core)], qslot.at[own_slots], loc_sem.at[4]),
        pltpu.make_async_copy(g.at[:, :, columns(core)], gslot.at[own_slots], loc_sem.at[5]),
    ]
    far_k = [remote(k.at[a], kprev.at[2 * core + a], far_ks.at[a], far_kr.at[a], after)
             for a in range(2)]
    far_v = [remote(v.at[a], vprev.at[2 * core + a], far_vs.at[a], far_vr.at[a], after)
             for a in range(2)]
    relay_k = [remote(kprev.at[2 * core + a], kprev.at[2 * core + a], rel_ks.at[a], rel_kr.at[a],
                      beside) for a in range(2)]
    relay_v = [remote(vprev.at[2 * core + a], vprev.at[2 * core + a], rel_vs.at[a], rel_vr.at[a],
                      beside) for a in range(2)]
    near = [
        remote(k, kown.at[own_slots], near_s.at[0], near_r.at[0], beside),
        remote(v, vown.at[own_slots], near_s.at[1], near_r.at[1], beside),
        remote(q.at[:, :, columns(other)], qslot.at[own_slots], near_s.at[2], near_r.at[2], beside),
        remote(g.at[:, :, columns(other)], gslot.at[own_slots], near_s.at[3], near_r.at[3], beside),
    ]

    barrier = pltpu.get_barrier_semaphore()
    pl.semaphore_signal(barrier, inc=1, device_id=(beside, grp), device_id_type=MESH)

    @pl.when(has_prev)
    def _():
        pl.semaphore_signal(barrier, inc=1, device_id=(before, grp), device_id_type=MESH)

    for copy in local[:4]:
        copy.start()
    pl.semaphore_wait(barrier, 1 + has_next.astype(jnp.int32))

    @pl.when(has_next)
    def _():
        pl.semaphore_signal(arrived, inc=1, device_id=(after, grp), device_id_type=MESH)
        for copy in far_k:
            copy.start()

    for copy in near[:2] + local[4:]:
        copy.start()

    docs = lens_v.shape[0]
    wide = padded.shape[1]
    padded[...] = jnp.zeros_like(padded)
    local[2].wait()
    padded[0:1, 0:docs] = lens_v[...].reshape(1, docs)
    length = padded[...]
    high = length >> 8
    low = length - (high << 8)
    row8 = lax.broadcasted_iota(jnp.int32, (8, wide), 0)
    both = jnp.where(row8 == 1, pltpu.roll(low, 1, 0), high).astype(F32).astype(BF16)
    until = lax.broadcasted_iota(jnp.int32, (wide, wide), 0)
    upto = lax.broadcasted_iota(jnp.int32, (wide, wide), 1)
    lower = jnp.where(upto <= until, 1.0, 0.0).astype(BF16)
    sums = dot(lower, both, NT)
    base = chip * (GROUP * SPAN)
    ends = sums[:, 0:1] * 256.0 + sums[:, 1:2] - base.astype(F32)
    least = -base.astype(F32)
    key_row = lax.broadcasted_iota(jnp.int32, (SPAN, SPAN), 0).astype(F32)
    query_col = lax.broadcasted_iota(jnp.int32, (SPAN, SPAN), 1).astype(F32)
    for j in range(GROUP):
        if j == 2:

            @pl.when(has_next)
            def _():
                for copy in far_v:
                    copy.start()

        pos = query_col[0:1] + float(j * SPAN)
        start = jnp.max(jnp.where(ends <= pos, ends, least), axis=0, keepdims=True)
        for b in range(GROUP + 1):
            key = b if b <= j else b - 1 - GROUP
            ok = key_row + float(key * SPAN) >= start
            if b == j:
                ok = ok & (key_row <= query_col)
            bias[j, b * SPAN : (b + 1) * SPAN] = jnp.where(ok, 0.0, -1e30)

    for copy in near[2:]:
        copy.start()

    local[3].wait()
    back = jnp.maximum(chip - 1, 0)
    here = [assign_s[s % 2, 2 * chip + s // 2] & (GROUP - 1) for s in range(GROUP)]
    there = [assign_s[s % 2, 2 * back + s // 2] & (GROUP - 1) for s in range(GROUP)]
    for copy in (local[0], local[1], local[4], local[5]):
        copy.wait()
    for copy in near:
        copy.wait_recv()
    for j in range(GROUP):
        slot = pick(here, j)
        rows = slice(j * SPAN, (j + 1) * SPAN)
        kb = kown[slot]
        vb = vown[slot]
        ko[rows] = kb
        vo[rows] = vb
        kot[:, rows] = kb.T
        vot[:, rows] = vb.T
        qb = qslot[slot]
        gb = gslot[slot]
        for h in range(heads):
            cols = slice(h * DIM, (h + 1) * DIM)
            qr[j, cols] = qb[:, cols]
            gr[j, cols] = gb[:, cols]
            qt[j, :, cols] = qb[:, cols].T
            gt[j, :, cols] = gb[:, cols].T

    scale = ROOT * math.log2(math.e)
    part_p[...] = jnp.zeros_like(part_p)
    part_o[...] = jnp.zeros_like(part_o)

    def scores(keys, j, first, n):
        s = dot(keys, qt[j], NN)
        top = None
        for at in range(0, n, PIECE):
            rows = slice(first + at, first + at + PIECE)
            piece = s[at : at + PIECE] * scale + every_head(bias[j, rows], heads)
            expo[j, rows] = piece
            top = fold(piece, jnp.max) if top is None else jnp.maximum(top, fold(piece, jnp.max))
        return jnp.max(top, axis=0, keepdims=True)

    def exponentials(j, first, n, top, low=None):
        total = None
        for at in range(0, n, PIECE):
            rows = slice(first + at, first + at + PIECE)
            e = jnp.exp2(expo[j, rows] - top)
            expo[j, rows] = e
            if low is not None:
                low[j, rows] = e.astype(BF16)
            total = fold(e, jnp.sum) if total is None else total + fold(e, jnp.sum)
        return jnp.sum(total, axis=0, keepdims=True)

    tops = []
    for j in range(GROUP):
        n = (j + 1) * SPAN
        tops.append(scores(ko[0:n], j, 0, n))
        dpo[j, 0:n] = dot(vo[0:n], gt[j], NN)
    for j in range(GROUP):
        n = (j + 1) * SPAN
        stat[j, 0:1] = tops[j]
        stat[j, 1:2] = exponentials(j, 0, n, tops[j], pb)
        oto[j] = dot(vot[:, 0:n], pb[j, 0:n], NN)

    @pl.when(has_prev)
    def _():
        pl.semaphore_wait(arrived, 1)
        for a in range(2):
            far_k[a].wait_recv()
            relay_k[a].start()
        for a in range(2):
            relay_k[a].wait_recv()

    @pl.when(jnp.logical_not(has_prev))
    def _():
        kprev[...] = jnp.zeros_like(kprev)
        vprev[...] = jnp.zeros_like(vprev)

    for i in range(GROUP):
        rows = slice(i * SPAN, (i + 1) * SPAN)
        kb = kprev[pick(there, i)]
        kp[rows] = kb
        kpt[:, rows] = kb.T

    tops = []
    for j in range(GROUP):
        top = scores(kp[j * SPAN :], j, (j + 1) * SPAN, (GROUP - j) * SPAN)
        tops.append(jnp.maximum(stat[j, 0:1], top))
    norms = []
    alphas = []
    for j in range(GROUP):
        total = exponentials(j, (j + 1) * SPAN, (GROUP - j) * SPAN, tops[j])
        shrink = jnp.exp2(stat[j, 0:1] - tops[j])
        r = 1.0 / (stat[j, 1:2] * shrink + total)
        norms.append(r)
        alphas.append(shrink * r)
        if j == 1:

            @pl.when(has_prev)
            def _():
                for a in range(2):
                    far_v[a].wait_recv()
                    relay_v[a].start()

    for j in range(GROUP):
        for at in range((j + 1) * SPAN, expo.shape[1], PIECE):
            rows = slice(at, at + PIECE)
            pr = expo[j, rows] * norms[j]
            expo[j, rows] = pr
            pb[j, rows] = pr.astype(BF16)

    @pl.when(has_prev)
    def _():
        for a in range(2):
            relay_v[a].wait_recv()

    for i in range(GROUP):
        rows = slice(i * SPAN, (i + 1) * SPAN)
        vb = vprev[pick(there, i)]
        vp[rows] = vb
        vpt[:, rows] = vb.T

    deltas = []

    def finish_out(j):
        out = oto[j] * alphas[j] + dot(vpt[:, j * SPAN :], pb[j, (j + 1) * SPAN :], NN)
        deltas.append(jnp.sum(out * gt[j].astype(F32), axis=0, keepdims=True))
        out = out.astype(BF16)
        for h in range(heads):
            cols = slice(h * DIM, (h + 1) * DIM)
            o_mine[j, :, cols] = out[:, cols].T

    def prev_dprobs(j):
        return dot(vp[j * SPAN :], gt[j], NN)

    def prev_grads(j, dp):
        at = (j + 1) * SPAN
        for p in range(0, dp.shape[0], PIECE):
            rows = slice(at + p, at + p + PIECE)
            sb[j, rows] = (expo[j, rows] * (dp[p : p + PIECE] - deltas[j])).astype(BF16)
        part_p[j:, :, 0:DIM] += spans(dot(sb[j, at:], qr[j], NN) * ROOT)
        part_p[j:, :, DIM:] += spans(dot(pb[j, at:], gr[j], NN))

    finish_out(0)
    dp = prev_dprobs(0)
    for j in range(1, GROUP):
        finish_out(j)
        next_dp = prev_dprobs(j)
        prev_grads(j - 1, dp)
        dp = next_dp
    prev_grads(GROUP - 1, dp)

    def mine_of(spans, a):
        return jnp.where(core == 0, spans[a], spans[2 + a])

    def theirs_of(spans, a):
        return jnp.where(core == 0, spans[2 + a], spans[a])

    swap_p = [remote(sum_send.at[a], sum_near.at[a], p_s.at[a], p_r.at[a], beside)
              for a in range(2)]
    far_p = [remote(far_send_buf.at[a], far_buf.at[a], f_s.at[a], f_r.at[a], before)
             for a in range(2)]
    for a in range(2):
        sum_send[a] = part_p[theirs_of(there, a)].astype(BF16)
        swap_p[a].start()

    swap_out = remote(o_send, o_near, oq_s.at[0], oq_r.at[0], beside)
    swap_dq = remote(q_send, q_near, oq_s.at[1], oq_r.at[1], beside)
    for a in range(2):
        o_send[a] = o_mine[theirs_of(here, a)]
    swap_out.start()

    def own_dscores(j):
        for at in range(0, (j + 1) * SPAN, PIECE):
            rows = slice(at, at + PIECE)
            pr = expo[j, rows] * alphas[j]
            pb[j, rows] = pr.astype(BF16)
            sb[j, rows] = (pr * (dpo[j, rows] - deltas[j])).astype(BF16)

    def query_grads(j):
        own = slice(0, (j + 1) * SPAN)
        at = (j + 1) * SPAN
        grad = dot(sb[j, own], ko[own], TN) + dot(sb[j, at:], kp[j * SPAN :], TN)
        grad = (grad * ROOT).astype(BF16)
        for h in range(heads):
            cols = slice(h * DIM, (h + 1) * DIM)
            q_mine[j, :, cols] = grad[cols]

    def own_grads(j):
        own = slice(0, (j + 1) * SPAN)
        part_o[0 : j + 1, :, 0:DIM] += spans(dot(sb[j, own], qr[j], NN) * ROOT)
        part_o[0 : j + 1, :, DIM:] += spans(dot(pb[j, own], gr[j], NN))

    own_dscores(0)
    for j in range(1, GROUP - 1):
        own_dscores(j)
        query_grads(j - 1)

    for a in range(2):
        swap_p[a].wait_recv()
        far_send_buf[a] = (
            part_p[mine_of(there, a)] + sum_near[a].astype(F32)).astype(BF16)

        @pl.when(has_prev)
        def _(a=a):
            far_p[a].start()

    own_dscores(GROUP - 1)
    query_grads(GROUP - 2)
    query_grads(GROUP - 1)
    for a in range(2):
        q_send[a] = q_mine[theirs_of(here, a)]
    swap_dq.start()

    for j in range(GROUP):
        own_grads(j)

    swap_o = [remote(own_send.at[a], own_near.at[a], o_s.at[a], o_r.at[a], beside)
              for a in range(2)]
    for a in range(2):
        own_send[a] = part_o[theirs_of(here, a)].astype(BF16)
        swap_o[a].start()

    for a in range(2):
        j = mine_of(here, a)
        attn[a, :, columns(core)] = o_mine[j]
        dq[a, :, columns(core)] = q_mine[j]
    swap_out.wait_recv()
    for a in range(2):
        attn[a, :, columns(other)] = o_near[a]
    swap_dq.wait_recv()
    for a in range(2):
        dq[a, :, columns(other)] = q_near[a]

    @pl.when(jnp.logical_not(has_next))
    def _():
        far_buf[...] = jnp.zeros_like(far_buf)

    for a in range(2):
        swap_o[a].wait_recv()

        @pl.when(has_next)
        def _(a=a):
            far_p[a].wait_recv()

        total = part_o[mine_of(here, a)] + own_near[a].astype(F32) + far_buf[a].astype(F32)
        dk[a] = total[:, 0:DIM].astype(BF16)
        dv[a] = total[:, DIM:].astype(BF16)

    for copy in near + swap_p + [swap_out, swap_dq] + swap_o:
        copy.wait_send()

    @pl.when(has_next)
    def _():
        for copy in far_k + far_v:
            copy.wait_send()

    @pl.when(has_prev)
    def _():
        for copy in relay_k + relay_v + far_p:
            copy.wait_send()


def store_kernel(*refs):
    n = (len(refs) - 1) // 2
    sem = refs[2 * n]
    copies = []
    for i in range(n):
        for a in range(2):
            copies.append(
                pltpu.make_async_copy(refs[i].at[a], refs[n + i].at[a], sem.at[len(copies)]))
    for copy in copies:
        copy.start()
    for copy in copies:
        copy.wait()


def shards(count, queries, keys, values, grad_out, lengths, assign):
    width = queries.shape[1]
    half = width // 2
    docs = lengths.shape[0]
    wide = -(-docs // 128) * 128
    hbm = pl.BlockSpec(memory_space=pltpu.HBM)
    vmem = pl.BlockSpec(memory_space=pltpu.VMEM)
    dma = pltpu.SemaphoreType.DMA
    shape = jax.ShapeDtypeStruct
    keyed = GROUP * SPAN
    seen = keyed + SPAN
    outs = (
        shape((2, SPAN, width), BF16),
        shape((2, SPAN, width), BF16),
        shape((2, SPAN, DIM), BF16),
        shape((2, SPAN, DIM), BF16),
    )
    results = pl.pallas_call(
        functools.partial(main_kernel, count),
        out_shape=outs,
        in_specs=[hbm] * 6,
        out_specs=(vmem,) * 4,
        scratch_shapes=[
            pltpu.VMEM((docs,), jnp.int32),
            pltpu.SMEM(assign.shape[::-1], jnp.int32),
            pltpu.VMEM((8, wide), jnp.int32),
            pltpu.VMEM((GROUP, SPAN, half), BF16),
            pltpu.VMEM((GROUP, SPAN, half), BF16),
            pltpu.VMEM((GROUP, SPAN, DIM), BF16),
            pltpu.VMEM((GROUP, SPAN, DIM), BF16),
            pltpu.VMEM((GROUP, SPAN, DIM), BF16),
            pltpu.VMEM((GROUP, SPAN, DIM), BF16),
            pltpu.VMEM((GROUP, half, DIM), BF16),
            pltpu.VMEM((GROUP, half, DIM), BF16),
            pltpu.VMEM((GROUP, DIM, half), BF16),
            pltpu.VMEM((GROUP, DIM, half), BF16),
            pltpu.VMEM((keyed, DIM), BF16),
            pltpu.VMEM((keyed, DIM), BF16),
            pltpu.VMEM((DIM, keyed), BF16),
            pltpu.VMEM((DIM, keyed), BF16),
            pltpu.VMEM((keyed, DIM), BF16),
            pltpu.VMEM((keyed, DIM), BF16),
            pltpu.VMEM((DIM, keyed), BF16),
            pltpu.VMEM((DIM, keyed), BF16),
            pltpu.VMEM((GROUP, seen, SPAN), F32),
            pltpu.VMEM((GROUP, seen, half), F32),
            pltpu.VMEM((GROUP, keyed, half), F32),
            pltpu.VMEM((GROUP, seen, half), BF16),
            pltpu.VMEM((GROUP, seen, half), BF16),
            pltpu.VMEM((GROUP, DIM, half), F32),
            pltpu.VMEM((GROUP, 8, half), F32),
            pltpu.VMEM((GROUP, SPAN, 2 * DIM), F32),
            pltpu.VMEM((GROUP, SPAN, 2 * DIM), F32),
            pltpu.VMEM((2, SPAN, 2 * DIM), BF16),
            pltpu.VMEM((2, SPAN, 2 * DIM), BF16),
            pltpu.VMEM((2, SPAN, 2 * DIM), BF16),
            pltpu.VMEM((2, SPAN, 2 * DIM), BF16),
            pltpu.VMEM((2, SPAN, 2 * DIM), BF16),
            pltpu.VMEM((2, SPAN, 2 * DIM), BF16),
            pltpu.VMEM((GROUP, SPAN, half), BF16),
            pltpu.VMEM((2, SPAN, half), BF16),
            pltpu.VMEM((2, SPAN, half), BF16),
            pltpu.VMEM((GROUP, SPAN, half), BF16),
            pltpu.VMEM((2, SPAN, half), BF16),
            pltpu.VMEM((2, SPAN, half), BF16),
            pltpu.SemaphoreType.REGULAR,
            dma((6,)),
            dma((2,)), dma((2,)), dma((2,)), dma((2,)),
            dma((2,)), dma((2,)), dma((2,)), dma((2,)),
            dma((4,)), dma((4,)),
            dma((2,)), dma((2,)), dma((2,)), dma((2,)), dma((2,)), dma((2,)),
            dma((2,)), dma((2,)),
        ],
        compiler_params=pltpu.CompilerParams(
            collective_id=0, has_side_effects=True, vmem_limit_bytes=40 * 2**20),
        name="attend",
    )(*[
        pltpu.with_memory_space_constraint(x, pltpu.HBM)
        for x in (
            queries.reshape(2, SPAN, width), grad_out.reshape(2, SPAN, width),
            keys.reshape(2, SPAN, DIM), values.reshape(2, SPAN, DIM), lengths, assign.T,
        )
    ])
    results = pl.pallas_call(
        store_kernel,
        out_shape=outs,
        in_specs=[pl.BlockSpec(memory_space=pltpu.VMEM)] * 4,
        out_specs=(hbm,) * 4,
        scratch_shapes=[dma((8,))],
        name="store",
    )(*[pltpu.with_memory_space_constraint(r, pltpu.VMEM) for r in results])
    return tuple(r.reshape(2 * SPAN, r.shape[2]) for r in results)


def solution(mesh):
    split = P("seq", "grp")
    return jax.shard_map(
        functools.partial(shards, mesh.shape["seq"]),
        mesh=mesh,
        in_specs=(split, split, split, split, P(), P()),
        out_specs=(split, split, split, split),
        check_vma=False,
    )
```

```python
import functools
import math

import jax
import jax.numpy as jnp
from jax import lax
from jax.experimental import pallas as pl
from jax.experimental.pallas import tpu as pltpu
from jax.sharding import PartitionSpec as P

MESH = pl.DeviceIdType.MESH
SPAN = 128
DIM = 128
GROUP = 4
F32 = jnp.float32
BF16 = jnp.bfloat16
NT = (((1,), (1,)), ((), ()))
NN = (((1,), (0,)), ((), ()))
TN = (((0,), (0,)), ((), ()))
ROOT = 1.0 / math.sqrt(DIM)
PIECE = 32


def dot(a, b, dims):
    return lax.dot_general(a, b, dims, preferred_element_type=F32)


def pick(values, wanted):
    index = jnp.int32(0)
    for i, value in enumerate(values):
        index = jnp.where(value == wanted, i, index)
    return index


def every_head(x, heads):
    return jnp.concatenate([x] * heads, axis=1)


def spans(x):
    return x.reshape(x.shape[0] // SPAN, SPAN, x.shape[1])


def fold(x, reduce):
    return reduce(x.reshape(x.shape[0] // 8, 8, x.shape[1]), axis=0)


def main_kernel(
    count, q, g, k, v, lens, assign, attn, dq, dk, dv,
    lens_v, assign_s, padded, qslot, gslot, kown, vown, kprev, vprev, qr, gr, qt, gt,
    ko, vo, kot, vot, kp, vp, kpt, vpt, bias, expo, dpo, pb, sb, oto, stat,
    part_p, part_o, sum_send, sum_near, far_send_buf, far_buf, own_send, own_near,
    o_mine, o_send, o_near, q_mine, q_send, q_near,
    arrived, loc_sem, far_ks, far_kr, far_vs, far_vr, rel_ks, rel_kr, rel_vs, rel_vr,
    near_s, near_r, p_s, p_r, f_s, f_r, o_s, o_r, oq_s, oq_r,
):
    me = lax.axis_index("seq")
    grp = lax.axis_index("grp")
    core = lax.rem(me, 2)
    other = 1 - core
    chip = me // 2
    beside = me + 1 - 2 * core
    has_prev = chip > 0
    has_next = chip < count // 2 - 1
    before = jnp.where(has_prev, me - 2, me)
    after = jnp.where(has_next, me + 2, me)
    width = q.shape[2] // 2
    heads = width // DIM

    def remote(src, dst, send, recv, device):
        return pltpu.make_async_remote_copy(
            src_ref=src, dst_ref=dst, send_sem=send, recv_sem=recv,
            device_id=(device, grp), device_id_type=MESH,
        )

    def columns(which):
        return pl.ds(pl.multiple_of(which * width, width), width)

    own_slots = pl.ds(2 * core, 2)
    local = [
        pltpu.make_async_copy(k, kown.at[own_slots], loc_sem.at[0]),
        pltpu.make_async_copy(v, vown.at[own_slots], loc_sem.at[1]),
        pltpu.make_async_copy(lens, lens_v, loc_sem.at[2]),
        pltpu.make_async_copy(assign, assign_s, loc_sem.at[3]),
        pltpu.make_async_copy(q.at[:, :, columns(core)], qslot.at[own_slots], loc_sem.at[4]),
        pltpu.make_async_copy(g.at[:, :, columns(core)], gslot.at[own_slots], loc_sem.at[5]),
    ]
    far_k = [remote(k.at[a], kprev.at[2 * core + a], far_ks.at[a], far_kr.at[a], after)
             for a in range(2)]
    far_v = [remote(v.at[a], vprev.at[2 * core + a], far_vs.at[a], far_vr.at[a], after)
             for a in range(2)]
    relay_k = [remote(kprev.at[2 * core + a], kprev.at[2 * core + a], rel_ks.at[a], rel_kr.at[a],
                      beside) for a in range(2)]
    relay_v = [remote(vprev.at[2 * core + a], vprev.at[2 * core + a], rel_vs.at[a], rel_vr.at[a],
                      beside) for a in range(2)]
    near = [
        remote(k, kown.at[own_slots], near_s.at[0], near_r.at[0], beside),
        remote(v, vown.at[own_slots], near_s.at[1], near_r.at[1], beside),
        remote(q.at[:, :, columns(other)], qslot.at[own_slots], near_s.at[2], near_r.at[2], beside),
        remote(g.at[:, :, columns(other)], gslot.at[own_slots], near_s.at[3], near_r.at[3], beside),
    ]

    barrier = pltpu.get_barrier_semaphore()
    pl.semaphore_signal(barrier, inc=1, device_id=(beside, grp), device_id_type=MESH)

    @pl.when(has_prev)
    def _():
        pl.semaphore_signal(barrier, inc=1, device_id=(before, grp), device_id_type=MESH)

    for copy in local[:4]:
        copy.start()
    pl.semaphore_wait(barrier, 1 + has_next.astype(jnp.int32))

    @pl.when(has_next)
    def _():
        pl.semaphore_signal(arrived, inc=1, device_id=(after, grp), device_id_type=MESH)
        for copy in far_k:
            copy.start()

    for copy in near[:2] + local[4:]:
        copy.start()

    docs = lens_v.shape[0]
    wide = padded.shape[1]
    padded[...] = jnp.zeros_like(padded)
    local[2].wait()
    padded[0:1, 0:docs] = lens_v[...].reshape(1, docs)
    length = padded[...]
    high = length >> 8
    low = length - (high << 8)
    row8 = lax.broadcasted_iota(jnp.int32, (8, wide), 0)
    both = jnp.where(row8 == 1, pltpu.roll(low, 1, 0), high).astype(F32).astype(BF16)
    until = lax.broadcasted_iota(jnp.int32, (wide, wide), 0)
    upto = lax.broadcasted_iota(jnp.int32, (wide, wide), 1)
    lower = jnp.where(upto <= until, 1.0, 0.0).astype(BF16)
    sums = dot(lower, both, NT)
    base = chip * (GROUP * SPAN)
    ends = sums[:, 0:1] * 256.0 + sums[:, 1:2] - base.astype(F32)
    least = -base.astype(F32)
    key_row = lax.broadcasted_iota(jnp.int32, (SPAN, SPAN), 0).astype(F32)
    query_col = lax.broadcasted_iota(jnp.int32, (SPAN, SPAN), 1).astype(F32)
    for j in range(GROUP):
        if j == 1:

            @pl.when(has_next)
            def _():
                for copy in far_v:
                    copy.start()

        pos = query_col[0:1] + float(j * SPAN)
        start = jnp.max(jnp.where(ends <= pos, ends, least), axis=0, keepdims=True)
        for b in range(GROUP + 1):
            key = b if b <= j else b - 1 - GROUP
            ok = key_row + float(key * SPAN) >= start
            if b == j:
                ok = ok & (key_row <= query_col)
            bias[j, b * SPAN : (b + 1) * SPAN] = jnp.where(ok, 0.0, -1e30)

    for copy in near[2:]:
        copy.start()

    local[3].wait()
    back = jnp.maximum(chip - 1, 0)
    here = [assign_s[s % 2, 2 * chip + s // 2] & (GROUP - 1) for s in range(GROUP)]
    there = [assign_s[s % 2, 2 * back + s // 2] & (GROUP - 1) for s in range(GROUP)]
    for copy in (local[0], local[1], local[4], local[5]):
        copy.wait()
    for copy in near:
        copy.wait_recv()
    for j in range(GROUP):
        slot = pick(here, j)
        rows = slice(j * SPAN, (j + 1) * SPAN)
        kb = kown[slot]
        vb = vown[slot]
        ko[rows] = kb
        vo[rows] = vb
        kot[:, rows] = kb.T
        vot[:, rows] = vb.T
        qb = qslot[slot]
        gb = gslot[slot]
        for h in range(heads):
            cols = slice(h * DIM, (h + 1) * DIM)
            qr[j, cols] = qb[:, cols]
            gr[j, cols] = gb[:, cols]
            qt[j, :, cols] = qb[:, cols].T
            gt[j, :, cols] = gb[:, cols].T

    scale = ROOT * math.log2(math.e)
    part_p[...] = jnp.zeros_like(part_p)
    part_o[...] = jnp.zeros_like(part_o)

    def scores(keys, j, first, n):
        s = dot(keys, qt[j], NN)
        top = None
        for at in range(0, n, PIECE):
            rows = slice(first + at, first + at + PIECE)
            piece = s[at : at + PIECE] * scale + every_head(bias[j, rows], heads)
            expo[j, rows] = piece
            top = fold(piece, jnp.max) if top is None else jnp.maximum(top, fold(piece, jnp.max))
        return jnp.max(top, axis=0, keepdims=True)

    def exponentials(j, first, n, top, low=None):
        total = None
        for at in range(0, n, PIECE):
            rows = slice(first + at, first + at + PIECE)
            e = jnp.exp2(expo[j, rows] - top)
            expo[j, rows] = e
            if low is not None:
                low[j, rows] = e.astype(BF16)
            total = fold(e, jnp.sum) if total is None else total + fold(e, jnp.sum)
        return jnp.sum(total, axis=0, keepdims=True)

    tops = []
    for j in range(GROUP):
        n = (j + 1) * SPAN
        tops.append(scores(ko[0:n], j, 0, n))
        dpo[j, 0:n] = dot(vo[0:n], gt[j], NN)
    for j in range(GROUP):
        n = (j + 1) * SPAN
        stat[j, 0:1] = tops[j]
        stat[j, 1:2] = exponentials(j, 0, n, tops[j], pb)
        oto[j] = dot(vot[:, 0:n], pb[j, 0:n], NN)

    @pl.when(has_prev)
    def _():
        pl.semaphore_wait(arrived, 1)
        for a in range(2):
            far_k[a].wait_recv()
            relay_k[a].start()
        for a in range(2):
            relay_k[a].wait_recv()

    @pl.when(jnp.logical_not(has_prev))
    def _():
        kprev[...] = jnp.zeros_like(kprev)
        vprev[...] = jnp.zeros_like(vprev)

    for i in range(GROUP):
        rows = slice(i * SPAN, (i + 1) * SPAN)
        kb = kprev[pick(there, i)]
        kp[rows] = kb
        kpt[:, rows] = kb.T

    tops = []
    for j in range(GROUP):
        top = scores(kp[j * SPAN :], j, (j + 1) * SPAN, (GROUP - j) * SPAN)
        tops.append(jnp.maximum(stat[j, 0:1], top))
    norms = []
    alphas = []
    for j in range(GROUP):
        total = exponentials(j, (j + 1) * SPAN, (GROUP - j) * SPAN, tops[j])
        shrink = jnp.exp2(stat[j, 0:1] - tops[j])
        r = 1.0 / (stat[j, 1:2] * shrink + total)
        norms.append(r)
        alphas.append(shrink * r)
        if j == 1:

            @pl.when(has_prev)
            def _():
                for a in range(2):
                    far_v[a].wait_recv()
                    relay_v[a].start()

    for j in range(GROUP):
        for at in range((j + 1) * SPAN, expo.shape[1], PIECE):
            rows = slice(at, at + PIECE)
            pr = expo[j, rows] * norms[j]
            expo[j, rows] = pr
            pb[j, rows] = pr.astype(BF16)

    @pl.when(has_prev)
    def _():
        for a in range(2):
            relay_v[a].wait_recv()

    for i in range(GROUP):
        rows = slice(i * SPAN, (i + 1) * SPAN)
        vb = vprev[pick(there, i)]
        vp[rows] = vb
        vpt[:, rows] = vb.T

    deltas = []

    def finish_out(j):
        out = oto[j] * alphas[j] + dot(vpt[:, j * SPAN :], pb[j, (j + 1) * SPAN :], NN)
        deltas.append(jnp.sum(out * gt[j].astype(F32), axis=0, keepdims=True))
        out = out.astype(BF16)
        for h in range(heads):
            cols = slice(h * DIM, (h + 1) * DIM)
            o_mine[j, :, cols] = out[:, cols].T

    def prev_dprobs(j):
        return dot(vp[j * SPAN :], gt[j], NN)

    def prev_grads(j, dp):
        at = (j + 1) * SPAN
        for p in range(0, dp.shape[0], PIECE):
            rows = slice(at + p, at + p + PIECE)
            sb[j, rows] = (expo[j, rows] * (dp[p : p + PIECE] - deltas[j])).astype(BF16)
        part_p[j:, :, 0:DIM] += spans(dot(sb[j, at:], qr[j], NN) * ROOT)
        part_p[j:, :, DIM:] += spans(dot(pb[j, at:], gr[j], NN))

    finish_out(0)
    dp = prev_dprobs(0)
    for j in range(1, GROUP):
        finish_out(j)
        next_dp = prev_dprobs(j)
        prev_grads(j - 1, dp)
        dp = next_dp
    prev_grads(GROUP - 1, dp)

    def mine_of(spans, a):
        return jnp.where(core == 0, spans[a], spans[2 + a])

    def theirs_of(spans, a):
        return jnp.where(core == 0, spans[2 + a], spans[a])

    swap_p = [remote(sum_send.at[a], sum_near.at[a], p_s.at[a], p_r.at[a], beside)
              for a in range(2)]
    far_p = [remote(far_send_buf.at[a], far_buf.at[a], f_s.at[a], f_r.at[a], before)
             for a in range(2)]
    for a in range(2):
        sum_send[a] = part_p[theirs_of(there, a)].astype(BF16)
        swap_p[a].start()

    swap_out = remote(o_send, o_near, oq_s.at[0], oq_r.at[0], beside)
    swap_dq = remote(q_send, q_near, oq_s.at[1], oq_r.at[1], beside)
    for a in range(2):
        o_send[a] = o_mine[theirs_of(here, a)]
    swap_out.start()

    def own_dscores(j):
        for at in range(0, (j + 1) * SPAN, PIECE):
            rows = slice(at, at + PIECE)
            pr = expo[j, rows] * alphas[j]
            pb[j, rows] = pr.astype(BF16)
            sb[j, rows] = (pr * (dpo[j, rows] - deltas[j])).astype(BF16)

    def query_grads(j):
        own = slice(0, (j + 1) * SPAN)
        at = (j + 1) * SPAN
        grad = dot(sb[j, own], ko[own], TN) + dot(sb[j, at:], kp[j * SPAN :], TN)
        grad = (grad * ROOT).astype(BF16)
        for h in range(heads):
            cols = slice(h * DIM, (h + 1) * DIM)
            q_mine[j, :, cols] = grad[cols]

    def own_grads(j):
        own = slice(0, (j + 1) * SPAN)
        part_o[0 : j + 1, :, 0:DIM] += spans(dot(sb[j, own], qr[j], NN) * ROOT)
        part_o[0 : j + 1, :, DIM:] += spans(dot(pb[j, own], gr[j], NN))

    own_dscores(0)
    for j in range(1, GROUP):
        own_dscores(j)
        query_grads(j - 1)
    query_grads(GROUP - 1)
    for a in range(2):
        q_send[a] = q_mine[theirs_of(here, a)]
    swap_dq.start()

    for a in range(2):
        swap_p[a].wait_recv()
        far_send_buf[a] = (
            part_p[mine_of(there, a)] + sum_near[a].astype(F32)).astype(BF16)

        @pl.when(has_prev)
        def _(a=a):
            far_p[a].start()

    for j in range(GROUP):
        own_grads(j)

    swap_o = [remote(own_send.at[a], own_near.at[a], o_s.at[a], o_r.at[a], beside)
              for a in range(2)]
    for a in range(2):
        own_send[a] = part_o[theirs_of(here, a)].astype(BF16)
        swap_o[a].start()

    for a in range(2):
        j = mine_of(here, a)
        attn[a, :, columns(core)] = o_mine[j]
        dq[a, :, columns(core)] = q_mine[j]
    swap_out.wait_recv()
    for a in range(2):
        attn[a, :, columns(other)] = o_near[a]
    swap_dq.wait_recv()
    for a in range(2):
        dq[a, :, columns(other)] = q_near[a]

    @pl.when(jnp.logical_not(has_next))
    def _():
        far_buf[...] = jnp.zeros_like(far_buf)

    for a in range(2):
        swap_o[a].wait_recv()

        @pl.when(has_next)
        def _(a=a):
            far_p[a].wait_recv()

        total = part_o[mine_of(here, a)] + own_near[a].astype(F32) + far_buf[a].astype(F32)
        dk[a] = total[:, 0:DIM].astype(BF16)
        dv[a] = total[:, DIM:].astype(BF16)

    for copy in near + swap_p + [swap_out, swap_dq] + swap_o:
        copy.wait_send()

    @pl.when(has_next)
    def _():
        for copy in far_k + far_v:
            copy.wait_send()

    @pl.when(has_prev)
    def _():
        for copy in relay_k + relay_v + far_p:
            copy.wait_send()


def store_kernel(*refs):
    n = (len(refs) - 1) // 2
    sem = refs[2 * n]
    copies = []
    for i in range(n):
        for a in range(2):
            copies.append(
                pltpu.make_async_copy(refs[i].at[a], refs[n + i].at[a], sem.at[len(copies)]))
    for copy in copies:
        copy.start()
    for copy in copies:
        copy.wait()


def shards(count, queries, keys, values, grad_out, lengths, assign):
    width = queries.shape[1]
    half = width // 2
    docs = lengths.shape[0]
    wide = -(-docs // 128) * 128
    hbm = pl.BlockSpec(memory_space=pltpu.HBM)
    vmem = pl.BlockSpec(memory_space=pltpu.VMEM)
    dma = pltpu.SemaphoreType.DMA
    shape = jax.ShapeDtypeStruct
    keyed = GROUP * SPAN
    seen = keyed + SPAN
    outs = (
        shape((2, SPAN, width), BF16),
        shape((2, SPAN, width), BF16),
        shape((2, SPAN, DIM), BF16),
        shape((2, SPAN, DIM), BF16),
    )
    results = pl.pallas_call(
        functools.partial(main_kernel, count),
        out_shape=outs,
        in_specs=[hbm] * 6,
        out_specs=(vmem,) * 4,
        scratch_shapes=[
            pltpu.VMEM((docs,), jnp.int32),
            pltpu.SMEM(assign.shape[::-1], jnp.int32),
            pltpu.VMEM((8, wide), jnp.int32),
            pltpu.VMEM((GROUP, SPAN, half), BF16),
            pltpu.VMEM((GROUP, SPAN, half), BF16),
            pltpu.VMEM((GROUP, SPAN, DIM), BF16),
            pltpu.VMEM((GROUP, SPAN, DIM), BF16),
            pltpu.VMEM((GROUP, SPAN, DIM), BF16),
            pltpu.VMEM((GROUP, SPAN, DIM), BF16),
            pltpu.VMEM((GROUP, half, DIM), BF16),
            pltpu.VMEM((GROUP, half, DIM), BF16),
            pltpu.VMEM((GROUP, DIM, half), BF16),
            pltpu.VMEM((GROUP, DIM, half), BF16),
            pltpu.VMEM((keyed, DIM), BF16),
            pltpu.VMEM((keyed, DIM), BF16),
            pltpu.VMEM((DIM, keyed), BF16),
            pltpu.VMEM((DIM, keyed), BF16),
            pltpu.VMEM((keyed, DIM), BF16),
            pltpu.VMEM((keyed, DIM), BF16),
            pltpu.VMEM((DIM, keyed), BF16),
            pltpu.VMEM((DIM, keyed), BF16),
            pltpu.VMEM((GROUP, seen, SPAN), F32),
            pltpu.VMEM((GROUP, seen, half), F32),
            pltpu.VMEM((GROUP, keyed, half), F32),
            pltpu.VMEM((GROUP, seen, half), BF16),
            pltpu.VMEM((GROUP, seen, half), BF16),
            pltpu.VMEM((GROUP, DIM, half), F32),
            pltpu.VMEM((GROUP, 8, half), F32),
            pltpu.VMEM((GROUP, SPAN, 2 * DIM), F32),
            pltpu.VMEM((GROUP, SPAN, 2 * DIM), F32),
            pltpu.VMEM((2, SPAN, 2 * DIM), BF16),
            pltpu.VMEM((2, SPAN, 2 * DIM), BF16),
            pltpu.VMEM((2, SPAN, 2 * DIM), BF16),
            pltpu.VMEM((2, SPAN, 2 * DIM), BF16),
            pltpu.VMEM((2, SPAN, 2 * DIM), BF16),
            pltpu.VMEM((2, SPAN, 2 * DIM), BF16),
            pltpu.VMEM((GROUP, SPAN, half), BF16),
            pltpu.VMEM((2, SPAN, half), BF16),
            pltpu.VMEM((2, SPAN, half), BF16),
            pltpu.VMEM((GROUP, SPAN, half), BF16),
            pltpu.VMEM((2, SPAN, half), BF16),
            pltpu.VMEM((2, SPAN, half), BF16),
            pltpu.SemaphoreType.REGULAR,
            dma((6,)),
            dma((2,)), dma((2,)), dma((2,)), dma((2,)),
            dma((2,)), dma((2,)), dma((2,)), dma((2,)),
            dma((4,)), dma((4,)),
            dma((2,)), dma((2,)), dma((2,)), dma((2,)), dma((2,)), dma((2,)),
            dma((2,)), dma((2,)),
        ],
        compiler_params=pltpu.CompilerParams(
            collective_id=0, has_side_effects=True, vmem_limit_bytes=40 * 2**20),
        name="attend",
    )(*[
        pltpu.with_memory_space_constraint(x, pltpu.HBM)
        for x in (
            queries.reshape(2, SPAN, width), grad_out.reshape(2, SPAN, width),
            keys.reshape(2, SPAN, DIM), values.reshape(2, SPAN, DIM), lengths, assign.T,
        )
    ])
    results = pl.pallas_call(
        store_kernel,
        out_shape=outs,
        in_specs=[pl.BlockSpec(memory_space=pltpu.VMEM)] * 4,
        out_specs=(hbm,) * 4,
        scratch_shapes=[dma((8,))],
        name="store",
    )(*[pltpu.with_memory_space_constraint(r, pltpu.VMEM) for r in results])
    return tuple(r.reshape(2 * SPAN, r.shape[2]) for r in results)


def solution(mesh):
    split = P("seq", "grp")
    return jax.shard_map(
        functools.partial(shards, mesh.shape["seq"]),
        mesh=mesh,
        in_specs=(split, split, split, split, P(), P()),
        out_specs=(split, split, split, split),
        check_vma=False,
    )
```
